32 devices in a mesh: batch: 8 (over y, x, core), chan: 4 (over z).
Axes of the slice: x: 2, y: 2, z: 4, core: 2. Of those that a mesh axis runs over, the one named last changes fastest.
Arguments:
- input_long: float32 [16, 512, 768], P('batch', None, 'chan'), may hold values from -25 to 25, as said below
- input_short: float32 [32, 128, 768], P('batch', None, 'chan'), may hold values from -25 to 25, as said below
- length_long: int32 [16], P('batch'), may hold values from 128 to 512, as said below
- length_short: int32 [32], P('batch'), may hold values from 32 to 128, as said below
- gain_mixer: float32 [2, 768], P(None, 'chan'), may hold values from 0.5 to 1.5
- weight_in: bfloat16 [2, 768, 3, 768], P(None, None, None, 'chan'), may hold values from -0.21875 to 0.21875
- short_taps: float32 [2, 3, 3, 768], P(None, None, None, 'chan'), may hold values from -4 to 4
- cond_taps: float32 [2, 3, 768], P(None, None, 'chan'), may hold values from -4 to 4
- static_filter: float32 [2, 512, 768], P(None, None, 'chan'), may hold values from -0.25 to 0.25
- weight_out: bfloat16 [2, 768, 768], P(None, 'chan'), may hold values from -0.21875 to 0.21875
- gain_mlp: float32 [2, 768], P(None, 'chan'), may hold values from 0.5 to 1.5
- weight_up: bfloat16 [2, 768, 2, 3072], P(None, None, None, 'chan'), may hold values from -0.21875 to 0.21875
- weight_down: bfloat16 [2, 3072, 768], P(None, 'chan'), may hold values from -0.109375 to 0.109375
- grad_long: float32 [16, 512, 768], P('batch', None, 'chan'), may hold values from -6 to 6
- grad_short: float32 [32, 128, 768], P('batch', None, 'chan'), may hold values from -6 to 6
Outputs:
- output_long: float32 [16, 512, 768], P('batch', None, 'chan')
- output_short: float32 [32, 128, 768], P('batch', None, 'chan')
- input_grad_long: float32 [16, 512, 768], P('batch', None, 'chan')
- input_grad_short: float32 [32, 128, 768], P('batch', None, 'chan')
- gain_mixer_grad: float32 [2, 768], P(None, 'chan')
- weight_in_grad: float32 [2, 768, 3, 768], P(None, None, None, 'chan')
- short_taps_grad: float32 [2, 3, 3, 768], P(None, None, None, 'chan')
- cond_taps_grad: float32 [2, 3, 768], P(None, None, 'chan')
- static_filter_grad: float32 [2, 512, 768], P(None, None, 'chan')
- weight_out_grad: float32 [2, 768, 768], P(None, 'chan')
- gain_mlp_grad: float32 [2, 768], P(None, 'chan')
- weight_up_grad: float32 [2, 768, 2, 3072], P(None, None, None, 'chan')
- weight_down_grad: float32 [2, 3072, 768], P(None, 'chan')
The draws below stay inside these ranges and needn't reach their ends.
Inputs may be any that keep to these rules, and one draw needn't show every extreme that they name: `input_long`: activations of each token, with feature scales that differ over the features. `input_short`: activations of each token, with feature scales that differ over the features. `length_long`: positions at and after a sequence's length are padding; in every draw some long sequence is full. `length_short`: positions at and after a sequence's length are padding; in every draw some short sequence is full.
All inputs are finite; a program needn't handle non-finite values.
Results may differ from the reference program's by a relative error of at most 0.03.
Values may be sent and summed in bfloat16 or wider, within the bound.
No kernel may reach another device: no remote copies, remote signals or barrier semaphores. Data moves between devices by JAX's collectives and lax.ppermute only.
A program may use at most 256 MiB of HBM per device.

```python
import math
from functools import partial
import jax
import jax.numpy as jnp
from jax import lax

D = 768
FF = 3072
LONG = 512
SHORT = 128
LAYERS = 2
NL_DEV = 2
NS_DEV = 4
NL = 16
NS = 32


def column_scale(key, start_scale, factor):
    places = jnp.arange(D, dtype=jnp.float32) / (D - 1)
    rough = jax.random.uniform(key, (D,), jnp.float32, 0.7, 1.4)
    return start_scale * factor ** places * rough


def draw_input_long(key, part):
    key = jax.random.fold_in(key, 11)
    first, second = jax.random.split(key, 2)
    return jnp.clip(jax.random.normal(first, (NL, LONG, D), jnp.float32), -6.0, 6.0) * column_scale(second, 0.55, 3.0)


def draw_input_short(key, part):
    key = jax.random.fold_in(key, 12)
    first, second = jax.random.split(key, 2)
    return jnp.clip(jax.random.normal(first, (NS, SHORT, D), jnp.float32), -6.0, 6.0) * column_scale(second, 0.55, 3.0)


def draw_length_long(key, part):
    key = jax.random.fold_in(key, 13)
    first, second = jax.random.split(key)
    drawn = jax.random.randint(first, (NL,), LONG // 4, LONG + 1)
    chosen = jax.random.randint(second, (), 0, NL)
    return jnp.where(jnp.arange(NL) == chosen, LONG, drawn).astype(jnp.int32)


def draw_length_short(key, part):
    key = jax.random.fold_in(key, 14)
    first, second = jax.random.split(key)
    drawn = jax.random.randint(first, (NS,), SHORT // 4, SHORT + 1)
    chosen = jax.random.randint(second, (), 0, NS)
    return jnp.where(jnp.arange(NS) == chosen, SHORT, drawn).astype(jnp.int32)


def levels(rng, extent, cuts, least, largest):
    def one(position, blocks):
        draws = jax.random.uniform(jax.random.fold_in(jax.random.fold_in(rng, 6), position), (blocks,), jnp.float32, least / len(cuts), largest / len(cuts))
        return jnp.repeat(jnp.exp(draws), extent[position] // blocks).reshape((-1,) + (1,) * (len(extent) - position - 1))

    level = one(*cuts[0])
    for cut in cuts[1:]:
        level = level * one(*cut)
    return level


def bell_draw(key, extent, deviation, most, cuts=(), held_as=jnp.bfloat16):
    values = deviation * jax.random.normal(key, extent, jnp.float32)
    if cuts:
        values = values * levels(key, extent, cuts, -0.22, 0.18)
    return jnp.clip(values, -most, most).astype(held_as)


def setup_inputs(seed: int = 0) -> dict:
    key_list = jax.random.split(jax.random.key(seed), 16)
    return {
        "input_long": draw_input_long(jax.random.fold_in(key_list[15], 71), 0),
        "input_short": draw_input_short(jax.random.fold_in(key_list[15], 71), 0),
        "length_long": draw_length_long(jax.random.fold_in(key_list[15], 71), 0),
        "length_short": draw_length_short(jax.random.fold_in(key_list[15], 71), 0),
        "gain_mixer": jnp.clip(1.0 + 0.1 * jax.random.normal(key_list[4], (LAYERS, D), jnp.float32), 0.5, 1.5),
        "weight_in": bell_draw(key_list[5], (LAYERS, D, 3, D), D ** -0.5, 0.21875, ((3, 4),)),
        "short_taps": bell_draw(key_list[6], (LAYERS, 3, 3, D), 0.6, 4.0, ((3, 4),), jnp.float32),
        "cond_taps": bell_draw(key_list[7], (LAYERS, 3, D), 0.6, 4.0, ((2, 4),), jnp.float32),
        "static_filter": bell_draw(key_list[8], (LAYERS, LONG, D), LONG ** -0.5, 0.25, ((2, 4),), jnp.float32),
        "weight_out": bell_draw(key_list[9], (LAYERS, D, D), D ** -0.5, 0.21875, ((1, 4),)),
        "gain_mlp": jnp.clip(1.0 + 0.1 * jax.random.normal(key_list[10], (LAYERS, D), jnp.float32), 0.5, 1.5),
        "weight_up": bell_draw(key_list[11], (LAYERS, D, 2, FF), D ** -0.5, 0.21875, ((3, 4),)),
        "weight_down": bell_draw(key_list[12], (LAYERS, FF, D), FF ** -0.5, 0.109375, ((1, 4),)),
        "grad_long": bell_draw(key_list[13], (NL, LONG, D), 1.0, 6.0, ((0, 8), (2, 4)), jnp.float32),
        "grad_short": bell_draw(key_list[14], (NS, SHORT, D), 1.0, 6.0, ((0, 8), (2, 4)), jnp.float32),
    }


EPS = 1e-05
HIGH = lax.Precision.HIGHEST

@jax.custom_vjp
def low(v):
    return lax.optimization_barrier(v.astype(jnp.bfloat16)).astype(jnp.float32)

@jax.custom_vjp
def low_back(v):
    return v

def low_keep(v):
    return (low(v), None)

def low_pass(kept, grad):
    return (grad,)

def back_keep(v):
    return (v, None)

def back_low(kept, grad):
    return (low(grad),)
low.defvjp(low_keep, low_pass)
low_back.defvjp(back_keep, back_low)

def layer_norm(values, gain):
    average = lax.optimization_barrier(jnp.mean(values, axis=-1, keepdims=True))
    centered = values - average
    variance = lax.optimization_barrier(jnp.mean(centered * centered, axis=-1, keepdims=True))
    return centered * lax.rsqrt(variance + EPS) * gain

def dense(left, right):
    return jnp.einsum('...d,de->...e', left, right, precision=HIGH)

def causal_taps(values, taps):
    length = values.shape[1]
    padded = jnp.pad(values, ((0, 0), (2, 0)) + ((0, 0),) * (values.ndim - 2))
    return taps[0] * padded[:, 2:] + taps[1] * padded[:, 1:length + 1] + taps[2] * padded[:, :length]

def mix_group(projected, lengths, short_taps, cond_taps, static_filter):
    length = projected.shape[1]
    conv = causal_taps(projected, short_taps)
    query = conv[:, :, 0]
    key_part = conv[:, :, 1]
    value_part = conv[:, :, 2]
    live = (jnp.arange(length)[None, :] < lengths[:, None]).astype(projected.dtype)
    gated = key_part * value_part * live[:, :, None]
    shaped = causal_taps(gated, cond_taps)
    spectrum = jnp.fft.rfft(shaped, n=2 * length, axis=1)
    magnitude = jnp.sqrt(jnp.real(spectrum) ** 2 + jnp.imag(spectrum) ** 2 + length) / math.sqrt(length) - 1.0
    fixed = jnp.fft.rfft(static_filter[:length], n=2 * length, axis=0)
    response = fixed[None] + magnitude
    signal = jnp.fft.rfft(gated, n=2 * length, axis=1)
    long_out = jnp.fft.irfft(response * signal, n=2 * length, axis=1)[:, :length]
    return query * long_out

def mix_shape(projected, lengths, per_group, short_taps, cond_taps, static_filter):
    seq_count = projected.shape[0]
    grouped = projected.reshape((seq_count // per_group, per_group) + projected.shape[1:])
    grouped_lengths = lengths.reshape(seq_count // per_group, per_group)

    def one_group(operands):
        return mix_group(operands[0], operands[1], short_taps, cond_taps, static_filter)
    mixed_rows = lax.map(jax.checkpoint(one_group), (grouped, grouped_lengths))
    return mixed_rows.reshape(projected.shape[:2] + (projected.shape[-1],))

def forward(lengths, input_long, input_short, gain_mixer, weight_in, short_taps, cond_taps, static_filter, weight_out, gain_mlp, weight_up, weight_down):
    streams = [input_long, input_short]
    for layer in range(LAYERS):
        results = []
        for stream, lens_here, per_group in zip(streams, lengths, (NL_DEV, NS_DEV)):
            normed = low(layer_norm(stream, gain_mixer[layer]))
            projected = low_back(dense(normed, weight_in[layer].reshape(D, 3 * D)))
            projected = projected.reshape(projected.shape[:-1] + (3, D))
            mixed = low(mix_shape(projected, lens_here, per_group, short_taps[layer], cond_taps[layer], static_filter[layer]))
            middle = stream + low_back(dense(mixed, weight_out[layer]))
            normed_mlp = low(layer_norm(middle, gain_mlp[layer]))
            gate_up = low_back(dense(normed_mlp, weight_up[layer].reshape(D, 2 * FF)))
            gate_up = gate_up.reshape(gate_up.shape[:-1] + (2, FF))
            activated = low(jax.nn.gelu(gate_up[..., 0, :], approximate=True) * gate_up[..., 1, :])
            results.append(middle + low_back(dense(activated, weight_down[layer])))
        streams = results
    return (streams[0], streams[1])

def reference(input_long, input_short, length_long, length_short, gain_mixer, weight_in, short_taps, cond_taps, static_filter, weight_out, gain_mlp, weight_up, weight_down, grad_long, grad_short):
    closed = partial(forward, (length_long, length_short))
    outputs, pull = jax.vjp(closed, input_long, input_short, gain_mixer, weight_in.astype(jnp.float32), short_taps, cond_taps, static_filter, weight_out.astype(jnp.float32), gain_mlp, weight_up.astype(jnp.float32), weight_down.astype(jnp.float32))
    grads = pull((grad_long, grad_short))
    return (outputs[0], outputs[1], grads[0], grads[1], grads[2], grads[3], grads[4], grads[5], grads[6], grads[7], grads[8], grads[9], grads[10])
```

```python
import functools
import math

import jax
import jax.numpy as jnp
import numpy as np
from jax import lax
from jax.experimental import pallas as pl
from jax.experimental.pallas import tpu as pltpu
from jax.sharding import PartitionSpec as P

EPS = 1e-05
BF16 = jnp.bfloat16
F32 = jnp.float32
VMEM_BYTES = 52 * 2**20
FAR, NEAR = (3, 1)


def nn(left, right):
    return lax.dot_general(left, right, (((1,), (0,)), ((), ())), preferred_element_type=F32)


def nt(left, right):
    return lax.dot_general(left, right, (((1,), (1,)), ((), ())), preferred_element_type=F32)


def tn(left, right):
    return lax.dot_general(left, right, (((0,), (0,)), ((), ())), preferred_element_type=F32)


def table(length):
    places = np.arange(length)[:, None]
    phase = (places * np.arange(length + 1)[None, :] % (2 * length)) * (np.pi / length)
    packed = np.concatenate(
        [np.cos(phase[:, :length]), np.cos(phase[:, length:]), -np.sin(phase[:, 1:length])], axis=1
    )
    return jnp.asarray(packed.astype(np.float32)).astype(BF16)


def swap(values, step):
    axis, mask = step
    return lax.ppermute(values, axis, [(i, i ^ mask) for i in range(lax.axis_size(axis))])


def pick(values, index):
    return lax.dynamic_index_in_dim(values, index, 0, keepdims=False)


def by_xor(values, index):
    return jnp.stack([pick(values, place ^ index) for place in range(values.shape[0])])


def copy_all(copies):
    for copy in copies:
        copy.start()
    for copy in copies:
        copy.wait()


def assemble_kernel(plan, ranks, place_ref, own_ref, *refs):
    *buffers, flat_ref, sems = refs
    pair = place_ref[1]
    step = pl.program_id(0)

    for other in range(ranks):

        @pl.when(step == other)
        def fill():
            copies = []
            if other == 0:
                copies.append(pltpu.make_async_copy(own_ref, flat_ref.at[0], sems.at[0]))
            for buffer, (half, blocks, start, count) in zip(buffers, plan):
                for at, (offset, owner) in enumerate(blocks):
                    if owner != other:
                        continue
                    row = pl.multiple_of(((pair ^ offset) * 2 + half) * count, 16)
                    copies.append(
                        pltpu.make_async_copy(
                            buffer.at[at, pl.ds(start, count)],
                            flat_ref.at[0, pl.ds(row, count)],
                            sems.at[len(copies)],
                        )
                    )
            copy_all(copies)


def assemble(place, own, buffers, plan, ranks):
    rows, width = own.shape
    return pl.pallas_call(
        functools.partial(assemble_kernel, plan, ranks),
        grid=(ranks,),
        out_shape=jax.ShapeDtypeStruct((ranks, rows, width), own.dtype),
        in_specs=[pl.BlockSpec(memory_space=pltpu.SMEM)]
        + [pl.BlockSpec(memory_space=pl.ANY)] * (1 + len(buffers)),
        out_specs=pl.BlockSpec((1, rows, width), lambda r: (r, 0, 0)),
        scratch_shapes=[pltpu.SemaphoreType.DMA((sum(len(p[1]) for p in plan),))],
        compiler_params=pltpu.CompilerParams(vmem_limit_bytes=VMEM_BYTES),
        cost_estimate=pl.CostEstimate(
            flops=0, bytes_accessed=4 * ranks * rows * width, transcendentals=0
        ),
        name="assemble",
    )(place, own, *buffers)


def cut_kernel(plans, orders, place_ref, *refs):
    sources, outs, sems = (refs[: len(plans)], refs[len(plans) : -1], refs[-1])
    pair = place_ref[1]
    step = pl.program_id(0)
    for owner in sorted({other for _, other in orders[0]}):

        @pl.when(step == owner)
        def spill():
            copies = []
            for half, blocks in enumerate(orders):
                for at, (offset, other) in enumerate(blocks):
                    if other != owner:
                        continue
                    middle = len(blocks) // 2
                    target = outs[2 * half + (1 if at >= middle else 0)].at[at % middle]
                    for source, (start, count) in zip(sources, plans):
                        row = pl.multiple_of(((pair ^ offset) * 2 + half) * count, 16)
                        copies.append(
                            pltpu.make_async_copy(
                                source.at[0, pl.ds(row, count)],
                                target.at[pl.ds(start, count)],
                                sems.at[len(copies)],
                            )
                        )
            copy_all(copies)


def cut(place, sources, plans, orders):
    ranks, _, width = sources[0].shape
    rows = sum(count for _, count in plans)
    shape = jax.ShapeDtypeStruct((len(orders[0]) // 2, rows, width), sources[0].dtype)
    kept0, sent0, kept1, sent1 = pl.pallas_call(
        functools.partial(cut_kernel, plans, orders),
        grid=(ranks,),
        out_shape=[shape] * 4,
        in_specs=[pl.BlockSpec(memory_space=pltpu.SMEM)]
        + [pl.BlockSpec((1,) + source.shape[1:], lambda r: (r, 0, 0)) for source in sources],
        out_specs=[pl.BlockSpec(memory_space=pl.ANY)] * 4,
        scratch_shapes=[
            pltpu.SemaphoreType.DMA((len(sources) * sum(len(blocks) for blocks in orders),))
        ],
        compiler_params=pltpu.CompilerParams(vmem_limit_bytes=VMEM_BYTES),
        cost_estimate=pl.CostEstimate(
            flops=0, bytes_accessed=8 * shape.size * 2, transcendentals=0
        ),
        name="cut",
    )(place, *sources)
    return ((kept0, sent0), (kept1, sent1))


def gelu_parts(gate):
    slope = math.sqrt(2.0 / math.pi)
    square = gate * gate
    bent = jnp.tanh(slope * (gate + 0.044715 * square * gate))
    gelu = 0.5 * gate * (1.0 + bent)
    grad = 0.5 * (1.0 + bent) + 0.5 * gate * (1.0 - bent * bent) * slope * (
        1.0 + 0.134145 * square
    )
    return (gelu, grad)


def mlp_forward_kernel(flat_ref, normed_ref, gate_up_ref, kept_ref, sent_ref, total):
    step = pl.program_id(0)
    width = normed_ref.shape[0]
    hidden = flat_ref.shape[1] - width
    gate_up = tn(flat_ref[0, :width], normed_ref[...])
    gate_up_ref[0] = gate_up.astype(BF16)
    activated = (gelu_parts(gate_up[:hidden])[0] * gate_up[hidden:]).astype(BF16)
    part = tn(flat_ref[0, width:], activated)

    @pl.when(step == 0)
    def start():
        total[...] = part

    @pl.when(step > 0)
    def add():
        total[...] += part

    @pl.when(step == pl.num_programs(0) - 1)
    def finish():
        own = kept_ref.shape[1]
        kept_ref[...] = total[:, :own]
        sent_ref[...] = total[:, own:].astype(BF16)


def mlp_forward(flat, normed):
    ranks, rows, width = flat.shape
    tokens = normed.shape[1]
    hidden = rows - width
    half = tokens // 2
    return pl.pallas_call(
        mlp_forward_kernel,
        grid=(ranks,),
        out_shape=[
            jax.ShapeDtypeStruct((ranks, 2 * hidden, tokens), BF16),
            jax.ShapeDtypeStruct((width, half), F32),
            jax.ShapeDtypeStruct((width, half), BF16),
        ],
        in_specs=[
            pl.BlockSpec((1, rows, width), lambda r: (r, 0, 0)),
            pl.BlockSpec((width, tokens), lambda r: (0, 0)),
        ],
        out_specs=[
            pl.BlockSpec((1, 2 * hidden, tokens), lambda r: (r, 0, 0)),
            pl.BlockSpec((width, half), lambda r: (0, 0)),
            pl.BlockSpec((width, half), lambda r: (0, 0)),
        ],
        scratch_shapes=[pltpu.VMEM((width, tokens), F32)],
        compiler_params=pltpu.CompilerParams(vmem_limit_bytes=VMEM_BYTES),
        cost_estimate=pl.CostEstimate(
            flops=6 * ranks * hidden * width * tokens,
            bytes_accessed=2 * flat.size + 4 * ranks * hidden * tokens,
            transcendentals=ranks * hidden * tokens,
        ),
        name="mlp_forward",
    )(flat, normed)


def mlp_back_kernel(
    flat_ref, normed_ref, gate_up_ref, coming_ref, grads_ref, kept_ref, sent_ref, total
):
    step = pl.program_id(0)
    width = normed_ref.shape[0]
    hidden = flat_ref.shape[1] - width
    gate = gate_up_ref[0, :hidden].astype(F32)
    up = gate_up_ref[0, hidden:].astype(F32)
    grad_act = nn(flat_ref[0, width:], coming_ref[...])
    gelu, slope = gelu_parts(gate)
    activated = (gelu * up).astype(BF16)
    grad_gate = (grad_act * up * slope).astype(BF16)
    grad_up = (grad_act * gelu).astype(BF16)
    grads_ref[0, width:] = nt(activated, coming_ref[...]).astype(BF16)
    grads_ref[0, :width, :hidden] = nt(normed_ref[...], grad_gate).astype(BF16)
    grads_ref[0, :width, hidden:] = nt(normed_ref[...], grad_up).astype(BF16)
    part = nn(flat_ref[0, :width, :hidden], grad_gate) + nn(flat_ref[0, :width, hidden:], grad_up)

    @pl.when(step == 0)
    def start():
        total[...] = part

    @pl.when(step > 0)
    def add():
        total[...] += part

    @pl.when(step == pl.num_programs(0) - 1)
    def finish():
        own = kept_ref.shape[1]
        kept_ref[...] = total[:, :own]
        sent_ref[...] = total[:, own:].astype(BF16)


def mlp_back(flat, normed, gate_up, coming):
    ranks, rows, width = flat.shape
    tokens = normed.shape[1]
    hidden = rows - width
    half = tokens // 2
    return pl.pallas_call(
        mlp_back_kernel,
        grid=(ranks,),
        out_shape=[
            jax.ShapeDtypeStruct(flat.shape, BF16),
            jax.ShapeDtypeStruct((width, half), F32),
            jax.ShapeDtypeStruct((width, half), BF16),
        ],
        in_specs=[
            pl.BlockSpec((1, rows, width), lambda r: (r, 0, 0)),
            pl.BlockSpec((width, tokens), lambda r: (0, 0)),
            pl.BlockSpec((1, 2 * hidden, tokens), lambda r: (r, 0, 0)),
            pl.BlockSpec((width, tokens), lambda r: (0, 0)),
        ],
        out_specs=[
            pl.BlockSpec((1, rows, width), lambda r: (r, 0, 0)),
            pl.BlockSpec((width, half), lambda r: (0, 0)),
            pl.BlockSpec((width, half), lambda r: (0, 0)),
        ],
        scratch_shapes=[pltpu.VMEM((width, tokens), F32)],
        compiler_params=pltpu.CompilerParams(vmem_limit_bytes=VMEM_BYTES),
        cost_estimate=pl.CostEstimate(
            flops=12 * ranks * hidden * width * tokens,
            bytes_accessed=4 * flat.size + 4 * ranks * hidden * tokens,
            transcendentals=ranks * hidden * tokens,
        ),
        name="mlp_back",
    )(flat, normed, gate_up, coming)


def delay(values, by):
    return jnp.pad(values, ((0, 0),) * (values.ndim - 1) + ((by, 0),))[..., : values.shape[-1]]


def advance(values, by):
    return jnp.pad(values, ((0, 0),) * (values.ndim - 1) + ((0, by),))[..., by:]


def taps_forward(values, taps):
    return taps[0] * values + taps[1] * delay(values, 1) + taps[2] * delay(values, 2)


def taps_back(values, taps):
    return taps[0] * values + taps[1] * advance(values, 1) + taps[2] * advance(values, 2)


def taps_grad(grads, values):
    return [
        jnp.sum(grads * (delay(values, k) if k else values), axis=(0, 2)) for k in range(3)
    ]


def transform(values, cosines):
    return lax.dot_general(
        values.astype(BF16),
        cosines,
        (((values.ndim - 1,), (0,)), ((), ())),
        preferred_element_type=F32,
    )


def transform_back(real_part, imag_part, cosines):
    packed = jnp.concatenate([real_part.astype(BF16), imag_part.astype(BF16)], axis=-1)
    return lax.dot_general(
        packed, cosines, (((packed.ndim - 1,), (1,)), ((), ())), preferred_element_type=F32
    )


def mix_forward(projected, live, short_taps, cond_taps, static_rows):
    count, width, length = projected[0].shape
    cosines = table(length)
    query, key_part, value_part = (
        taps_forward(values, short_taps[group]) for group, values in enumerate(projected)
    )
    gated = key_part * value_part * live
    shaped = taps_forward(gated, cond_taps)
    spectra = transform(jnp.concatenate([gated, shaped], axis=0), cosines)
    signal_re, signal_im = (spectra[:count, :, :length], spectra[:count, :, length:])
    shaped_re, shaped_im = (spectra[count:, :, :length], spectra[count:, :, length:])
    fixed = transform(static_rows[:, :length], cosines)
    fixed_re, fixed_im = (fixed[:, :length], fixed[:, length:])
    edge = (jnp.arange(length) == 0)[None, None, :]
    square_im = shaped_im * shaped_im
    root = jnp.sqrt(shaped_re * shaped_re + jnp.where(edge, 0.0, square_im) + length)
    root_last = jnp.sqrt(square_im + length)
    scale = 1.0 / math.sqrt(length)
    filter_re = fixed_re + (root * scale - 1.0)
    filter_last = fixed_im + (root_last * scale - 1.0)
    weight = jnp.where(edge, 0.5 / length, 1.0 / length)
    product_re = filter_re * signal_re - jnp.where(edge, 0.0, fixed_im * signal_im)
    product_im = jnp.where(
        edge, filter_last * signal_im, filter_re * signal_im + fixed_im * signal_re
    )
    long_out = transform_back(product_re * weight, product_im * weight, cosines)
    stored = (
        projected, query, key_part, value_part, gated, signal_re, signal_im, shaped_re, shaped_im,
        fixed_im, root, root_last, filter_re, filter_last, long_out, edge, weight, cosines,
    )
    return (query * long_out, stored)


def mix_back(grad_mixed, live, short_taps, cond_taps, stored):
    (
        projected, query, key_part, value_part, gated, signal_re, signal_im, shaped_re, shaped_im,
        fixed_im, root, root_last, filter_re, filter_last, long_out, edge, weight, cosines,
    ) = stored
    count, width, length = gated.shape
    scale = 1.0 / math.sqrt(length)
    grad_query = grad_mixed * long_out
    grad_product = transform(grad_mixed * query, cosines)
    product_re = grad_product[..., :length] * weight
    product_im = grad_product[..., length:] * weight
    grad_signal_re = filter_re * product_re + jnp.where(edge, 0.0, fixed_im * product_im)
    grad_signal_im = jnp.where(
        edge, filter_last * product_im, filter_re * product_im - fixed_im * product_re
    )
    crossed = signal_im * product_im
    grad_filter = signal_re * product_re + jnp.where(edge, 0.0, crossed)
    grad_fixed_im = jnp.where(edge, crossed, signal_re * product_im - signal_im * product_re)
    slope = grad_filter * scale / root
    grad_shaped_re = slope * shaped_re
    grad_shaped_im = jnp.where(edge, crossed * scale / root_last, slope) * shaped_im
    grad_static = transform_back(
        jnp.sum(grad_filter, axis=0), jnp.sum(grad_fixed_im, axis=0), cosines
    )
    back = transform_back(
        jnp.concatenate([grad_signal_re, grad_shaped_re], axis=0),
        jnp.concatenate([grad_signal_im, grad_shaped_im], axis=0),
        cosines,
    )
    grad_shaped = back[count:]
    grad_gated = (back[:count] + taps_back(grad_shaped, cond_taps)) * live
    grad_cond = taps_grad(grad_shaped, gated)
    grads = (grad_query, grad_gated * value_part, grad_gated * key_part)
    grad_projected = [taps_back(grad, short_taps[group]) for group, grad in enumerate(grads)]
    grad_taps = [taps_grad(grad, projected[group]) for group, grad in enumerate(grads)]
    return (grad_projected, grad_taps, grad_cond, grad_static)


def norm_forward(values, gain):
    average = jnp.mean(values, axis=0, keepdims=True)
    centered = values - average
    inv_std = lax.rsqrt(jnp.mean(centered * centered, axis=0, keepdims=True) + EPS)
    normal_rows = centered * inv_std
    return ((normal_rows * gain).astype(BF16), (normal_rows, inv_std, gain))


def norm_back(grads, stored):
    normal_rows, inv_std, gain = stored
    scaled = grads * gain
    total = jnp.mean(scaled, axis=0, keepdims=True)
    crossed = jnp.mean(scaled * normal_rows, axis=0, keepdims=True)
    gain_grad = jnp.sum(grads * normal_rows, axis=1)
    return (inv_std * (scaled - total - normal_rows * crossed), gain_grad)


def on_device(
    input_long,
    input_short,
    length_long,
    length_short,
    gain_mixer,
    weight_in,
    short_taps,
    cond_taps,
    static_filter,
    weight_out,
    gain_mlp,
    weight_up,
    weight_down,
    grad_long,
    grad_short,
):
    count_long, seq_long, chan_width = input_long.shape
    count_short, seq_short = (input_short.shape[0], input_short.shape[1])
    layers = weight_in.shape[0]
    ranks = lax.axis_size("chan")
    pairs = lax.axis_size("batch") // 2
    place = lax.axis_index("chan")
    core = lax.axis_index("batch") % 2
    pair = lax.axis_index("batch") // 2
    width = chan_width * ranks
    hidden = weight_down.shape[1] // 2
    chans = chan_width // 2
    half_long = seq_long // 2
    tokens = half_long + seq_short
    mate = ("batch", 1)
    first = core == 0
    pieces = 4
    piece = pair % pieces
    plane = {1: ("batch", 2), 2: ("batch", 4)}
    extra_steps = []
    mask = 2 * pieces
    while mask < 2 * pairs:
        extra_steps.append(("batch", mask))
        mask *= 2
    spot = jnp.stack([core, piece]).astype(jnp.int32)
    plane_orders = ((1, 2), (2, 1))

    def exchange(blocks):
        came = [pick(blocks, place)]
        came += [swap(pick(blocks, place ^ r), ("chan", r)) for r in range(1, ranks)]
        return by_xor(jnp.stack(came), place)

    def to_tokens(long_rows, short_rows, extra=None):
        turned = jnp.swapaxes(long_rows, 1, 2).astype(BF16)
        halves = jnp.stack([turned[:, :, :half_long], turned[:, :, half_long:]])
        kept = pick(halves, core)
        came = swap(pick(halves, 1 - core), mate)
        ordered = jnp.where(first, jnp.concatenate([kept, came]), jnp.concatenate([came, kept]))
        parts = [ordered, jnp.swapaxes(short_rows, 1, 2).astype(BF16)]
        if extra is not None:
            parts.append(jnp.broadcast_to(extra[None], (ranks,) + extra.shape))
        gathered = exchange(jnp.concatenate(parts, axis=2))
        return gathered.reshape(width, -1)

    def from_tokens(values):
        gathered = exchange(values.reshape(ranks, chan_width, tokens))
        halves = gathered[:, :, :half_long].reshape(2, count_long, chan_width, half_long)
        kept = pick(halves, core)
        came = swap(pick(halves, 1 - core), mate)
        ordered = jnp.where(
            first, jnp.concatenate([kept, came], axis=2), jnp.concatenate([came, kept], axis=2)
        )
        return (jnp.swapaxes(ordered, 1, 2), jnp.swapaxes(gathered[:, :, half_long:], 1, 2))

    def both_cores(values):
        return jnp.concatenate([values, swap(values, mate)], axis=1)

    def both_ordered(values):
        came = swap(values, mate)
        low, high = (jnp.where(first, values, came), jnp.where(first, came, values))
        return jnp.concatenate(
            [low[:, :half_long], high[:, :half_long], low[:, half_long:], high[:, half_long:]],
            axis=1,
        )

    def core_part(values, which):
        long_part = lax.dynamic_slice_in_dim(values, which * half_long, half_long, 1)
        short_part = lax.dynamic_slice_in_dim(values, seq_long + which * seq_short, seq_short, 1)
        return jnp.concatenate([long_part, short_part], axis=1)

    def own_sum(sent, kept):
        return kept + swap(sent, mate).astype(F32)

    def mlp_rows(layer):
        up = lax.dynamic_slice_in_dim(weight_up[layer], core * hidden, hidden, 2)
        down = lax.dynamic_slice_in_dim(weight_down[layer], core * hidden, hidden, 0)
        return jnp.concatenate([up.reshape(width, 2 * hidden), down])

    def mixer_rows(layer):
        into = jnp.transpose(weight_in[layer], (1, 2, 0))
        into = lax.dynamic_slice_in_dim(into, core * chans, chans, 1)
        out = lax.dynamic_slice_in_dim(weight_out[layer], core * chans, chans, 0)
        taps = jnp.concatenate([short_taps[layer].reshape(9, chan_width), cond_taps[layer]]).T
        coarse = lax.reduce_precision(taps, 8, 7)
        static = jnp.concatenate([static_filter[layer].T, coarse, taps - coarse], axis=1)
        static = jnp.pad(static.astype(BF16), ((0, 0), (0, width - static.shape[1])))
        static = lax.dynamic_slice_in_dim(static, core * chans, chans, 0)
        spare = jnp.zeros((mixer_count - 5 * chans, width), BF16)
        return jnp.concatenate([into.reshape(3 * chans, width), out, static, spare])

    mixer_count = -(-5 * chans // (32 * pieces)) * 32 * pieces
    mlp_count = width + hidden
    own_rows = [
        {"mixer": mixer_rows(layer), "mlp": mlp_rows(layer)} for layer in range(layers)
    ]

    def half_rows(kind):
        return (mixer_count if kind == "mixer" else mlp_count) // (2 * pieces)

    def own_block(layer, kind, half):
        count = half_rows(kind)
        return lax.dynamic_slice_in_dim(
            own_rows[layer][kind], (piece * 2 + half) * count, count, 0
        )

    def gather_weights(wanted):
        parts = [own_block(layer, kind, half) for half in range(2) for layer, kind in wanted]
        block = jnp.concatenate(parts)[None]
        rows = block.shape[1] // 2
        far = swap(block, ("chan", FAR))
        near = swap(jnp.concatenate([block, far]), ("chan", NEAR))
        others = (FAR, NEAR, FAR ^ NEAR)
        foreign = jnp.concatenate([far, near])
        buffers, blocks = ([], [])
        for half in range(2):
            held = foreign[:, half * rows : (half + 1) * rows]
            held_blocks = [(0, other) for other in others]
            one, two = plane_orders[half]
            held = jnp.concatenate([held, swap(held, plane[one])])
            held_blocks = held_blocks + [(one, other) for other in others]
            buffers += [held, swap(held, plane[two])]
            blocks += [held_blocks, [(offset ^ two, other) for offset, other in held_blocks]]
        start = 0
        found = {}
        for layer, kind in wanted:
            count = half_rows(kind)
            plan = tuple((at // 2, tuple(blocks[at]), start, count) for at in range(4))
            found[layer, kind] = assemble(spot, own_rows[layer][kind], buffers, plan, ranks)
            start += count
        return found

    weights = gather_weights([(0, "mixer")])
    gains = jnp.stack([gain_mixer, gain_mlp], axis=1).reshape(2 * layers, chan_width)
    gains_coarse = lax.reduce_precision(gains, 8, 7)
    extra = jnp.concatenate([gains_coarse, gains - gains_coarse]).astype(BF16).T
    extra = jnp.pad(extra, ((0, 0), (0, 128 - extra.shape[1])))
    arrived = to_tokens(input_long, input_short, extra)
    gains = arrived[:, tokens:].astype(F32)
    gains = gains[:, : 2 * layers] + gains[:, 2 * layers : 4 * layers]
    gains = [[gains[:, 2 * layer + which][:, None] for which in range(2)] for layer in range(layers)]
    weights.update(gather_weights([(0, "mlp")]))
    for layer in range(1, layers):
        weights.update(gather_weights([(layer, "mlp"), (layer, "mixer")]))
    upstream = to_tokens(grad_long, grad_short).astype(F32)

    own_lengths = jnp.concatenate([length_long, length_short])
    other_lengths = swap(own_lengths, mate)
    low, high = (
        jnp.where(first, own_lengths, other_lengths),
        jnp.where(first, other_lengths, own_lengths),
    )
    live_long = jnp.arange(seq_long) < pick(
        jnp.concatenate([low[:count_long], high[:count_long]]), place
    )
    live_short = jnp.arange(seq_short) < jnp.stack(
        [pick(low[count_long:], place), pick(high[count_long:], place)]
    )[:, None]
    live_long = live_long.astype(F32)[None, None, :]
    live_short = live_short.astype(F32)[:, None, :]

    def by_sequence(values):
        shorts = [
            values[:, seq_long + i * seq_short : seq_long + (i + 1) * seq_short] for i in range(2)
        ]
        return (values[:, :seq_long][None], jnp.stack(shorts))

    def by_token(whole, shorts):
        return jnp.concatenate([whole[0], shorts[0], shorts[1]], axis=1)

    def mixer_part(flat, index, count=1):
        return flat[:, index * chans : (index + count) * chans]

    residual_start = arrived[:, :tokens].astype(F32)
    residual = residual_start
    stored_all = []
    for layer in range(layers):
        flat = weights[layer, "mixer"]
        normed, norm_stored = norm_forward(residual, gains[layer][0])
        normed = both_ordered(normed)
        into = jnp.concatenate([mixer_part(flat, g).reshape(-1, width) for g in range(3)])
        out_rows = mixer_part(flat, 3).reshape(-1, width)
        filters = mixer_part(flat, 4).reshape(-1, width)
        taps = filters[:, seq_long : seq_long + 24].astype(F32)
        taps = taps[:, :12] + taps[:, 12:]
        shorts = [[taps[:, 3 * k + group][:, None] for k in range(3)] for group in range(3)]
        conds = [taps[:, 9 + k][:, None] for k in range(3)]
        static_rows = filters[:, :seq_long]
        projected = nn(into, normed)
        count = out_rows.shape[0]
        sequences = [by_sequence(projected[g * count : (g + 1) * count]) for g in range(3)]
        mixed_long, stored_long = mix_forward(
            [s[0] for s in sequences], live_long, shorts, conds, static_rows
        )
        mixed_short, stored_short = mix_forward(
            [s[1] for s in sequences], live_short, shorts, conds, static_rows
        )
        mixed = by_token(mixed_long, mixed_short).astype(BF16)
        sent = tn(out_rows, core_part(mixed, 1 - core)).astype(BF16)
        kept = tn(out_rows, core_part(mixed, core))
        middle = residual + own_sum(sent, kept)
        normed_mlp, mlp_stored = norm_forward(middle, gains[layer][1])
        normed_mlp = both_cores(normed_mlp)
        gate_up, kept, sent = mlp_forward(weights[layer, "mlp"], normed_mlp)
        residual = middle + own_sum(sent, kept)
        stored_all.append(
            (
                normed, norm_stored, into, out_rows, shorts, conds, stored_long, stored_short,
                mixed, normed_mlp, mlp_stored, gate_up,
            )
        )

    gone_long, gone_short = from_tokens((residual - residual_start).astype(BF16))
    output_long = input_long + gone_long.astype(F32)
    output_short = input_short + gone_short.astype(F32)

    orders = []
    for one, two in plane_orders:
        orders.append(
            tuple(
                (a * one + c * two, (b * NEAR) ^ (d * FAR))
                for a in range(2) for b in range(2) for c in range(2) for d in range(2)
            )
        )

    def scatter_grads(sources, kinds):
        plans, start = ([], 0)
        for kind in kinds:
            plans.append((start, half_rows(kind)))
            start += half_rows(kind)
        done = []
        for half, (kept, sent) in enumerate(cut(spot, sources, tuple(plans), tuple(orders))):
            one, two = plane_orders[half]
            steps = [plane[one], ("chan", NEAR), plane[two], ("chan", FAR)]
            for at, step in enumerate(steps):
                came = swap(sent, step)
                middle = kept.shape[0] // 2
                if at + 1 < len(steps):
                    sent = (kept[middle:].astype(F32) + came[middle:].astype(F32)).astype(BF16)
                    kept = (kept[:middle].astype(F32) + came[:middle].astype(F32)).astype(BF16)
                else:
                    kept = (kept.astype(F32) + came.astype(F32)).astype(BF16)
            for step in extra_steps:
                kept = (kept.astype(F32) + swap(kept, step).astype(F32)).astype(BF16)
            done.append({kind: kept[0, a : a + n] for kind, (a, n) in zip(kinds, plans)})
        return {kind: [done[0][kind], done[1][kind]] for kind in kinds}

    upstream_start = upstream
    reduced = {}
    waiting = None
    for layer in reversed(range(layers)):
        (
            normed, norm_stored, into, out_rows, shorts, conds, stored_long, stored_short,
            mixed, normed_mlp, mlp_stored, gate_up,
        ) = stored_all[layer]
        coming = both_cores(upstream.astype(BF16))
        grads, kept, sent = mlp_back(weights[layer, "mlp"], normed_mlp, gate_up, coming)
        if waiting is None:
            reduced[layer, "mlp"] = scatter_grads([grads], ["mlp"])["mlp"]
        else:
            done = scatter_grads([grads, waiting], ["mlp", "mixer"])
            reduced[layer, "mlp"] = done["mlp"]
            reduced[layer + 1, "mixer"] = done["mixer"]
        change, grad_gain_mlp = norm_back(own_sum(sent, kept), mlp_stored)
        upstream = upstream + change
        coming = both_ordered(upstream.astype(BF16))
        grad_out = nt(mixed, coming).astype(BF16)
        grad_mixed_long, grad_mixed_short = by_sequence(nn(out_rows, coming))
        back_long = mix_back(grad_mixed_long, live_long, shorts, conds, stored_long)
        back_short = mix_back(grad_mixed_short, live_short, shorts, conds, stored_short)
        grad_proj = jnp.concatenate(
            [by_token(back_long[0][group], back_short[0][group]) for group in range(3)]
        ).astype(BF16)
        grad_into = nt(grad_proj, normed).astype(BF16)
        sent = tn(into, core_part(grad_proj, 1 - core)).astype(BF16)
        kept = tn(into, core_part(grad_proj, core))
        change, grad_gain_mixer = norm_back(own_sum(sent, kept), norm_stored)
        upstream = upstream + change
        grad_static = back_long[3]
        grad_static = jnp.concatenate(
            [grad_static[:, :seq_short] + back_short[3], grad_static[:, seq_short:]], axis=1
        )
        grad_taps = [
            back_long[1][group][k] + back_short[1][group][k] for k in range(3) for group in range(3)
        ]
        grad_taps += [back_long[2][k] + back_short[2][k] for k in range(3)]
        lanes = jnp.concatenate([grad_static, jnp.stack(grad_taps, axis=1)], axis=1)
        lanes = jnp.pad(lanes, ((0, 0), (0, width - lanes.shape[1]))).astype(BF16)
        gain_rows = jnp.concatenate(
            [values.reshape(ranks, chan_width) for values in (grad_gain_mixer, grad_gain_mlp)],
            axis=1,
        )
        gain_rows = by_xor(gain_rows, place).astype(BF16)[:, None]
        gain_rows = jnp.pad(
            gain_rows,
            ((0, 0), (0, mixer_count - 5 * chans - 1), (0, width - 2 * chan_width)),
        )
        waiting = jnp.concatenate(
            [
                grad_into.reshape(3, ranks, chans, width).swapaxes(0, 1).reshape(ranks, -1, width),
                grad_out.reshape(ranks, chans, width),
                lanes.reshape(ranks, chans, width),
                gain_rows,
            ],
            axis=1,
        )
    reduced[0, "mixer"] = scatter_grads([waiting], ["mixer"])["mixer"]

    gone_long, gone_short = from_tokens((upstream - upstream_start).astype(BF16))
    back_long = grad_long + gone_long.astype(F32)
    back_short = grad_short + gone_short.astype(F32)

    def gather_grads(wanted):
        packed = []
        for half in range(2):
            one, two = plane_orders[half]
            block = jnp.concatenate([reduced[key][half] for key in wanted])[None]
            block = jnp.concatenate([block, swap(block, plane[one])])
            block = jnp.concatenate([block, swap(block, plane[two])])
            offsets = [0, one, two, one ^ two]
            packed.append(jnp.stack([block[offsets.index(p)] for p in range(pieces)]))
        packed = jnp.concatenate(packed, axis=1)
        came = swap(packed, mate)
        rows = packed.shape[1] // 2
        result = {}
        at = 0
        for layer, kind in wanted:
            count = half_rows(kind)
            sides = []
            for values in (packed, came):
                mine = jnp.concatenate(
                    [values[:, at : at + count], values[:, rows + at : rows + at + count]], axis=1
                )
                sides.append(by_xor(mine, piece).reshape(-1, width))
            result[layer, kind] = jnp.where(first, jnp.stack(sides), jnp.stack(sides[::-1]))
            at += count
        return result

    final = gather_grads(
        [(layer, kind) for layer in range(layers) for kind in ("mlp", "mixer") if (layer, kind) != (0, "mixer")]
    )
    final.update(gather_grads([(0, "mixer")]))

    def stacked(function, kind):
        return jnp.stack([function(final[layer, kind].astype(F32)) for layer in range(layers)])

    def part_of(values, index, count=1):
        rows = values[:, index * chans : (index + count) * chans]
        return rows.reshape(2, count, chans, width).swapaxes(0, 1).reshape(count, 2 * chans, width)

    def lanes_of(values, start, stop):
        return part_of(values, 4)[0][:, start:stop].T

    def gain_of(values, which):
        rows = values[:, 5 * chans, which * chan_width : (which + 1) * chan_width]
        return rows[0] + rows[1]

    def up_of(values):
        both = values[:, :width].reshape(2, width, 2, hidden)
        return jnp.moveaxis(both, 0, 2).reshape(width, 2, 2 * hidden)

    return (
        output_long,
        output_short,
        back_long,
        back_short,
        stacked(lambda values: gain_of(values, 0), "mixer"),
        stacked(lambda values: jnp.transpose(part_of(values, 0, 3), (2, 0, 1)), "mixer"),
        stacked(
            lambda values: lanes_of(values, seq_long, seq_long + 9).reshape(3, 3, chan_width),
            "mixer",
        ),
        stacked(lambda values: lanes_of(values, seq_long + 9, seq_long + 12), "mixer"),
        stacked(lambda values: lanes_of(values, 0, seq_long), "mixer"),
        stacked(lambda values: part_of(values, 3)[0], "mixer"),
        stacked(lambda values: gain_of(values, 1), "mixer"),
        stacked(up_of, "mlp"),
        stacked(lambda values: values[:, width:].reshape(2 * hidden, width), "mlp"),
    )


def solution(mesh):
    tokens = P("batch", None, "chan")
    placed = (
        tokens,
        tokens,
        P("batch"),
        P("batch"),
        P(None, "chan"),
        P(None, None, None, "chan"),
        P(None, None, None, "chan"),
        P(None, None, "chan"),
        P(None, None, "chan"),
        P(None, "chan", None),
        P(None, "chan"),
        P(None, None, None, "chan"),
        P(None, "chan", None),
        tokens,
        tokens,
    )
    return jax.shard_map(
        on_device,
        mesh=mesh,
        in_specs=placed,
        out_specs=(tokens,) * 4 + placed[4:13],
        check_vma=False,
    )
```

```python
import functools
import math

import jax
import jax.numpy as jnp
import numpy as np
from jax import lax
from jax.experimental import pallas as pl
from jax.experimental.pallas import tpu as pltpu
from jax.sharding import PartitionSpec as P

EPS = 1e-05
BF16 = jnp.bfloat16
F32 = jnp.float32
VMEM_BYTES = 52 * 2**20
FAR, NEAR = (3, 1)


def nn(left, right):
    return lax.dot_general(left, right, (((1,), (0,)), ((), ())), preferred_element_type=F32)


def nt(left, right):
    return lax.dot_general(left, right, (((1,), (1,)), ((), ())), preferred_element_type=F32)


def tn(left, right):
    return lax.dot_general(left, right, (((0,), (0,)), ((), ())), preferred_element_type=F32)


def table(length):
    places = np.arange(length)[:, None]
    phase = (places * np.arange(length + 1)[None, :] % (2 * length)) * (np.pi / length)
    packed = np.concatenate(
        [np.cos(phase[:, :length]), np.cos(phase[:, length:]), -np.sin(phase[:, 1:length])], axis=1
    )
    return jnp.asarray(packed.astype(np.float32)).astype(BF16)


def swap(values, step):
    axis, mask = step
    return lax.ppermute(values, axis, [(i, i ^ mask) for i in range(lax.axis_size(axis))])


def pick(values, index):
    return lax.dynamic_index_in_dim(values, index, 0, keepdims=False)


def by_xor(values, index):
    return jnp.stack([pick(values, place ^ index) for place in range(values.shape[0])])


def block_copies(plan, place_ref, own_ref, buffers, flat_ref, sems, wanted):
    if wanted == 0:
        return [pltpu.make_async_copy(own_ref, flat_ref.at[0], sems.at[0, 0])]
    copies = []
    for buffer, (half, blocks, start, count) in zip(buffers, plan):
        for at, (offset, other) in enumerate(blocks):
            if other == wanted:
                row = pl.multiple_of(((place_ref[1] ^ offset) * 2 + half) * count, 16)
                copies.append(
                    pltpu.make_async_copy(
                        buffer.at[at, pl.ds(start, count)],
                        flat_ref.at[wanted, pl.ds(row, count)],
                        sems.at[wanted, len(copies)],
                    )
                )
    return copies


def fill(plan, place_ref, own_ref, buffers, flat_ref, sems, per_step):
    step = pl.program_id(0)
    ranks = flat_ref.shape[0]
    args = (plan, place_ref, own_ref, buffers, flat_ref, sems)

    @pl.when(step == 0)
    def begin():
        for wanted in range(ranks):
            for copy in block_copies(*args, wanted):
                copy.start()

    for wanted in range(ranks):

        @pl.when(step == wanted // per_step)
        def arrive():
            for copy in block_copies(*args, wanted):
                copy.wait()


def spill_copies(orders, count, start, place_ref, rows_ref, outs, sems, slot, wanted):
    copies = []
    for half, blocks in enumerate(orders):
        for at, (offset, other) in enumerate(blocks):
            if other != wanted:
                continue
            middle = len(blocks) // 2
            target = outs[2 * half + (1 if at >= middle else 0)].at[at % middle]
            row = pl.multiple_of(((place_ref[1] ^ offset) * 2 + half) * count, 16)
            copies.append(
                pltpu.make_async_copy(
                    rows_ref.at[slot, pl.ds(row, count)],
                    target.at[pl.ds(start, count)],
                    sems.at[slot, len(copies)],
                )
            )
    return copies


def grouped(refs, *counts):
    groups, at = ([], 0)
    for count in counts:
        groups.append(refs[at : at + count])
        at += count
    return groups


def whole(shape):
    return pl.BlockSpec(shape, lambda i: (0,) * len(shape))


SMEM = pl.BlockSpec(memory_space=pltpu.SMEM)
ANY = pl.BlockSpec(memory_space=pl.ANY)
PARAMS = pltpu.CompilerParams(vmem_limit_bytes=VMEM_BYTES)


def gelu_parts(gate):
    slope = math.sqrt(2.0 / math.pi)
    square = gate * gate
    bent = jnp.tanh(slope * (gate + 0.044715 * square * gate))
    gelu = 0.5 * gate * (1.0 + bent)
    grad = 0.5 * (1.0 + bent) + 0.5 * gate * (1.0 - bent * bent) * slope * (
        1.0 + 0.134145 * square
    )
    return (gelu, grad)


def add_total(total, part):
    step = pl.program_id(0)

    @pl.when(step == 0)
    def start():
        total[...] = part

    @pl.when(step > 0)
    def add():
        total[...] += part


def split_total(total, kept_ref, sent_ref):
    @pl.when(pl.program_id(0) == pl.num_programs(0) - 1)
    def finish():
        own = kept_ref.shape[1]
        kept_ref[...] = total[:, :own]
        sent_ref[...] = total[:, own:].astype(BF16)


def mlp_forward_kernel(plan, *refs):
    (place_ref, normed_ref, own_ref), buffers, outs, scratch = grouped(refs, 3, len(plan), 3, 3)
    gate_up_ref, kept_ref, sent_ref = outs
    flat_ref, total, sems = scratch
    fill(plan, place_ref, own_ref, buffers, flat_ref, sems, 1)
    step = pl.program_id(0)
    width = normed_ref.shape[0]
    hidden = flat_ref.shape[1] - width
    gate_up = tn(flat_ref[step, :width], normed_ref[...])
    gate_up_ref[0] = gate_up.astype(BF16)
    activated = (gelu_parts(gate_up[:hidden])[0] * gate_up[hidden:]).astype(BF16)
    add_total(total, tn(flat_ref[step, width:], activated))
    split_total(total, kept_ref, sent_ref)


def mlp_forward(place, rows, normed):
    own, buffers, plan, ranks = rows
    count, width = own.shape
    tokens = normed.shape[1]
    hidden = count - width
    half = tokens // 2
    return pl.pallas_call(
        functools.partial(mlp_forward_kernel, plan),
        grid=(ranks,),
        out_shape=[
            jax.ShapeDtypeStruct((ranks, 2 * hidden, tokens), BF16),
            jax.ShapeDtypeStruct((width, half), F32),
            jax.ShapeDtypeStruct((width, half), BF16),
        ],
        in_specs=[SMEM, whole((width, tokens)), ANY] + [ANY] * len(buffers),
        out_specs=[
            pl.BlockSpec((1, 2 * hidden, tokens), lambda r: (r, 0, 0)),
            whole((width, half)),
            whole((width, half)),
        ],
        scratch_shapes=[
            pltpu.VMEM((ranks, count, width), BF16),
            pltpu.VMEM((width, tokens), F32),
            pltpu.SemaphoreType.DMA((ranks, 8)),
        ],
        compiler_params=PARAMS,
        cost_estimate=pl.CostEstimate(
            flops=6 * ranks * hidden * width * tokens,
            bytes_accessed=2 * ranks * own.size + 4 * ranks * hidden * tokens,
            transcendentals=ranks * hidden * tokens,
        ),
        name="mlp_forward",
    )(place, normed, own, *buffers)


def spill(orders, count, start, place_ref, grads_ref, outs, sems, per_step):
    step = pl.program_id(0)
    ranks = per_step * pl.num_programs(0)
    for wanted in range(ranks):
        at = wanted // per_step
        slot = (at % 2) * per_step + wanted % per_step

        @pl.when(step == at)
        def leave():
            for copy in spill_copies(
                orders, count, start, place_ref, grads_ref, outs, sems, slot, wanted
            ):
                copy.start()


def spill_wait(orders, count, start, place_ref, grads_ref, outs, sems, per_step, last):
    step = pl.program_id(0)
    steps = 4 // per_step
    for wanted in range(4):
        at = wanted // per_step
        slot = (at % 2) * per_step + wanted % per_step
        due = steps - 1 if last else at + 2
        if last and at + 2 < steps:
            continue
        if not last and at + 2 >= steps:
            continue

        @pl.when(step == due)
        def gone():
            for copy in spill_copies(
                orders, count, start, place_ref, grads_ref, outs, sems, slot, wanted
            ):
                copy.wait()


def mlp_back_kernel(plan, orders, start, aliased, *refs):
    (place_ref, normed_ref, coming_ref, gate_up_ref, own_ref), buffers, _, outs, scratch = grouped(
        refs, 5, len(plan), 4 if aliased else 0, 6, 5
    )
    kept_ref, sent_ref = outs[:2]
    flat_ref, grads_ref, total, sems, out_sems = scratch
    fill(plan, place_ref, own_ref, buffers, flat_ref, sems, 1)
    step = pl.program_id(0)
    width = normed_ref.shape[0]
    hidden = flat_ref.shape[1] - width
    count = flat_ref.shape[1] // (2 * len(orders[0]) // flat_ref.shape[0])
    spilled = (orders, count, start, place_ref, grads_ref, outs[2:], out_sems, 1)
    spill_wait(*spilled, False)
    slot = step % 2
    gate = gate_up_ref[0, :hidden].astype(F32)
    up = gate_up_ref[0, hidden:].astype(F32)
    grad_act = nn(flat_ref[step, width:], coming_ref[...])
    gelu, slope = gelu_parts(gate)
    activated = (gelu * up).astype(BF16)
    grad_gate = (grad_act * up * slope).astype(BF16)
    grad_up = (grad_act * gelu).astype(BF16)
    grads_ref[slot, width:] = nt(activated, coming_ref[...]).astype(BF16)
    grads_ref[slot, :width, :hidden] = nt(normed_ref[...], grad_gate).astype(BF16)
    grads_ref[slot, :width, hidden:] = nt(normed_ref[...], grad_up).astype(BF16)
    spill(*spilled)
    add_total(
        total,
        nn(flat_ref[step, :width, :hidden], grad_gate)
        + nn(flat_ref[step, :width, hidden:], grad_up),
    )
    split_total(total, kept_ref, sent_ref)
    spill_wait(*spilled, True)


def mlp_back(place, rows, normed, gate_up, coming, orders, start, into):
    own, buffers, plan, ranks = rows
    count, width = own.shape
    tokens = normed.shape[1]
    hidden = count - width
    half = tokens // 2
    aliased = not isinstance(into, int)
    blocks = jax.ShapeDtypeStruct(
        (len(orders[0]) // 2, into[0].shape[1] if aliased else into, width), BF16
    )
    first_alias = 5 + len(buffers)
    results = pl.pallas_call(
        functools.partial(mlp_back_kernel, plan, orders, start, aliased),
        grid=(ranks,),
        out_shape=[
            jax.ShapeDtypeStruct((width, half), F32),
            jax.ShapeDtypeStruct((width, half), BF16),
        ]
        + [blocks] * 4,
        in_specs=[
            SMEM,
            whole((width, tokens)),
            whole((width, tokens)),
            pl.BlockSpec((1, 2 * hidden, tokens), lambda r: (r, 0, 0)),
            ANY,
        ]
        + [ANY] * (len(buffers) + (4 if aliased else 0)),
        out_specs=[whole((width, half)), whole((width, half))] + [ANY] * 4,
        input_output_aliases={first_alias + i: 2 + i for i in range(4)} if aliased else {},
        scratch_shapes=[
            pltpu.VMEM((ranks, count, width), BF16),
            pltpu.VMEM((2, count, width), BF16),
            pltpu.VMEM((width, tokens), F32),
            pltpu.SemaphoreType.DMA((ranks, 8)),
            pltpu.SemaphoreType.DMA((2, 8)),
        ],
        compiler_params=PARAMS,
        cost_estimate=pl.CostEstimate(
            flops=12 * ranks * hidden * width * tokens,
            bytes_accessed=4 * ranks * own.size + 4 * ranks * hidden * tokens,
            transcendentals=ranks * hidden * tokens,
        ),
        name="mlp_back",
    )(place, normed, coming, gate_up, own, *buffers, *(into if aliased else ()))
    return (results[0], results[1], results[2:])


def delayed(layout, values, by):
    return jnp.where(layout["inside"] >= by, pltpu.roll(values, by, 1), 0.0)


def advanced(layout, values, by):
    moved = pltpu.roll(values, layout["tokens"] - by, 1)
    return jnp.where(layout["inside"] < layout["length"] - by, moved, 0.0)


def layout_of(long, short, tokens):
    lane = lax.broadcasted_iota(jnp.int32, (1, tokens), 1)
    return {
        "long": long,
        "short": short,
        "tokens": tokens,
        "inside": jnp.where(lane < long, lane, (lane - long) % short),
        "length": jnp.where(lane < long, long, short),
    }


def taps_forward(layout, values, taps):
    return (
        taps[0] * values
        + taps[1] * delayed(layout, values, 1)
        + taps[2] * delayed(layout, values, 2)
    )


def taps_back(layout, values, taps):
    return (
        taps[0] * values
        + taps[1] * advanced(layout, values, 1)
        + taps[2] * advanced(layout, values, 2)
    )


def taps_grad(layout, grads, values):
    moved = [values, delayed(layout, values, 1), delayed(layout, values, 2)]
    return [jnp.sum(grads * value, axis=1, keepdims=True) for value in moved]


def sequences(layout, values):
    long, short = (layout["long"], layout["short"])
    shorts = [values[:, at : at + short] for at in range(long, layout["tokens"], short)]
    return (values[:, :long], jnp.concatenate(shorts, axis=0))


def rejoined(long_part, short_part):
    rows = long_part.shape[0]
    shorts = [short_part[at * rows : (at + 1) * rows] for at in range(short_part.shape[0] // rows)]
    return jnp.concatenate([long_part] + shorts, axis=1)


def repeated(values, times):
    return jnp.concatenate([values] * times, axis=0) if times > 1 else values


def at_edge(edge, edge_values, others):
    head = jnp.where(edge[:, :128], edge_values, others[:, :128])
    return jnp.concatenate([head, others[:, 128:]], axis=1) if others.shape[1] > 128 else head


def turned_back(real_part, imag_part, cosines):
    return nt(jnp.concatenate([real_part.astype(BF16), imag_part.astype(BF16)], axis=1), cosines)


def filter_of(gated, shaped, static_rows, cosines):
    rows, length = gated.shape
    times = rows // static_rows.shape[0]
    edge = lax.broadcasted_iota(jnp.int32, (1, length), 1) == 0
    spectra = nn(jnp.concatenate([gated, shaped], axis=0).astype(BF16), cosines)
    shaped_re, shaped_im = (spectra[rows:, :length], spectra[rows:, length:])
    fixed = nn(static_rows, cosines)
    fixed_re = repeated(fixed[:, :length], times)
    fixed_im = repeated(fixed[:, length:], times)
    square = shaped_im * shaped_im
    power = shaped_re * shaped_re + jnp.where(edge, 0.0, square) + length
    inv_root = lax.rsqrt(power)
    power_last = square[:, :128] + length
    inv_root_last = lax.rsqrt(power_last)
    scale = 1.0 / math.sqrt(length)
    return {
        "length": length,
        "times": times,
        "edge": edge,
        "weight": jnp.where(edge, 0.5 / length, 1.0 / length),
        "signal_re": spectra[:rows, :length],
        "signal_im": spectra[:rows, length:],
        "shaped_re": shaped_re,
        "shaped_im": shaped_im,
        "fixed_im": fixed_im,
        "fixed_sine": jnp.where(edge, 0.0, fixed_im),
        "slope": scale * inv_root,
        "slope_last": scale * inv_root_last,
        "filter_re": fixed_re + (power * inv_root * scale - 1.0),
        "filter_last": fixed_im[:, :128] + (power_last * inv_root_last * scale - 1.0),
    }


def filtered(parts, cosines):
    signal_re, signal_im = (parts["signal_re"], parts["signal_im"])
    product_re = parts["filter_re"] * signal_re - parts["fixed_sine"] * signal_im
    product_im = at_edge(
        parts["edge"],
        parts["filter_last"] * signal_im[:, :128],
        parts["filter_re"] * signal_im + parts["fixed_im"] * signal_re,
    )
    return turned_back(product_re * parts["weight"], product_im * parts["weight"], cosines)


def filter_back(parts, grad_out, cosines):
    length, times, edge = (parts["length"], parts["times"], parts["edge"])
    signal_re, signal_im = (parts["signal_re"], parts["signal_im"])
    filter_re, fixed_im = (parts["filter_re"], parts["fixed_im"])
    turned = nn(grad_out.astype(BF16), cosines)
    product_re = turned[:, :length] * parts["weight"]
    product_im = turned[:, length:] * parts["weight"]
    grad_signal_re = filter_re * product_re + parts["fixed_sine"] * product_im
    grad_signal_im = at_edge(
        edge,
        parts["filter_last"] * product_im[:, :128],
        filter_re * product_im - fixed_im * product_re,
    )
    crossed = signal_im * product_im
    grad_filter = signal_re * product_re + jnp.where(edge, 0.0, crossed)
    grad_fixed_im = at_edge(
        edge, crossed[:, :128], signal_re * product_im - signal_im * product_re
    )
    slope = grad_filter * parts["slope"]
    grad_shaped_re = slope * parts["shaped_re"]
    grad_shaped_im = (
        at_edge(edge, crossed[:, :128] * parts["slope_last"], slope) * parts["shaped_im"]
    )
    count = grad_out.shape[0]
    rows = count // times
    grad_static = turned_back(
        sum(grad_filter[i * rows : (i + 1) * rows] for i in range(times)),
        sum(grad_fixed_im[i * rows : (i + 1) * rows] for i in range(times)),
        cosines,
    )
    back = turned_back(
        jnp.concatenate([grad_signal_re, grad_shaped_re], axis=0),
        jnp.concatenate([grad_signal_im, grad_shaped_im], axis=0),
        cosines,
    )
    return (back[:count], back[count:], grad_static)


def mixer_rows_of(flat_ref, step, per_step, chans):
    def rows(index):
        return [
            flat_ref[step * per_step + i, index * chans : (index + 1) * chans]
            for i in range(per_step)
        ]

    into = jnp.concatenate(rows(0) + rows(1) + rows(2), axis=0)
    filters = jnp.concatenate(rows(4), axis=0)
    return (into, jnp.concatenate(rows(3), axis=0), filters)


def mixer_taps(filters, start):
    lanes = filters[:, start : start + 128].astype(F32)
    taps = [lanes[:, k : k + 1] + lanes[:, 12 + k : 13 + k] for k in range(12)]
    return ([[taps[3 * k + group] for k in range(3)] for group in range(3)], taps[9:])


def own_lanes(ref, which, layout):
    half_long, short = (layout["long"] // 2, layout["short"])
    at = pl.multiple_of(which * half_long, 128)
    after = pl.multiple_of(layout["long"] + which * short, 128)
    return jnp.concatenate([ref[:, pl.ds(at, half_long)], ref[:, pl.ds(after, short)]], axis=1)


def mixer_forward_kernel(plan, sizes, *refs):
    inputs, buffers, outs, scratch = grouped(refs, 6, len(plan), 4, 4)
    place_ref, live_ref, long_ref, short_ref, normed_ref, own_ref = inputs
    proj_ref, long_out_ref, kept_ref, sent_ref = outs
    flat_ref, mixed_ref, total, sems = scratch
    long, short, chans, per_step = sizes
    fill(plan, place_ref, own_ref, buffers, flat_ref, sems, per_step)
    step = pl.program_id(0)
    layout = layout_of(long, short, normed_ref.shape[1])
    into, out_rows, filters = mixer_rows_of(flat_ref, step, per_step, chans)
    short_taps, cond_taps = mixer_taps(filters, long)
    rows = per_step * chans
    proj = nn(into, normed_ref[...])
    proj_ref[0] = proj.astype(BF16)
    query, key_part, value_part = (
        taps_forward(layout, proj[g * rows : (g + 1) * rows], short_taps[g]) for g in range(3)
    )
    gated = key_part * value_part * live_ref[:1]
    shaped = taps_forward(layout, gated, cond_taps)
    gated_parts, shaped_parts = (sequences(layout, gated), sequences(layout, shaped))
    results = [
        filtered(
            filter_of(gated_parts[i], shaped_parts[i], filters[:, :length], ref[...]), ref[...]
        )
        for i, (length, ref) in enumerate(((long, long_ref), (short, short_ref)))
    ]
    long_out = rejoined(*results)
    long_out_ref[0] = long_out.astype(BF16)
    mixed_ref[...] = (query * long_out).astype(BF16)
    core = place_ref[0]
    half = kept_ref.shape[1]
    part_kept = tn(out_rows, own_lanes(mixed_ref, core, layout))
    part_sent = tn(out_rows, own_lanes(mixed_ref, 1 - core, layout))
    add_total(total, jnp.concatenate([part_kept, part_sent], axis=1))
    split_total(total, kept_ref, sent_ref)


def mixer_forward(place, rows, normed, live, tables, sizes):
    own, buffers, plan, ranks = rows
    count, width = own.shape
    tokens = normed.shape[1]
    half = tokens // 2
    chans, per_step = sizes[2:]
    steps = ranks // per_step
    group = per_step * chans
    return pl.pallas_call(
        functools.partial(mixer_forward_kernel, plan, sizes),
        grid=(steps,),
        out_shape=[
            jax.ShapeDtypeStruct((steps, 3 * group, tokens), BF16),
            jax.ShapeDtypeStruct((steps, group, tokens), BF16),
            jax.ShapeDtypeStruct((width, half), F32),
            jax.ShapeDtypeStruct((width, half), BF16),
        ],
        in_specs=[SMEM, whole(live.shape)]
        + [whole(t.shape) for t in tables]
        + [whole((width, tokens)), ANY]
        + [ANY] * len(buffers),
        out_specs=[
            pl.BlockSpec((1, 3 * group, tokens), lambda r: (r, 0, 0)),
            pl.BlockSpec((1, group, tokens), lambda r: (r, 0, 0)),
            whole((width, half)),
            whole((width, half)),
        ],
        scratch_shapes=[
            pltpu.VMEM((ranks, count, width), BF16),
            pltpu.VMEM((group, tokens), BF16),
            pltpu.VMEM((width, tokens), F32),
            pltpu.SemaphoreType.DMA((ranks, 8)),
        ],
        compiler_params=PARAMS,
        cost_estimate=pl.CostEstimate(
            flops=2 * ranks * chans * (4 * width * tokens + 8 * sizes[0] * sizes[0]),
            bytes_accessed=2 * ranks * own.size,
            transcendentals=ranks * chans * 2 * tokens,
        ),
        name="mixer_forward",
    )(place, live, *tables, normed, own, *buffers)


def mixer_back_kernel(plan, orders, start, sizes, *refs):
    inputs, buffers, outs, scratch = grouped(refs, 9, len(plan), 6, 6)
    place_ref, live_ref, long_ref, short_ref, normed_ref, coming_ref = inputs[:6]
    proj_ref, long_out_ref, own_ref = inputs[6:]
    kept_ref, sent_ref = outs[:2]
    flat_ref, grads_ref, total, rows_ref, sems, out_sems = scratch
    long, short, chans, per_step = sizes
    fill(plan, place_ref, own_ref, buffers, flat_ref, sems, per_step)
    step = pl.program_id(0)
    layout = layout_of(long, short, normed_ref.shape[1])
    into, out_rows, filters = mixer_rows_of(flat_ref, step, per_step, chans)
    short_taps, cond_taps = mixer_taps(filters, long)
    rows = per_step * chans
    grad_mixed = nn(out_rows, coming_ref[...])
    proj = [proj_ref[0, g * rows : (g + 1) * rows].astype(F32) for g in range(3)]
    query, key_part, value_part = (taps_forward(layout, proj[g], short_taps[g]) for g in range(3))
    live = live_ref[:1]
    gated = key_part * value_part * live
    shaped = taps_forward(layout, gated, cond_taps)
    long_out = long_out_ref[0].astype(F32)
    mixed = (query * long_out).astype(BF16)
    grad_query = grad_mixed * long_out
    grad_long_out = sequences(layout, grad_mixed * query)
    gated_parts, shaped_parts = (sequences(layout, gated), sequences(layout, shaped))
    backs = [
        filter_back(
            filter_of(gated_parts[i], shaped_parts[i], filters[:, :length], ref[...]),
            grad_long_out[i],
            ref[...],
        )
        for i, (length, ref) in enumerate(((long, long_ref), (short, short_ref)))
    ]
    grad_gated = rejoined(backs[0][0], backs[1][0])
    grad_shaped = rejoined(backs[0][1], backs[1][1])
    grad_static = jnp.concatenate(
        [backs[0][2][:, :short] + backs[1][2], backs[0][2][:, short:]], axis=1
    )
    grad_cond = taps_grad(layout, grad_shaped, gated)
    grad_gated = (grad_gated + taps_back(layout, grad_shaped, cond_taps)) * live
    grads = (grad_query, grad_gated * value_part, grad_gated * key_part)
    grad_taps = [taps_grad(layout, grads[g], proj[g]) for g in range(3)]
    grad_proj = jnp.concatenate(
        [taps_back(layout, grads[g], short_taps[g]) for g in range(3)], axis=0
    ).astype(BF16)
    lane = lax.broadcasted_iota(jnp.int32, (1, flat_ref.shape[2] - long), 1)
    lanes = sum(
        jnp.where(lane == 3 * k + group, grad_taps[group][k], 0.0)
        for k in range(3)
        for group in range(3)
    )
    lanes += sum(jnp.where(lane == 9 + k, grad_cond[k], 0.0) for k in range(3))
    grad_into = nt(grad_proj, normed_ref[...]).astype(BF16)
    grad_out = nt(mixed, coming_ref[...]).astype(BF16)
    grad_filters = jnp.concatenate([grad_static, lanes], axis=1).astype(BF16)
    for i in range(per_step):
        part = slice(i * chans, (i + 1) * chans)
        at = step * per_step + i
        for g in range(3):
            grads_ref[at, g * chans : (g + 1) * chans] = grad_into[g * rows : (g + 1) * rows][part]
        grads_ref[at, 3 * chans : 4 * chans] = grad_out[part]
        grads_ref[at, 4 * chans : 5 * chans] = grad_filters[part]
        spare = flat_ref.shape[1] - 5 * chans
        if spare:
            grads_ref[at, 5 * chans :] = jnp.zeros((spare, flat_ref.shape[2]), BF16)
    count = flat_ref.shape[1] // (2 * len(orders[0]) // flat_ref.shape[0])
    spilled = (orders, count, start, place_ref, grads_ref, outs[2:], out_sems, per_step)
    spill(*spilled)
    add_total(total, tn(into, grad_proj))

    @pl.when(step == pl.num_programs(0) - 1)
    def finish():
        core = place_ref[0]
        kept_ref[...] = own_lanes(total, core, layout)
        sent_ref[...] = own_lanes(total, 1 - core, layout).astype(BF16)

    spill_wait(*spilled, True)


def mixer_back(place, rows, normed, coming, proj, long_out, live, tables, sizes, orders, start, into):
    own, buffers, plan, ranks = rows
    count, width = own.shape
    tokens = normed.shape[1]
    half = tokens // 2
    chans, per_step = sizes[2:]
    steps = ranks // per_step
    group = per_step * chans
    blocks = jax.ShapeDtypeStruct((len(orders[0]) // 2, into, width), BF16)
    results = pl.pallas_call(
        functools.partial(mixer_back_kernel, plan, orders, start, sizes),
        grid=(steps,),
        out_shape=[
            jax.ShapeDtypeStruct((width, half), F32),
            jax.ShapeDtypeStruct((width, half), BF16),
        ]
        + [blocks] * 4,
        in_specs=[SMEM, whole(live.shape)]
        + [whole(t.shape) for t in tables]
        + [
            whole((width, tokens)),
            whole((width, tokens)),
            pl.BlockSpec((1, 3 * group, tokens), lambda r: (r, 0, 0)),
            pl.BlockSpec((1, group, tokens), lambda r: (r, 0, 0)),
            ANY,
        ]
        + [ANY] * len(buffers),
        out_specs=[whole((width, half)), whole((width, half))] + [ANY] * 4,
        scratch_shapes=[
            pltpu.VMEM((ranks, count, width), BF16),
            pltpu.VMEM((ranks, count, width), BF16),
            pltpu.VMEM((width, tokens), F32),
            pltpu.VMEM((8, 128), F32),
            pltpu.SemaphoreType.DMA((ranks, 8)),
            pltpu.SemaphoreType.DMA((ranks, 8)),
        ],
        compiler_params=PARAMS,
        cost_estimate=pl.CostEstimate(
            flops=2 * ranks * chans * (8 * width * tokens + 16 * sizes[0] * sizes[0]),
            bytes_accessed=4 * ranks * own.size,
            transcendentals=ranks * chans * 2 * tokens,
        ),
        name="mixer_back",
    )(place, live, *tables, normed, coming, proj, long_out, own, *buffers)
    return (results[0], results[1], results[2:])


def final_copies(plan, start, place_ref, sources, flat_ref, sems):
    count = flat_ref.shape[1] // (2 * len(plan[0]))
    copies = []
    for side in range(2):
        core = place_ref[0] if side == 0 else 1 - place_ref[0]
        for half in range(2):
            for at, offset in enumerate(plan[half]):
                row = pl.multiple_of(((place_ref[1] ^ offset) * 2 + half) * count, 16)
                copies.append(
                    pltpu.make_async_copy(
                        sources[2 * side + half].at[at, pl.ds(start, count)],
                        flat_ref.at[core, pl.ds(row, count)],
                        sems.at[len(copies)],
                    )
                )
    return copies


def final_mlp_kernel(plan, start, aliased, *refs):
    (place_ref,), sources, _, outs, (flat_ref, sems) = grouped(
        refs, 1, 4, 2 if aliased else 0, 2, 2
    )
    up_ref, down_ref = outs
    step = pl.program_id(0)
    width = flat_ref.shape[2]
    hidden = flat_ref.shape[1] - width

    @pl.when(step == 0)
    def gather():
        copies = final_copies(plan, start, place_ref, sources, flat_ref, sems)
        for copy in copies:
            copy.start()
        for copy in copies:
            copy.wait()

    rows = up_ref.shape[1]
    part = pl.ds(pl.multiple_of(step * rows, 16), rows)
    for core in range(2):
        lanes = slice(core * hidden, (core + 1) * hidden)
        up_ref[0, :, 0, lanes] = flat_ref[core, part, :hidden].astype(F32)
        up_ref[0, :, 1, lanes] = flat_ref[core, part, hidden:].astype(F32)
    each = down_ref.shape[1]
    per_core = hidden // each
    at = pl.multiple_of(width + (step % per_core) * each, 16)
    down_ref[0] = flat_ref[step // per_core, pl.ds(at, each)].astype(F32)


def final_mlp(place, sources, plan, start, count, layer, layers, into):
    width = sources[0].shape[2]
    hidden = count - width
    steps = 4
    aliased = into is not None
    return pl.pallas_call(
        functools.partial(final_mlp_kernel, plan, start, aliased),
        grid=(steps,),
        out_shape=[
            jax.ShapeDtypeStruct((layers, width, 2, 2 * hidden), F32),
            jax.ShapeDtypeStruct((layers, 2 * hidden, width), F32),
        ],
        in_specs=[SMEM] + [ANY] * (6 if aliased else 4),
        out_specs=[
            pl.BlockSpec((1, width // steps, 2, 2 * hidden), lambda i: (layer, i, 0, 0)),
            pl.BlockSpec((1, 2 * hidden // steps, width), lambda i: (layer, i, 0)),
        ],
        input_output_aliases={5: 0, 6: 1} if aliased else {},
        scratch_shapes=[
            pltpu.VMEM((2, count, width), BF16),
            pltpu.SemaphoreType.DMA((4 * len(plan[0]),)),
        ],
        compiler_params=PARAMS,
        cost_estimate=pl.CostEstimate(
            flops=0, bytes_accessed=12 * count * width, transcendentals=0
        ),
        name="final_mlp",
    )(place, *sources, *(into if aliased else ()))


def final_mixer_kernel(plan, start, chans, aliased, *refs):
    (place_ref,), sources, _, outs, (flat_ref, sems) = grouped(
        refs, 1, 4, 3 if aliased else 0, 3, 2
    )
    into_ref, out_ref, filter_ref = outs
    copies = final_copies(plan, start, place_ref, sources, flat_ref, sems)
    for copy in copies:
        copy.start()
    for copy in copies:
        copy.wait()
    for core in range(2):
        lanes = slice(core * chans, (core + 1) * chans)
        for g in range(3):
            into_ref[0, g, lanes] = flat_ref[core, g * chans : (g + 1) * chans].astype(F32)
        out_ref[0, lanes] = flat_ref[core, 3 * chans : 4 * chans].astype(F32)
        filter_ref[0, lanes] = flat_ref[core, 4 * chans : 5 * chans].astype(F32)


def final_mixer(place, sources, plan, start, count, chans, layer, layers, into):
    width = sources[0].shape[2]
    aliased = into is not None
    return pl.pallas_call(
        functools.partial(final_mixer_kernel, plan, start, chans, aliased),
        grid=(1,),
        out_shape=[
            jax.ShapeDtypeStruct((layers, 3, 2 * chans, width), F32),
            jax.ShapeDtypeStruct((layers, 2 * chans, width), F32),
            jax.ShapeDtypeStruct((layers, 2 * chans, width), F32),
        ],
        in_specs=[SMEM] + [ANY] * (7 if aliased else 4),
        out_specs=[
            pl.BlockSpec((1, 3, 2 * chans, width), lambda i: (layer, 0, 0, 0)),
            pl.BlockSpec((1, 2 * chans, width), lambda i: (layer, 0, 0)),
            pl.BlockSpec((1, 2 * chans, width), lambda i: (layer, 0, 0)),
        ],
        input_output_aliases={5: 0, 6: 1, 7: 2} if aliased else {},
        scratch_shapes=[
            pltpu.VMEM((2, count, width), BF16),
            pltpu.SemaphoreType.DMA((4 * len(plan[0]),)),
        ],
        compiler_params=PARAMS,
        cost_estimate=pl.CostEstimate(
            flops=0, bytes_accessed=12 * count * width, transcendentals=0
        ),
        name="final_mixer",
    )(place, *sources, *(into if aliased else ()))


def norm_forward(values, gain):
    average = jnp.mean(values, axis=0, keepdims=True)
    centered = values - average
    inv_std = lax.rsqrt(jnp.mean(centered * centered, axis=0, keepdims=True) + EPS)
    normal_rows = centered * inv_std
    return ((normal_rows * gain).astype(BF16), (normal_rows, inv_std, gain))


def norm_back(grads, stored):
    normal_rows, inv_std, gain = stored
    scaled = grads * gain
    total = jnp.mean(scaled, axis=0, keepdims=True)
    crossed = jnp.mean(scaled * normal_rows, axis=0, keepdims=True)
    gain_grad = jnp.sum(grads * normal_rows, axis=1)
    return (inv_std * (scaled - total - normal_rows * crossed), gain_grad)


def on_device(
    input_long,
    input_short,
    length_long,
    length_short,
    gain_mixer,
    weight_in,
    short_taps,
    cond_taps,
    static_filter,
    weight_out,
    gain_mlp,
    weight_up,
    weight_down,
    grad_long,
    grad_short,
):
    count_long, seq_long, chan_width = input_long.shape
    count_short, seq_short = (input_short.shape[0], input_short.shape[1])
    layers = weight_in.shape[0]
    ranks = lax.axis_size("chan")
    pairs = lax.axis_size("batch") // 2
    place = lax.axis_index("chan")
    core = lax.axis_index("batch") % 2
    pair = lax.axis_index("batch") // 2
    width = chan_width * ranks
    hidden = weight_down.shape[1] // 2
    chans = chan_width // 2
    half_long = seq_long // 2
    tokens = half_long + seq_short
    mate = ("batch", 1)
    first = core == 0
    pieces = 4
    piece = pair % pieces
    plane = {1: ("batch", 2), 2: ("batch", 4)}
    extra_steps = []
    mask = 2 * pieces
    while mask < 2 * pairs:
        extra_steps.append(("batch", mask))
        mask *= 2
    spot = jnp.stack([core, piece]).astype(jnp.int32)
    plane_orders = ((1, 2), (2, 1))

    def exchange(blocks):
        came = [pick(blocks, place)]
        came += [swap(pick(blocks, place ^ r), ("chan", r)) for r in range(1, ranks)]
        return by_xor(jnp.stack(came), place)

    def to_tokens(long_rows, short_rows, extra=None):
        turned = jnp.swapaxes(long_rows, 1, 2).astype(BF16)
        halves = jnp.stack([turned[:, :, :half_long], turned[:, :, half_long:]])
        kept = pick(halves, core)
        came = swap(pick(halves, 1 - core), mate)
        ordered = jnp.where(first, jnp.concatenate([kept, came]), jnp.concatenate([came, kept]))
        parts = [ordered, jnp.swapaxes(short_rows, 1, 2).astype(BF16)]
        if extra is not None:
            parts.append(jnp.broadcast_to(extra[None], (ranks,) + extra.shape))
        gathered = exchange(jnp.concatenate(parts, axis=2))
        return gathered.reshape(width, -1)

    def from_tokens(values):
        gathered = exchange(values.reshape(ranks, chan_width, -1))
        halves = gathered[:, :, :half_long].reshape(2, count_long, chan_width, half_long)
        kept = pick(halves, core)
        came = swap(pick(halves, 1 - core), mate)
        ordered = jnp.where(
            first, jnp.concatenate([kept, came], axis=2), jnp.concatenate([came, kept], axis=2)
        )
        short_part = jnp.swapaxes(gathered[:, :, half_long:tokens], 1, 2)
        result = (jnp.swapaxes(ordered, 1, 2), short_part)
        return result + ((gathered[:, :, tokens:],) if values.shape[1] > tokens else ())

    def both_cores(values):
        return jnp.concatenate([values, swap(values, mate)], axis=1)

    def both_ordered(values):
        came = swap(values, mate)
        low, high = (jnp.where(first, values, came), jnp.where(first, came, values))
        return jnp.concatenate(
            [low[:, :half_long], high[:, :half_long], low[:, half_long:], high[:, half_long:]],
            axis=1,
        )

    def own_sum(sent, kept):
        return kept + swap(sent, mate).astype(F32)

    def mlp_rows(layer):
        up = lax.dynamic_slice_in_dim(weight_up[layer], core * hidden, hidden, 2)
        down = lax.dynamic_slice_in_dim(weight_down[layer], core * hidden, hidden, 0)
        return jnp.concatenate([up.reshape(width, 2 * hidden), down])

    def mixer_rows(layer):
        into = jnp.transpose(weight_in[layer], (1, 2, 0))
        into = lax.dynamic_slice_in_dim(into, core * chans, chans, 1)
        out = lax.dynamic_slice_in_dim(weight_out[layer], core * chans, chans, 0)
        taps = jnp.concatenate([short_taps[layer].reshape(9, chan_width), cond_taps[layer]]).T
        coarse = lax.reduce_precision(taps, 8, 7)
        static = jnp.concatenate([static_filter[layer].T, coarse, taps - coarse], axis=1)
        static = jnp.pad(static.astype(BF16), ((0, 0), (0, width - static.shape[1])))
        static = lax.dynamic_slice_in_dim(static, core * chans, chans, 0)
        spare = jnp.zeros((mixer_count - 5 * chans, width), BF16)
        return jnp.concatenate([into.reshape(3 * chans, width), out, static, spare])

    mixer_count = -(-5 * chans // (32 * pieces)) * 32 * pieces
    mlp_count = width + hidden
    own_rows = [
        {"mixer": mixer_rows(layer), "mlp": mlp_rows(layer)} for layer in range(layers)
    ]

    def half_rows(kind):
        return (mixer_count if kind == "mixer" else mlp_count) // (2 * pieces)

    def own_block(layer, kind, half):
        count = half_rows(kind)
        return lax.dynamic_slice_in_dim(
            own_rows[layer][kind], (piece * 2 + half) * count, count, 0
        )

    def gather_weights(wanted):
        parts = [own_block(layer, kind, half) for half in range(2) for layer, kind in wanted]
        block = jnp.concatenate(parts)[None]
        rows = block.shape[1] // 2
        far = swap(block, ("chan", FAR))
        near = swap(jnp.concatenate([block, far]), ("chan", NEAR))
        others = (FAR, NEAR, FAR ^ NEAR)
        foreign = jnp.concatenate([far, near])
        buffers, blocks = ([], [])
        for half in range(2):
            held = foreign[:, half * rows : (half + 1) * rows]
            held_blocks = [(0, other) for other in others]
            one, two = plane_orders[half]
            held = jnp.concatenate([held, swap(held, plane[one])])
            held_blocks = held_blocks + [(one, other) for other in others]
            buffers += [held, swap(held, plane[two])]
            blocks += [held_blocks, [(offset ^ two, other) for offset, other in held_blocks]]
        start = 0
        found = {}
        for layer, kind in wanted:
            count = half_rows(kind)
            plan = tuple((at // 2, tuple(blocks[at]), start, count) for at in range(4))
            found[layer, kind] = (own_rows[layer][kind], tuple(buffers), plan, ranks)
            start += count
        return found

    weights = gather_weights([(0, "mixer")])
    gains = jnp.stack([gain_mixer, gain_mlp], axis=1).reshape(2 * layers, chan_width)
    gains_coarse = lax.reduce_precision(gains, 8, 7)
    extra = jnp.concatenate([gains_coarse, gains - gains_coarse]).astype(BF16).T
    extra = jnp.pad(extra, ((0, 0), (0, 128 - extra.shape[1])))
    arrived = to_tokens(input_long, input_short, extra)
    gains = arrived[:, tokens:].astype(F32)
    gains = gains[:, : 2 * layers] + gains[:, 2 * layers : 4 * layers]
    gains = [[gains[:, 2 * layer + which][:, None] for which in range(2)] for layer in range(layers)]
    for layer in range(layers):
        wanted = [(layer, "mlp")] + ([(layer + 1, "mixer")] if layer + 1 < layers else [])
        weights.update(gather_weights(wanted))
    upstream = to_tokens(grad_long, grad_short).astype(F32)

    own_lengths = jnp.concatenate([length_long, length_short])
    other_lengths = swap(own_lengths, mate)
    low, high = (
        jnp.where(first, own_lengths, other_lengths),
        jnp.where(first, other_lengths, own_lengths),
    )
    spans = [pick(jnp.concatenate([low[:count_long], high[:count_long]]), place)]
    spans += [pick(side[count_long:], place) for side in (low, high)]
    live = jnp.concatenate(
        [
            jnp.arange(length) < span
            for length, span in zip((seq_long, seq_short, seq_short), spans)
        ]
    )
    live = jnp.broadcast_to(live.astype(F32)[None], (8, live.shape[0]))
    tables = (table(seq_long), table(seq_short))
    sizes = (seq_long, seq_short, chans, 2)

    residual_start = arrived[:, :tokens].astype(F32)
    residual = residual_start
    stored_all = []
    for layer in range(layers):
        normed, norm_stored = norm_forward(residual, gains[layer][0])
        normed = both_ordered(normed)
        proj, long_out, kept, sent = mixer_forward(
            spot, weights[layer, "mixer"], normed, live, tables, sizes
        )
        middle = residual + own_sum(sent, kept)
        normed_mlp, mlp_stored = norm_forward(middle, gains[layer][1])
        normed_mlp = both_cores(normed_mlp)
        gate_up, kept, sent = mlp_forward(spot, weights[layer, "mlp"], normed_mlp)
        residual = middle + own_sum(sent, kept)
        stored_all.append((normed, norm_stored, proj, long_out, normed_mlp, mlp_stored, gate_up))

    gone_long, gone_short = from_tokens((residual - residual_start).astype(BF16))
    output_long = input_long + gone_long.astype(F32)
    output_short = input_short + gone_short.astype(F32)

    orders = []
    for one, two in plane_orders:
        orders.append(
            tuple(
                (a * one + c * two, (b * NEAR) ^ (d * FAR))
                for a in range(2) for b in range(2) for c in range(2) for d in range(2)
            )
        )
    orders = tuple(orders)

    def scatter_grads(blocks):
        done = []
        for half in range(2):
            kept, sent = blocks[2 * half : 2 * half + 2]
            one, two = plane_orders[half]
            steps = [plane[one], ("chan", NEAR), plane[two], ("chan", FAR)]
            for at, step in enumerate(steps):
                came = swap(sent, step)
                middle = kept.shape[0] // 2
                if at + 1 < len(steps):
                    sent = (kept[middle:].astype(F32) + came[middle:].astype(F32)).astype(BF16)
                    kept = (kept[:middle].astype(F32) + came[:middle].astype(F32)).astype(BF16)
                else:
                    kept = (kept.astype(F32) + came.astype(F32)).astype(BF16)
            for step in extra_steps:
                kept = (kept.astype(F32) + swap(kept, step).astype(F32)).astype(BF16)
            done.append(kept)
        return done

    upstream_start = upstream
    reduced = []
    gain_grads = {}
    mlp_half, mixer_half = (half_rows("mlp"), half_rows("mixer"))
    blocks = mlp_half
    for layer in reversed(range(layers)):
        normed, norm_stored, proj, long_out, normed_mlp, mlp_stored, gate_up = stored_all[layer]
        coming = both_cores(upstream.astype(BF16))
        kept, sent, blocks = mlp_back(
            spot, weights[layer, "mlp"], normed_mlp, gate_up, coming, orders, 0, blocks
        )
        reduced.append(scatter_grads(blocks))
        change, gain_grads[layer, 1] = norm_back(own_sum(sent, kept), mlp_stored)
        upstream = upstream + change
        coming = both_ordered(upstream.astype(BF16))
        last = layer == 0
        kept, sent, blocks = mixer_back(
            spot, weights[layer, "mixer"], normed, coming, proj, long_out, live, tables, sizes,
            orders, 0 if last else mlp_half, mixer_half if last else mlp_half + mixer_half,
        )
        if last:
            reduced.append(scatter_grads(blocks))
        change, gain_grads[layer, 0] = norm_back(own_sum(sent, kept), norm_stored)
        upstream = upstream + change

    gain_parts = jnp.stack(
        [gain_grads[layer, which] for layer in range(layers) for which in range(2)], axis=1
    )
    gain_coarse = lax.reduce_precision(gain_parts, 8, 7)
    gain_lanes = jnp.concatenate([gain_coarse, gain_parts - gain_coarse], axis=1).astype(BF16)
    gain_lanes = jnp.pad(gain_lanes, ((0, 0), (0, 128 - gain_lanes.shape[1])))
    gone_long, gone_short, gain_sums = from_tokens(
        jnp.concatenate([(upstream - upstream_start).astype(BF16), gain_lanes], axis=1)
    )
    back_long = grad_long + gone_long.astype(F32)
    back_short = grad_short + gone_short.astype(F32)
    gain_sums = jnp.sum(gain_sums[:, :, : 4 * layers].astype(F32), axis=0)
    gain_sums = (gain_sums[:, : 2 * layers] + gain_sums[:, 2 * layers :]).T
    for step in [mate] + list(plane.values()) + extra_steps:
        gain_sums = gain_sums + swap(gain_sums, step)

    pair_orders = tuple((0, one, two, one ^ two) for one, two in plane_orders)

    def gather_grads(sums):
        halves = []
        for half in range(2):
            one, two = plane_orders[half]
            block = sums[half]
            block = jnp.concatenate([block, swap(block, plane[one])])
            halves.append(jnp.concatenate([block, swap(block, plane[two])]))
        return halves + [swap(block, mate) for block in halves]

    mlp_out, mixer_out = (None, None)
    for index, sums in enumerate(reduced):
        sources = gather_grads(sums)
        layer = layers - 1 - index
        if layer >= 0:
            mlp_out = final_mlp(
                spot, sources, pair_orders, 0, mlp_count, layer, layers, mlp_out
            )
        if index > 0:
            start = mlp_half if layer >= 0 else 0
            mixer_out = final_mixer(
                spot, sources, pair_orders, start, mixer_count, chans, layer + 1, layers, mixer_out
            )
    into_out, out_out, filter_out = mixer_out
    taps = jnp.swapaxes(filter_out[:, :, seq_long : seq_long + 12], 1, 2)

    return (
        output_long,
        output_short,
        back_long,
        back_short,
        gain_sums[0::2],
        jnp.transpose(into_out, (0, 3, 1, 2)),
        taps[:, :9].reshape(layers, 3, 3, chan_width),
        taps[:, 9:],
        jnp.swapaxes(filter_out[:, :, :seq_long], 1, 2),
        out_out,
        gain_sums[1::2],
        mlp_out[0],
        mlp_out[1],
    )


def solution(mesh):
    tokens = P("batch", None, "chan")
    placed = (
        tokens,
        tokens,
        P("batch"),
        P("batch"),
        P(None, "chan"),
        P(None, None, None, "chan"),
        P(None, None, None, "chan"),
        P(None, None, "chan"),
        P(None, None, "chan"),
        P(None, "chan", None),
        P(None, "chan"),
        P(None, None, None, "chan"),
        P(None, "chan", None),
        tokens,
        tokens,
    )
    return jax.shard_map(
        on_device,
        mesh=mesh,
        in_specs=placed,
        out_specs=(tokens,) * 4 + placed[4:13],
        check_vma=False,
    )
```

```python
import functools
import math

import jax
import jax.numpy as jnp
import numpy as np
from jax import lax
from jax.experimental import pallas as pl
from jax.experimental.pallas import tpu as pltpu
from jax.sharding import PartitionSpec as P

EPS = 1e-05
BF16 = jnp.bfloat16
F32 = jnp.float32
VMEM_BYTES = 52 * 2**20
FAR, NEAR = (3, 1)


def nn(left, right):
    return lax.dot_general(left, right, (((1,), (0,)), ((), ())), preferred_element_type=F32)


def nt(left, right):
    return lax.dot_general(left, right, (((1,), (1,)), ((), ())), preferred_element_type=F32)


def tn(left, right):
    return lax.dot_general(left, right, (((0,), (0,)), ((), ())), preferred_element_type=F32)


def table(length):
    places = np.arange(length)[:, None]
    phase = (places * np.arange(length + 1)[None, :] % (2 * length)) * (np.pi / length)
    packed = np.concatenate(
        [np.cos(phase[:, :length]), np.cos(phase[:, length:]), -np.sin(phase[:, 1:length])], axis=1
    )
    return jnp.asarray(packed.astype(np.float32)).astype(BF16)


def swap(values, step):
    axis, mask = step
    return lax.ppermute(values, axis, [(i, i ^ mask) for i in range(lax.axis_size(axis))])


def after(values, *others):
    return lax.optimization_barrier((values,) + others)[0]


def pick(values, index):
    return lax.dynamic_index_in_dim(values, index, 0, keepdims=False)


def by_xor(values, index):
    return jnp.stack([pick(values, place ^ index) for place in range(values.shape[0])])


def block_copies(plan, place_ref, own_ref, buffers, flat_ref, sems, wanted):
    if wanted == 0:
        return [pltpu.make_async_copy(own_ref, flat_ref.at[0], sems.at[0, 0])]
    copies = []
    for buffer, (half, blocks, start, count) in zip(buffers, plan):
        for at, (offset, other) in enumerate(blocks):
            if other == wanted:
                row = pl.multiple_of(((place_ref[1] ^ offset) * 2 + half) * count, 16)
                copies.append(
                    pltpu.make_async_copy(
                        buffer.at[at, pl.ds(start, count)],
                        flat_ref.at[wanted, pl.ds(row, count)],
                        sems.at[wanted, len(copies)],
                    )
                )
    return copies


def fill(plan, place_ref, own_ref, buffers, flat_ref, sems, per_step):
    step = pl.program_id(0)
    ranks = flat_ref.shape[0]
    args = (plan, place_ref, own_ref, buffers, flat_ref, sems)

    @pl.when(step == 0)
    def begin():
        for wanted in range(ranks):
            for copy in block_copies(*args, wanted):
                copy.start()

    for wanted in range(ranks):

        @pl.when(step == wanted // per_step)
        def arrive():
            for copy in block_copies(*args, wanted):
                copy.wait()


def spill_copies(routes, count, place_ref, rows_ref, outs, sems, slot, wanted):
    copies = []
    for targets, half, offset, start in routes:
        out, at = targets[wanted]
        row = pl.multiple_of(((place_ref[1] ^ offset) * 2 + half) * count, 16)
        copies.append(
            pltpu.make_async_copy(
                rows_ref.at[slot, pl.ds(row, count)],
                outs[out].at[at, pl.ds(start, count)],
                sems.at[slot, len(copies)],
            )
        )
    return copies


def grouped(refs, *counts):
    groups, at = ([], 0)
    for count in counts:
        groups.append(refs[at : at + count])
        at += count
    return groups


def whole(shape):
    return pl.BlockSpec(shape, lambda i: (0,) * len(shape))


SMEM = pl.BlockSpec(memory_space=pltpu.SMEM)
ANY = pl.BlockSpec(memory_space=pl.ANY)
PARAMS = pltpu.CompilerParams(vmem_limit_bytes=VMEM_BYTES)


def gelu_parts(gate):
    slope = math.sqrt(2.0 / math.pi)
    square = gate * gate
    bent = jnp.tanh(slope * (gate + 0.044715 * square * gate))
    gelu = 0.5 * gate * (1.0 + bent)
    grad = 0.5 * (1.0 + bent) + 0.5 * gate * (1.0 - bent * bent) * slope * (
        1.0 + 0.134145 * square
    )
    return (gelu, grad)


def add_total(total, part):
    step = pl.program_id(0)

    @pl.when(step == 0)
    def start():
        total[...] = part

    @pl.when(step > 0)
    def add():
        total[...] += part


def split_total(total, kept_ref, sent_ref):
    @pl.when(pl.program_id(0) == pl.num_programs(0) - 1)
    def finish():
        own = kept_ref.shape[1]
        kept_ref[...] = total[:, :own]
        sent_ref[...] = total[:, own:].astype(BF16)


def mlp_forward_kernel(plan, *refs):
    (place_ref, normed_ref, own_ref), buffers, outs, scratch = grouped(refs, 3, len(plan), 3, 3)
    gate_up_ref, kept_ref, sent_ref = outs
    flat_ref, total, sems = scratch
    fill(plan, place_ref, own_ref, buffers, flat_ref, sems, 1)
    step = pl.program_id(0)
    width = normed_ref.shape[0]
    hidden = flat_ref.shape[1] - width
    gate_up = tn(flat_ref[step, :width], normed_ref[...])
    gate_up_ref[0] = gate_up.astype(BF16)
    activated = (gelu_parts(gate_up[:hidden])[0] * gate_up[hidden:]).astype(BF16)
    add_total(total, tn(flat_ref[step, width:], activated))
    split_total(total, kept_ref, sent_ref)


def mlp_forward(place, rows, normed):
    own, buffers, plan, ranks = rows
    count, width = own.shape
    tokens = normed.shape[1]
    hidden = count - width
    half = tokens // 2
    return pl.pallas_call(
        functools.partial(mlp_forward_kernel, plan),
        grid=(ranks,),
        out_shape=[
            jax.ShapeDtypeStruct((ranks, 2 * hidden, tokens), BF16),
            jax.ShapeDtypeStruct((width, half), F32),
            jax.ShapeDtypeStruct((width, half), BF16),
        ],
        in_specs=[SMEM, whole((width, tokens)), ANY] + [ANY] * len(buffers),
        out_specs=[
            pl.BlockSpec((1, 2 * hidden, tokens), lambda r: (r, 0, 0)),
            whole((width, half)),
            whole((width, half)),
        ],
        scratch_shapes=[
            pltpu.VMEM((ranks, count, width), BF16),
            pltpu.VMEM((width, tokens), F32),
            pltpu.SemaphoreType.DMA((ranks, 8)),
        ],
        compiler_params=PARAMS,
        cost_estimate=pl.CostEstimate(flops=1, bytes_accessed=1, transcendentals=0),
        name="mlp_forward",
    )(place, normed, own, *buffers)


def spill(routes, count, place_ref, grads_ref, outs, sems, per_step):
    step = pl.program_id(0)
    ranks = per_step * pl.num_programs(0)
    for wanted in range(ranks):
        at = wanted // per_step
        slot = (at % 2) * per_step + wanted % per_step

        @pl.when(step == at)
        def leave():
            for copy in spill_copies(
                routes, count, place_ref, grads_ref, outs, sems, slot, wanted
            ):
                copy.start()


def spill_wait(routes, count, place_ref, grads_ref, outs, sems, per_step, last):
    step = pl.program_id(0)
    steps = 4 // per_step
    for wanted in range(4):
        at = wanted // per_step
        slot = (at % 2) * per_step + wanted % per_step
        due = steps - 1 if last else at + 2
        if last and at + 2 < steps:
            continue
        if not last and at + 2 >= steps:
            continue

        @pl.when(step == due)
        def gone():
            for copy in spill_copies(
                routes, count, place_ref, grads_ref, outs, sems, slot, wanted
            ):
                copy.wait()


def mlp_back_kernel(plan, routes, count, *refs):
    (place_ref, normed_ref, coming_ref, gate_up_ref, own_ref), buffers, outs, scratch = grouped(
        refs, 5, len(plan), 6, 5
    )
    kept_ref, sent_ref = outs[:2]
    flat_ref, grads_ref, total, sems, out_sems = scratch
    fill(plan, place_ref, own_ref, buffers, flat_ref, sems, 1)
    step = pl.program_id(0)
    width = normed_ref.shape[0]
    hidden = flat_ref.shape[1] - width
    spilled = (routes, count, place_ref, grads_ref, outs[2:], out_sems, 1)
    spill_wait(*spilled, False)
    slot = step % 2
    gate = gate_up_ref[0, :hidden].astype(F32)
    up = gate_up_ref[0, hidden:].astype(F32)
    grad_act = nn(flat_ref[step, width:], coming_ref[...])
    gelu, slope = gelu_parts(gate)
    activated = (gelu * up).astype(BF16)
    grad_gate = (grad_act * up * slope).astype(BF16)
    grad_up = (grad_act * gelu).astype(BF16)
    grads_ref[slot, width:] = nt(activated, coming_ref[...]).astype(BF16)
    grads_ref[slot, :width, :hidden] = nt(normed_ref[...], grad_gate).astype(BF16)
    grads_ref[slot, :width, hidden:] = nt(normed_ref[...], grad_up).astype(BF16)
    spill(*spilled)
    add_total(
        total,
        nn(flat_ref[step, :width, :hidden], grad_gate)
        + nn(flat_ref[step, :width, hidden:], grad_up),
    )
    split_total(total, kept_ref, sent_ref)
    spill_wait(*spilled, True)


def mlp_back(place, rows, normed, gate_up, coming, routes, blocks, block_rows):
    own, buffers, plan, ranks = rows
    count, width = own.shape
    tokens = normed.shape[1]
    hidden = count - width
    half = tokens // 2
    results = pl.pallas_call(
        functools.partial(mlp_back_kernel, plan, routes, plan[0][3]),
        grid=(ranks,),
        out_shape=[
            jax.ShapeDtypeStruct((width, half), F32),
            jax.ShapeDtypeStruct((width, half), BF16),
        ]
        + [jax.ShapeDtypeStruct((blocks, block_rows, width), BF16)] * 4,
        in_specs=[
            SMEM,
            whole((width, tokens)),
            whole((width, tokens)),
            pl.BlockSpec((1, 2 * hidden, tokens), lambda r: (r, 0, 0)),
            ANY,
        ]
        + [ANY] * len(buffers),
        out_specs=[whole((width, half)), whole((width, half))] + [ANY] * 4,
        scratch_shapes=[
            pltpu.VMEM((ranks, count, width), BF16),
            pltpu.VMEM((2, count, width), BF16),
            pltpu.VMEM((width, tokens), F32),
            pltpu.SemaphoreType.DMA((ranks, 8)),
            pltpu.SemaphoreType.DMA((2, 8)),
        ],
        compiler_params=PARAMS,
        cost_estimate=pl.CostEstimate(
            flops=12 * ranks * hidden * width * tokens,
            bytes_accessed=4 * ranks * own.size + 4 * ranks * hidden * tokens,
            transcendentals=ranks * hidden * tokens,
        ),
        name="mlp_back",
    )(place, normed, coming, gate_up, own, *buffers)
    return (results[0], results[1], results[2:])


def delayed(layout, values, by):
    return jnp.where(layout["inside"] >= by, pltpu.roll(values, by, 1), 0.0)


def advanced(layout, values, by):
    moved = pltpu.roll(values, layout["tokens"] - by, 1)
    return jnp.where(layout["inside"] < layout["length"] - by, moved, 0.0)


def layout_of(long, short, tokens):
    lane = lax.broadcasted_iota(jnp.int32, (1, tokens), 1)
    return {
        "long": long,
        "short": short,
        "tokens": tokens,
        "inside": jnp.where(lane < long, lane, (lane - long) % short),
        "length": jnp.where(lane < long, long, short),
    }


def taps_forward(layout, values, taps):
    return (
        taps[0] * values
        + taps[1] * delayed(layout, values, 1)
        + taps[2] * delayed(layout, values, 2)
    )


def taps_back(layout, values, taps):
    return (
        taps[0] * values
        + taps[1] * advanced(layout, values, 1)
        + taps[2] * advanced(layout, values, 2)
    )


def taps_grad(layout, grads, values):
    moved = [values, delayed(layout, values, 1), delayed(layout, values, 2)]
    return [jnp.sum(grads * value, axis=1, keepdims=True) for value in moved]


def sequences(layout, values):
    long, short = (layout["long"], layout["short"])
    shorts = [values[:, at : at + short] for at in range(long, layout["tokens"], short)]
    return (values[:, :long], jnp.concatenate(shorts, axis=0))


def rejoined(long_part, short_part):
    rows = long_part.shape[0]
    shorts = [short_part[at * rows : (at + 1) * rows] for at in range(short_part.shape[0] // rows)]
    return jnp.concatenate([long_part] + shorts, axis=1)


def repeated(values, times):
    return jnp.concatenate([values] * times, axis=0) if times > 1 else values


def at_edge(edge, edge_values, others):
    head = jnp.where(edge[:, :128], edge_values, others[:, :128])
    return jnp.concatenate([head, others[:, 128:]], axis=1) if others.shape[1] > 128 else head


def turned_back(real_part, imag_part, cosines):
    return nt(jnp.concatenate([real_part.astype(BF16), imag_part.astype(BF16)], axis=1), cosines)


def filter_of(gated, shaped, static_rows, cosines):
    rows, length = gated.shape
    times = rows // static_rows.shape[0]
    edge = lax.broadcasted_iota(jnp.int32, (1, length), 1) == 0
    spectra = nn(jnp.concatenate([gated, shaped], axis=0).astype(BF16), cosines)
    shaped_re, shaped_im = (spectra[rows:, :length], spectra[rows:, length:])
    fixed = nn(static_rows, cosines)
    fixed_re = repeated(fixed[:, :length], times)
    fixed_im = repeated(fixed[:, length:], times)
    square = shaped_im * shaped_im
    power = shaped_re * shaped_re + jnp.where(edge, 0.0, square) + length
    inv_root = lax.rsqrt(power)
    power_last = square[:, :128] + length
    inv_root_last = lax.rsqrt(power_last)
    scale = 1.0 / math.sqrt(length)
    return {
        "length": length,
        "times": times,
        "edge": edge,
        "weight": jnp.where(edge, 0.5 / length, 1.0 / length),
        "signal_re": spectra[:rows, :length],
        "signal_im": spectra[:rows, length:],
        "shaped_re": shaped_re,
        "shaped_im": shaped_im,
        "fixed_im": fixed_im,
        "fixed_sine": jnp.where(edge, 0.0, fixed_im),
        "slope": scale * inv_root,
        "slope_last": scale * inv_root_last,
        "filter_re": fixed_re + (power * inv_root * scale - 1.0),
        "filter_last": fixed_im[:, :128] + (power_last * inv_root_last * scale - 1.0),
    }


def filtered(parts, cosines):
    signal_re, signal_im = (parts["signal_re"], parts["signal_im"])
    product_re = parts["filter_re"] * signal_re - parts["fixed_sine"] * signal_im
    product_im = at_edge(
        parts["edge"],
        parts["filter_last"] * signal_im[:, :128],
        parts["filter_re"] * signal_im + parts["fixed_im"] * signal_re,
    )
    return turned_back(product_re * parts["weight"], product_im * parts["weight"], cosines)


def filter_back(parts, grad_out, cosines):
    length, times, edge = (parts["length"], parts["times"], parts["edge"])
    signal_re, signal_im = (parts["signal_re"], parts["signal_im"])
    filter_re, fixed_im = (parts["filter_re"], parts["fixed_im"])
    turned = nn(grad_out.astype(BF16), cosines)
    product_re = turned[:, :length] * parts["weight"]
    product_im = turned[:, length:] * parts["weight"]
    grad_signal_re = filter_re * product_re + parts["fixed_sine"] * product_im
    grad_signal_im = at_edge(
        edge,
        parts["filter_last"] * product_im[:, :128],
        filter_re * product_im - fixed_im * product_re,
    )
    crossed = signal_im * product_im
    grad_filter = signal_re * product_re + jnp.where(edge, 0.0, crossed)
    grad_fixed_im = at_edge(
        edge, crossed[:, :128], signal_re * product_im - signal_im * product_re
    )
    slope = grad_filter * parts["slope"]
    grad_shaped_re = slope * parts["shaped_re"]
    grad_shaped_im = (
        at_edge(edge, crossed[:, :128] * parts["slope_last"], slope) * parts["shaped_im"]
    )
    count = grad_out.shape[0]
    rows = count // times
    grad_static = turned_back(
        sum(grad_filter[i * rows : (i + 1) * rows] for i in range(times)),
        sum(grad_fixed_im[i * rows : (i + 1) * rows] for i in range(times)),
        cosines,
    )
    back = turned_back(
        jnp.concatenate([grad_signal_re, grad_shaped_re], axis=0),
        jnp.concatenate([grad_signal_im, grad_shaped_im], axis=0),
        cosines,
    )
    return (back[:count], back[count:], grad_static)


def mixer_rows_of(flat_ref, step, per_step, chans):
    def rows(index):
        return [
            flat_ref[step * per_step + i, index * chans : (index + 1) * chans]
            for i in range(per_step)
        ]

    into = jnp.concatenate(rows(0) + rows(1) + rows(2), axis=0)
    filters = jnp.concatenate(rows(4), axis=0)
    return (into, jnp.concatenate(rows(3), axis=0), filters)


def mixer_taps(filters, start):
    lanes = filters[:, start : start + 128].astype(F32)
    taps = [lanes[:, k : k + 1] + lanes[:, 12 + k : 13 + k] for k in range(12)]
    return ([[taps[3 * k + group] for k in range(3)] for group in range(3)], taps[9:])


def own_lanes(ref, which, layout):
    half_long, short = (layout["long"] // 2, layout["short"])
    at = pl.multiple_of(which * half_long, 128)
    after = pl.multiple_of(layout["long"] + which * short, 128)
    return jnp.concatenate([ref[:, pl.ds(at, half_long)], ref[:, pl.ds(after, short)]], axis=1)


def mixer_forward_kernel(plan, sizes, *refs):
    inputs, buffers, outs, scratch = grouped(refs, 6, len(plan), 4, 4)
    place_ref, live_ref, long_ref, short_ref, normed_ref, own_ref = inputs
    proj_ref, long_out_ref, kept_ref, sent_ref = outs
    flat_ref, mixed_ref, total, sems = scratch
    long, short, chans, per_step = sizes
    fill(plan, place_ref, own_ref, buffers, flat_ref, sems, per_step)
    step = pl.program_id(0)
    layout = layout_of(long, short, normed_ref.shape[1])
    into, out_rows, filters = mixer_rows_of(flat_ref, step, per_step, chans)
    short_taps, cond_taps = mixer_taps(filters, long)
    rows = per_step * chans
    proj = nn(into, normed_ref[...])
    proj_ref[0] = proj.astype(BF16)
    query, key_part, value_part = (
        taps_forward(layout, proj[g * rows : (g + 1) * rows], short_taps[g]) for g in range(3)
    )
    gated = key_part * value_part * live_ref[:1]
    shaped = taps_forward(layout, gated, cond_taps)
    gated_parts, shaped_parts = (sequences(layout, gated), sequences(layout, shaped))
    results = [
        filtered(
            filter_of(gated_parts[i], shaped_parts[i], filters[:, :length], ref[...]), ref[...]
        )
        for i, (length, ref) in enumerate(((long, long_ref), (short, short_ref)))
    ]
    long_out = rejoined(*results)
    long_out_ref[0] = long_out.astype(BF16)
    mixed_ref[...] = (query * long_out).astype(BF16)
    core = place_ref[0]
    half = kept_ref.shape[1]
    part_kept = tn(out_rows, own_lanes(mixed_ref, core, layout))
    part_sent = tn(out_rows, own_lanes(mixed_ref, 1 - core, layout))
    add_total(total, jnp.concatenate([part_kept, part_sent], axis=1))
    split_total(total, kept_ref, sent_ref)


def mixer_forward(place, rows, normed, live, tables, sizes):
    own, buffers, plan, ranks = rows
    count, width = own.shape
    tokens = normed.shape[1]
    half = tokens // 2
    chans, per_step = sizes[2:]
    steps = ranks // per_step
    group = per_step * chans
    return pl.pallas_call(
        functools.partial(mixer_forward_kernel, plan, sizes),
        grid=(steps,),
        out_shape=[
            jax.ShapeDtypeStruct((steps, 3 * group, tokens), BF16),
            jax.ShapeDtypeStruct((steps, group, tokens), BF16),
            jax.ShapeDtypeStruct((width, half), F32),
            jax.ShapeDtypeStruct((width, half), BF16),
        ],
        in_specs=[SMEM, whole(live.shape)]
        + [whole(t.shape) for t in tables]
        + [whole((width, tokens)), ANY]
        + [ANY] * len(buffers),
        out_specs=[
            pl.BlockSpec((1, 3 * group, tokens), lambda r: (r, 0, 0)),
            pl.BlockSpec((1, group, tokens), lambda r: (r, 0, 0)),
            whole((width, half)),
            whole((width, half)),
        ],
        scratch_shapes=[
            pltpu.VMEM((ranks, count, width), BF16),
            pltpu.VMEM((group, tokens), BF16),
            pltpu.VMEM((width, tokens), F32),
            pltpu.SemaphoreType.DMA((ranks, 8)),
        ],
        compiler_params=PARAMS,
        cost_estimate=pl.CostEstimate(flops=1, bytes_accessed=1, transcendentals=0),
        name="mixer_forward",
    )(place, live, *tables, normed, own, *buffers)


def mixer_back_kernel(plan, routes, count, sizes, targets, *refs):
    inputs, buffers, outs, scratch = grouped(refs, 9, len(plan), 2 + targets, 6)
    place_ref, live_ref, long_ref, short_ref, normed_ref, coming_ref = inputs[:6]
    proj_ref, long_out_ref, own_ref = inputs[6:]
    kept_ref, sent_ref = outs[:2]
    flat_ref, grads_ref, total, rows_ref, sems, out_sems = scratch
    long, short, chans, per_step = sizes
    fill(plan, place_ref, own_ref, buffers, flat_ref, sems, per_step)
    step = pl.program_id(0)
    layout = layout_of(long, short, normed_ref.shape[1])
    into, out_rows, filters = mixer_rows_of(flat_ref, step, per_step, chans)
    short_taps, cond_taps = mixer_taps(filters, long)
    rows = per_step * chans
    grad_mixed = nn(out_rows, coming_ref[...])
    proj = [proj_ref[0, g * rows : (g + 1) * rows].astype(F32) for g in range(3)]
    query, key_part, value_part = (taps_forward(layout, proj[g], short_taps[g]) for g in range(3))
    live = live_ref[:1]
    gated = key_part * value_part * live
    shaped = taps_forward(layout, gated, cond_taps)
    long_out = long_out_ref[0].astype(F32)
    mixed = (query * long_out).astype(BF16)
    grad_query = grad_mixed * long_out
    grad_long_out = sequences(layout, grad_mixed * query)
    gated_parts, shaped_parts = (sequences(layout, gated), sequences(layout, shaped))
    backs = [
        filter_back(
            filter_of(gated_parts[i], shaped_parts[i], filters[:, :length], ref[...]),
            grad_long_out[i],
            ref[...],
        )
        for i, (length, ref) in enumerate(((long, long_ref), (short, short_ref)))
    ]
    grad_gated = rejoined(backs[0][0], backs[1][0])
    grad_shaped = rejoined(backs[0][1], backs[1][1])
    grad_static = jnp.concatenate(
        [backs[0][2][:, :short] + backs[1][2], backs[0][2][:, short:]], axis=1
    )
    grad_cond = taps_grad(layout, grad_shaped, gated)
    grad_gated = (grad_gated + taps_back(layout, grad_shaped, cond_taps)) * live
    grads = (grad_query, grad_gated * value_part, grad_gated * key_part)
    grad_taps = [taps_grad(layout, grads[g], proj[g]) for g in range(3)]
    grad_proj = jnp.concatenate(
        [taps_back(layout, grads[g], short_taps[g]) for g in range(3)], axis=0
    ).astype(BF16)
    lane = lax.broadcasted_iota(jnp.int32, (1, flat_ref.shape[2] - long), 1)
    lanes = sum(
        jnp.where(lane == 3 * k + group, grad_taps[group][k], 0.0)
        for k in range(3)
        for group in range(3)
    )
    lanes += sum(jnp.where(lane == 9 + k, grad_cond[k], 0.0) for k in range(3))
    grad_into = nt(grad_proj, normed_ref[...]).astype(BF16)
    grad_out = nt(mixed, coming_ref[...]).astype(BF16)
    grad_filters = jnp.concatenate([grad_static, lanes], axis=1).astype(BF16)
    for i in range(per_step):
        part = slice(i * chans, (i + 1) * chans)
        at = step * per_step + i
        for g in range(3):
            grads_ref[at, g * chans : (g + 1) * chans] = grad_into[g * rows : (g + 1) * rows][part]
        grads_ref[at, 3 * chans : 4 * chans] = grad_out[part]
        grads_ref[at, 4 * chans : 5 * chans] = grad_filters[part]
        spare = flat_ref.shape[1] - 5 * chans
        if spare:
            grads_ref[at, 5 * chans :] = jnp.zeros((spare, flat_ref.shape[2]), BF16)
    spilled = (routes, count, place_ref, grads_ref, outs[2:], out_sems, per_step)
    spill(*spilled)
    add_total(total, tn(into, grad_proj))

    @pl.when(step == pl.num_programs(0) - 1)
    def finish():
        core = place_ref[0]
        kept_ref[...] = own_lanes(total, core, layout)
        sent_ref[...] = own_lanes(total, 1 - core, layout).astype(BF16)

    spill_wait(*spilled, True)


def mixer_back(
    place, rows, normed, coming, proj, long_out, live, tables, sizes, routes, blocks, block_rows
):
    outs = 1 + max(target[0] for route in routes for target in route[0].values())
    own, buffers, plan, ranks = rows
    count, width = own.shape
    tokens = normed.shape[1]
    half = tokens // 2
    chans, per_step = sizes[2:]
    steps = ranks // per_step
    group = per_step * chans
    results = pl.pallas_call(
        functools.partial(mixer_back_kernel, plan, routes, plan[0][3], sizes, outs),
        grid=(steps,),
        out_shape=[
            jax.ShapeDtypeStruct((width, half), F32),
            jax.ShapeDtypeStruct((width, half), BF16),
        ]
        + [jax.ShapeDtypeStruct((blocks, block_rows, width), BF16)] * outs,
        in_specs=[SMEM, whole(live.shape)]
        + [whole(t.shape) for t in tables]
        + [
            whole((width, tokens)),
            whole((width, tokens)),
            pl.BlockSpec((1, 3 * group, tokens), lambda r: (r, 0, 0)),
            pl.BlockSpec((1, group, tokens), lambda r: (r, 0, 0)),
            ANY,
        ]
        + [ANY] * len(buffers),
        out_specs=[whole((width, half)), whole((width, half))] + [ANY] * outs,
        scratch_shapes=[
            pltpu.VMEM((ranks, count, width), BF16),
            pltpu.VMEM((ranks, count, width), BF16),
            pltpu.VMEM((width, tokens), F32),
            pltpu.VMEM((8, 128), F32),
            pltpu.SemaphoreType.DMA((ranks, 8)),
            pltpu.SemaphoreType.DMA((ranks, 8)),
        ],
        compiler_params=PARAMS,
        cost_estimate=pl.CostEstimate(flops=1, bytes_accessed=1, transcendentals=0),
        name="mixer_back",
    )(place, live, *tables, normed, coming, proj, long_out, own, *buffers)
    return (results[0], results[1], results[2:])


def final_copies(place_ref, sources, flat_ref, sems):
    copies = []
    for side, source in enumerate(sources):
        core = place_ref[0] if side == 0 else 1 - place_ref[0]
        count = source.shape[1]
        for offset in range(source.shape[0]):
            row = pl.multiple_of((place_ref[1] ^ offset) * count, 16)
            copies.append(
                pltpu.make_async_copy(
                    source.at[offset], flat_ref.at[core, pl.ds(row, count)], sems.at[len(copies)]
                )
            )
    return copies


def final_mlp_kernel(aliased, *refs):
    (place_ref,), sources, _, outs, (flat_ref, sems) = grouped(
        refs, 1, 2, 2 if aliased else 0, 2, 2
    )
    up_ref, down_ref = outs
    step = pl.program_id(0)
    width = flat_ref.shape[2]
    hidden = flat_ref.shape[1] - width

    @pl.when(step == 0)
    def gather():
        copies = final_copies(place_ref, sources, flat_ref, sems)
        for copy in copies:
            copy.start()
        for copy in copies:
            copy.wait()

    rows = up_ref.shape[1]
    part = pl.ds(pl.multiple_of(step * rows, 16), rows)
    for core in range(2):
        lanes = slice(core * hidden, (core + 1) * hidden)
        up_ref[0, :, 0, lanes] = flat_ref[core, part, :hidden].astype(F32)
        up_ref[0, :, 1, lanes] = flat_ref[core, part, hidden:].astype(F32)
    each = down_ref.shape[1]
    per_core = hidden // each
    at = pl.multiple_of(width + (step % per_core) * each, 16)
    down_ref[0] = flat_ref[step // per_core, pl.ds(at, each)].astype(F32)


def final_mlp(place, sources, count, layer, layers, into):
    width = sources[0].shape[2]
    hidden = count - width
    steps = 4
    aliased = into is not None
    return pl.pallas_call(
        functools.partial(final_mlp_kernel, aliased),
        grid=(steps,),
        out_shape=[
            jax.ShapeDtypeStruct((layers, width, 2, 2 * hidden), F32),
            jax.ShapeDtypeStruct((layers, 2 * hidden, width), F32),
        ],
        in_specs=[SMEM] + [ANY] * (4 if aliased else 2),
        out_specs=[
            pl.BlockSpec((1, width // steps, 2, 2 * hidden), lambda i: (layer, i, 0, 0)),
            pl.BlockSpec((1, 2 * hidden // steps, width), lambda i: (layer, i, 0)),
        ],
        input_output_aliases={3: 0, 4: 1} if aliased else {},
        scratch_shapes=[
            pltpu.VMEM((2, count, width), BF16),
            pltpu.SemaphoreType.DMA((2 * sources[0].shape[0],)),
        ],
        compiler_params=PARAMS,
        cost_estimate=pl.CostEstimate(flops=1, bytes_accessed=1, transcendentals=0),
        name="final_mlp",
    )(place, *sources, *(into if aliased else ()))


def final_mixer_kernel(chans, aliased, *refs):
    (place_ref,), sources, _, outs, (flat_ref, sems) = grouped(
        refs, 1, 2, 3 if aliased else 0, 3, 2
    )
    into_ref, out_ref, filter_ref = outs
    copies = final_copies(place_ref, sources, flat_ref, sems)
    for copy in copies:
        copy.start()
    for copy in copies:
        copy.wait()
    for core in range(2):
        lanes = slice(core * chans, (core + 1) * chans)
        for g in range(3):
            into_ref[0, g, lanes] = flat_ref[core, g * chans : (g + 1) * chans].astype(F32)
        out_ref[0, lanes] = flat_ref[core, 3 * chans : 4 * chans].astype(F32)
        filter_ref[0, lanes] = flat_ref[core, 4 * chans : 5 * chans].astype(F32)


def final_mixer(place, sources, count, chans, layer, layers, into):
    width = sources[0].shape[2]
    aliased = into is not None
    return pl.pallas_call(
        functools.partial(final_mixer_kernel, chans, aliased),
        grid=(1,),
        out_shape=[
            jax.ShapeDtypeStruct((layers, 3, 2 * chans, width), F32),
            jax.ShapeDtypeStruct((layers, 2 * chans, width), F32),
            jax.ShapeDtypeStruct((layers, 2 * chans, width), F32),
        ],
        in_specs=[SMEM] + [ANY] * (5 if aliased else 2),
        out_specs=[
            pl.BlockSpec((1, 3, 2 * chans, width), lambda i: (layer, 0, 0, 0)),
            pl.BlockSpec((1, 2 * chans, width), lambda i: (layer, 0, 0)),
            pl.BlockSpec((1, 2 * chans, width), lambda i: (layer, 0, 0)),
        ],
        input_output_aliases={3: 0, 4: 1, 5: 2} if aliased else {},
        scratch_shapes=[
            pltpu.VMEM((2, count, width), BF16),
            pltpu.SemaphoreType.DMA((2 * sources[0].shape[0],)),
        ],
        compiler_params=PARAMS,
        cost_estimate=pl.CostEstimate(flops=1, bytes_accessed=1, transcendentals=0),
        name="final_mixer",
    )(place, *sources, *(into if aliased else ()))


def norm_forward(values, gain):
    average = jnp.mean(values, axis=0, keepdims=True)
    centered = values - average
    inv_std = lax.rsqrt(jnp.mean(centered * centered, axis=0, keepdims=True) + EPS)
    normal_rows = centered * inv_std
    return ((normal_rows * gain).astype(BF16), (normal_rows, inv_std, gain))


def norm_back(grads, stored):
    normal_rows, inv_std, gain = stored
    scaled = grads * gain
    total = jnp.mean(scaled, axis=0, keepdims=True)
    crossed = jnp.mean(scaled * normal_rows, axis=0, keepdims=True)
    gain_grad = jnp.sum(grads * normal_rows, axis=1)
    return (inv_std * (scaled - total - normal_rows * crossed), gain_grad)


def on_device(
    input_long,
    input_short,
    length_long,
    length_short,
    gain_mixer,
    weight_in,
    short_taps,
    cond_taps,
    static_filter,
    weight_out,
    gain_mlp,
    weight_up,
    weight_down,
    grad_long,
    grad_short,
):
    count_long, seq_long, chan_width = input_long.shape
    count_short, seq_short = (input_short.shape[0], input_short.shape[1])
    layers = weight_in.shape[0]
    ranks = lax.axis_size("chan")
    pairs = lax.axis_size("batch") // 2
    place = lax.axis_index("chan")
    core = lax.axis_index("batch") % 2
    pair = lax.axis_index("batch") // 2
    width = chan_width * ranks
    hidden = weight_down.shape[1] // 2
    chans = chan_width // 2
    half_long = seq_long // 2
    tokens = half_long + seq_short
    mate = ("batch", 1)
    first = core == 0
    pieces = 4
    piece = pair % pieces
    plane = {1: ("batch", 2), 2: ("batch", 4)}
    extra_steps = []
    mask = 2 * pieces
    while mask < 2 * pairs:
        extra_steps.append(("batch", mask))
        mask *= 2
    spot = jnp.stack([core, piece, place]).astype(jnp.int32)
    plane_orders = ((1, 2), (2, 1))

    def to_tokens(long_rows, short_rows, extra=None):
        turned = jnp.swapaxes(long_rows, 1, 2).astype(BF16)
        halves = jnp.stack([turned[..., :half_long], turned[..., half_long:]])
        kept = pick(halves, core)
        came = swap(pick(halves, 1 - core), mate)
        ordered = jnp.where(first, jnp.concatenate([kept, came]), jnp.concatenate([came, kept]))
        parts = [ordered, jnp.swapaxes(short_rows, 1, 2).astype(BF16)]
        if extra is not None:
            parts.append(jnp.broadcast_to(extra[None], (ranks,) + extra.shape))
        yield from exchange(jnp.concatenate(parts, axis=2), lambda v: v.reshape(width, -1))

    def exchange(blocks, then):
        came = {0: pick(blocks, place)}
        both = jnp.stack([pick(blocks, place ^ FAR), pick(blocks, place ^ NEAR ^ FAR)])
        first_came = swap(both, ("chan", FAR))
        first_came = after(first_came, *(yield [both]))
        came[FAR] = first_came[0]
        both = jnp.stack([pick(blocks, place ^ NEAR), first_came[1]])
        second_came = swap(both, ("chan", NEAR))
        second_came = after(second_came, *(yield [both]))
        came[NEAR], came[NEAR ^ FAR] = (second_came[0], second_came[1])
        result = then(by_xor(jnp.stack([came[r] for r in range(ranks)]), place))
        yield result

    def from_tokens(values):
        steps = exchange(values.reshape(ranks, chan_width, -1), lambda gathered: gathered)
        ties = yield next(steps)
        ties = yield steps.send(ties)
        gathered = steps.send(ties)
        halves = gathered[:, :, :half_long].reshape(2, count_long, chan_width, half_long)
        kept = pick(halves, core)
        sent = pick(halves, 1 - core)
        came = swap(sent, mate)
        came = after(came, *(yield [sent]))
        ordered = jnp.where(
            first, jnp.concatenate([kept, came], axis=2), jnp.concatenate([came, kept], axis=2)
        )
        short_part = jnp.swapaxes(gathered[:, :, half_long:tokens], 1, 2)
        yield (jnp.swapaxes(ordered, 1, 2), short_part, gathered[:, :, tokens:])

    def both_cores(values):
        return jnp.concatenate([values, swap(values, mate)], axis=1)

    def both_ordered(values):
        came = swap(values, mate)
        low, high = (jnp.where(first, values, came), jnp.where(first, came, values))
        return jnp.concatenate(
            [low[:, :half_long], high[:, :half_long], low[:, half_long:], high[:, half_long:]],
            axis=1,
        )

    def own_sum(sent, kept):
        return kept + swap(sent, mate).astype(F32)

    def mlp_rows(layer):
        up = lax.dynamic_slice_in_dim(weight_up[layer], core * hidden, hidden, 2)
        down = lax.dynamic_slice_in_dim(weight_down[layer], core * hidden, hidden, 0)
        return jnp.concatenate([up.reshape(width, 2 * hidden), down])

    def mixer_rows(layer):
        into = jnp.transpose(weight_in[layer], (1, 2, 0))
        into = lax.dynamic_slice_in_dim(into, core * chans, chans, 1)
        out = lax.dynamic_slice_in_dim(weight_out[layer], core * chans, chans, 0)
        taps = jnp.concatenate([short_taps[layer].reshape(9, chan_width), cond_taps[layer]]).T
        coarse = lax.reduce_precision(taps, 8, 7)
        static = jnp.concatenate([static_filter[layer].T, coarse, taps - coarse], axis=1)
        static = jnp.pad(static.astype(BF16), ((0, 0), (0, width - static.shape[1])))
        static = lax.dynamic_slice_in_dim(static, core * chans, chans, 0)
        spare = jnp.zeros((mixer_count - 5 * chans, width), BF16)
        return jnp.concatenate([into.reshape(3 * chans, width), out, static, spare])

    mixer_count = -(-5 * chans // (32 * pieces)) * 32 * pieces
    mlp_count = width + hidden
    own_rows = [
        {"mixer": mixer_rows(layer), "mlp": mlp_rows(layer)} for layer in range(layers)
    ]

    def half_rows(kind):
        return (mixer_count if kind == "mixer" else mlp_count) // (2 * pieces)

    def own_block(layer, kind, half):
        count = half_rows(kind)
        return lax.dynamic_slice_in_dim(
            own_rows[layer][kind], (piece * 2 + half) * count, count, 0
        )

    others = (FAR, NEAR, FAR ^ NEAR)

    def gather(layer, kind):
        block = jnp.concatenate([own_block(layer, kind, half) for half in range(2)])[None]
        count = half_rows(kind)
        far = swap(block, ("chan", FAR))
        far = after(far, *(yield [block]))
        both = jnp.concatenate([block, far])
        near = swap(both, ("chan", NEAR))
        near = after(near, *(yield [both]))
        foreign = jnp.concatenate([far, near])
        held = [foreign[:, half * count : (half + 1) * count] for half in range(2)]
        came = [swap(held[half], plane[plane_orders[half][0]]) for half in range(2)]
        ties = yield held
        held = [jnp.concatenate([held[half], after(came[half], *ties)]) for half in range(2)]
        buffers, plan = ([], [])
        for half, (one, two) in enumerate(plane_orders):
            blocks = [(0, other) for other in others] + [(one, other) for other in others]
            buffers += [held[half], swap(held[half], plane[two])]
            plan.append((half, tuple(blocks), 0, count))
            plan.append((half, tuple((offset ^ two, other) for offset, other in blocks), 0, count))
        weights[layer, kind] = (own_rows[layer][kind], tuple(buffers), tuple(plan), ranks)
        yield held

    line = []

    def go(steps, *ties):
        line[:] = steps.send((*line, *ties))

    def begin(steps):
        line.extend(next(steps))
        return steps

    def finish(steps):
        return steps.send(tuple(line))

    weights = {}
    gains = jnp.stack([gain_mixer, gain_mlp], axis=1).reshape(2 * layers, chan_width)
    gains_coarse = lax.reduce_precision(gains, 8, 7)
    gains = jnp.concatenate([gains_coarse, gains - gains_coarse]).astype(BF16).T
    gains = jnp.pad(gains, ((0, 0), (0, 128 - gains.shape[1])))
    mixer_0 = begin(gather(0, "mixer"))
    input_steps = begin(to_tokens(input_long, input_short, gains))
    mlp_0 = begin(gather(0, "mlp"))
    go(mixer_0)
    go(input_steps)
    go(mixer_0)
    go(mlp_0)
    arrived = finish(input_steps)
    gains = arrived[:, tokens : tokens + 4 * layers].astype(F32)
    gains = gains[:, : 2 * layers] + gains[:, 2 * layers :]
    gains = gains.T.reshape(layers, 2, width, 1)

    own_lengths = jnp.concatenate([length_long, length_short])
    other_lengths = swap(own_lengths, mate)
    low, high = (
        jnp.where(first, own_lengths, other_lengths),
        jnp.where(first, other_lengths, own_lengths),
    )
    spans = [pick(jnp.concatenate([low[:count_long], high[:count_long]]), place)]
    spans += [pick(side[count_long:], place) for side in (low, high)]
    live = jnp.concatenate(
        [
            jnp.arange(length) < span
            for length, span in zip((seq_long, seq_short, seq_short), spans)
        ]
    )
    live = jnp.broadcast_to(live.astype(F32)[None], (8, live.shape[0]))
    tables = (table(seq_long), table(seq_short))
    sizes = (seq_long, seq_short, chans, 2)

    residual_start = arrived[:, :tokens].astype(F32)
    residual = residual_start
    stored_all = []
    for layer in range(layers):
        normed, norm_stored = norm_forward(residual, gains[layer, 0])
        normed = both_ordered(normed)
        if layer == 0:
            mixer_1 = begin(gather(1, "mixer"))
            go(mixer_0)
            go(mlp_0)
        else:
            go(mlp_1)
        proj, long_out, kept, sent = mixer_forward(
            spot, weights[layer, "mixer"], after(normed, *line), live, tables, sizes
        )
        if layer == 0:
            go(mixer_1, kept)
        else:
            grad_steps = begin(to_tokens(grad_long, grad_short))
        sent = after(sent, *line)
        middle = residual + own_sum(sent, kept)
        normed_mlp, mlp_stored = norm_forward(middle, gains[layer, 1])
        normed_mlp = both_cores(normed_mlp)
        if layer == 0:
            go(mlp_0)
            mlp_1 = begin(gather(1, "mlp"))
            go(mixer_1)
            go(mlp_1)
            go(mixer_1)
            go(mlp_1)
        else:
            go(grad_steps)
        gate_up, kept, sent = mlp_forward(
            spot, weights[layer, "mlp"], after(normed_mlp, *line)
        )
        residual = middle + own_sum(sent, kept)
        stored_all.append((normed, norm_stored, proj, long_out, normed_mlp, mlp_stored, gate_up))
    upstream = finish(grad_steps).astype(F32)

    output_steps = from_tokens((residual - residual_start).astype(BF16))

    chan_order = (0, FAR, NEAR, NEAR ^ FAR)

    def routes(near_first, count):
        found = []
        for half, (one, two) in enumerate(plane_orders):
            for a in range(2):
                for c in range(2):
                    if near_first:
                        targets = {r: (i // 2, 4 * a + 2 * c + i % 2) for i, r in enumerate(chan_order)}
                    else:
                        targets = {r: (2 * half + a, ranks * c + i) for i, r in enumerate(chan_order)}
                    found.append((targets, half, a * one + c * two, near_first * half * count))
        return tuple(found)

    def added(values):
        return sum(value.astype(F32) for value in values).astype(BF16)

    def spread_sums(block, early):
        for step in extra_steps:
            block = added([block, swap(block, step)])
        parts = [(block, plane_orders[early])] if early is not None else []
        if early is None:
            middle = block.shape[1] // 2
            parts = [(block[:, :middle], plane_orders[0]), (block[:, middle:], plane_orders[1])]
        came = [swap(part, plane[one]) for part, (one, _) in parts]
        ties = yield [part for part, _ in parts]
        both = [jnp.concatenate([part, after(c, *ties)]) for (part, _), c in zip(parts, came)]
        came = [swap(part, plane[two]) for part, (_, (_, two)) in zip(both, parts)]
        ties = yield both
        pieces_of = []
        for part, c, (_, (one, two)) in zip(both, came, parts):
            c = after(c, *ties)
            by = {0: part[:1], one: part[1:], two: c[:1], one ^ two: c[1:]}
            pieces_of.append(jnp.concatenate([by[offset] for offset in range(pieces)]))
        mine = jnp.concatenate(pieces_of, axis=1)
        came = swap(mine, mate)
        ties = yield [mine]
        yield (mine, after(came, *ties))

    def scatter(blocks, early):
        near_first = len(blocks) == 2
        if near_first:
            came = swap(blocks[1], ("chan", NEAR))
            ties = yield [blocks[1]]
            block = added([blocks[0], after(came, *ties)])
            count = block.shape[1] // 2
            parts = [block[:, half * count : (half + 1) * count] for half in range(2)]
            kept = [part[:4] for part in parts]
            sent = [part[4:] for part in parts]
        else:
            kept, sent = (blocks[0::2], blocks[1::2])
        came = [swap(part, plane[one]) for part, (one, _) in zip(sent, plane_orders)]
        ties = yield list(sent)
        came = [after(value, *ties) for value in came]
        middle = kept[0].shape[0] // 2
        sent = [added([k[middle:], c[middle:]]) for k, c in zip(kept, came)]
        kept = [added([k[:middle], c[:middle]]) for k, c in zip(kept, came)]
        came = [swap(part, plane[two]) for part, (_, two) in zip(sent, plane_orders)]
        ties = yield sent
        came = [after(value, *ties) for value in came]
        block = jnp.concatenate([added([k, c]) for k, c in zip(kept, came)], axis=1)
        for mask in (FAR,) if near_first else (NEAR, FAR):
            kept, sent = (block[: block.shape[0] // 2], block[block.shape[0] // 2 :])
            came = swap(sent, ("chan", mask))
            ties = yield [sent]
            block = added([kept, after(came, *ties)])
        yield from spread_sums(block, early)

    upstream_start = upstream
    gain_grads = {}
    scatters = []
    mlp_half, mixer_half = (half_rows("mlp"), half_rows("mixer"))

    line[:] = []
    for layer in reversed(range(layers)):
        normed, norm_stored, proj, long_out, normed_mlp, mlp_stored, gate_up = stored_all[layer]
        last = layer == 0
        coming = both_cores(upstream.astype(BF16))
        kept, sent, blocks = mlp_back(
            spot, weights[layer, "mlp"], normed_mlp, gate_up, coming,
            routes(False, mlp_half), 2 * ranks, mlp_half,
        )
        if last:
            go(scatters[0], kept)
            go(scatters[1], kept)
        scatters.append(begin(scatter(blocks, None if last else 0)))
        sent = after(sent, *line)
        change, gain_grads[layer, 1] = norm_back(own_sum(sent, kept), mlp_stored)
        upstream = upstream + change
        coming = both_ordered(upstream.astype(BF16))
        if last:
            go(scatters[0])
            go(scatters[1])
        else:
            begin(output_steps)
        kept, sent, blocks = mixer_back(
            spot, weights[layer, "mixer"], normed, after(coming, *line), proj, long_out, live,
            tables, sizes, routes(True, mixer_half), 2 * ranks, 2 * mixer_half,
        )
        if last:
            go(scatters[2], kept)
        else:
            go(scatters[0], kept)
        scatters.append(begin(scatter(blocks, None if last else 1)))
        sent = after(sent, *line)
        change, gain_grads[layer, 0] = norm_back(own_sum(sent, kept), norm_stored)
        upstream = upstream + change
        if not last:
            go(output_steps)

    mlp_early, mixer_early, mlp_late, mixer_late = scatters

    gain_parts = jnp.stack(
        [gain_grads[layer, which] for layer in range(layers) for which in range(2)], axis=1
    )
    gain_coarse = lax.reduce_precision(gain_parts, 8, 7)
    gain_lanes = jnp.concatenate([gain_coarse, gain_parts - gain_coarse], axis=1).astype(BF16)
    gain_lanes = jnp.pad(gain_lanes, ((0, 0), (0, 128 - gain_lanes.shape[1])))
    go(mlp_early)
    go(mixer_early)
    go(output_steps)
    go(mlp_late)
    go(mlp_early)
    go(mixer_late)
    go(mixer_early)
    go(mlp_late)
    changed = jnp.concatenate([(upstream - upstream_start).astype(BF16), gain_lanes], axis=1)
    back_steps = begin(from_tokens(after(changed, *line)))
    go(mixer_late)
    go(mlp_early)
    go(mixer_early)
    go(mlp_late)
    go(mixer_late)
    mlp_out = final_mlp(spot, finish(mlp_early), mlp_count, 1, layers, None)
    line.append(mlp_out[1])
    go(mixer_early)
    go(back_steps)
    go(mlp_late)
    go(mixer_late)
    mixer_out = final_mixer(spot, finish(mixer_early), mixer_count, chans, 1, layers, None)
    line.append(mixer_out[1])
    go(back_steps)
    go(mlp_late)
    go(mixer_late)
    go(mixer_late)

    gone_long, gone_short, _ = finish(output_steps)
    output_long = input_long + gone_long.astype(F32)
    output_short = input_short + gone_short.astype(F32)
    gone_long, gone_short, gain_sums = finish(back_steps)
    back_long = grad_long + gone_long.astype(F32)
    back_short = grad_short + gone_short.astype(F32)
    gain_sums = jnp.sum(gain_sums[:, :, : 4 * layers].astype(F32), axis=0)
    gain_sums = (gain_sums[:, : 2 * layers] + gain_sums[:, 2 * layers :]).T
    for step in [mate] + list(plane.values()) + extra_steps:
        gain_sums = gain_sums + swap(gain_sums, step)

    mlp_out = final_mlp(spot, finish(mlp_late), mlp_count, 0, layers, mlp_out)
    mixer_out = final_mixer(spot, finish(mixer_late), mixer_count, chans, 0, layers, mixer_out)
    into_out, out_out, filter_out = mixer_out
    taps = jnp.swapaxes(filter_out[:, :, seq_long : seq_long + 12], 1, 2)

    return (
        output_long,
        output_short,
        back_long,
        back_short,
        gain_sums[0::2],
        jnp.transpose(into_out, (0, 3, 1, 2)),
        taps[:, :9].reshape(layers, 3, 3, chan_width),
        taps[:, 9:],
        jnp.swapaxes(filter_out[:, :, :seq_long], 1, 2),
        out_out,
        gain_sums[1::2],
        mlp_out[0],
        mlp_out[1],
    )


def solution(mesh):
    tokens = P("batch", None, "chan")
    placed = (
        tokens,
        tokens,
        P("batch"),
        P("batch"),
        P(None, "chan"),
        P(None, None, None, "chan"),
        P(None, None, None, "chan"),
        P(None, None, "chan"),
        P(None, None, "chan"),
        P(None, "chan", None),
        P(None, "chan"),
        P(None, None, None, "chan"),
        P(None, "chan", None),
        tokens,
        tokens,
    )
    return jax.shard_map(
        on_device,
        mesh=mesh,
        in_specs=placed,
        out_specs=(tokens,) * 4 + placed[4:13],
        check_vma=False,
    )
```

```python
import functools
import math

import jax
import jax.numpy as jnp
import numpy as np
from jax import lax
from jax.experimental import pallas as pl
from jax.experimental.pallas import tpu as pltpu
from jax.sharding import PartitionSpec as P

EPS = 1e-05
BF16 = jnp.bfloat16
F32 = jnp.float32
VMEM_BYTES = 52 * 2**20
FAR, NEAR = (3, 1)


def nn(left, right):
    return lax.dot_general(left, right, (((1,), (0,)), ((), ())), preferred_element_type=F32)


def nt(left, right):
    return lax.dot_general(left, right, (((1,), (1,)), ((), ())), preferred_element_type=F32)


def tn(left, right):
    return lax.dot_general(left, right, (((0,), (0,)), ((), ())), preferred_element_type=F32)


def table(length):
    places = np.arange(length)[:, None]
    phase = (places * np.arange(length + 1)[None, :] % (2 * length)) * (np.pi / length)
    packed = np.concatenate(
        [np.cos(phase[:, :length]), np.cos(phase[:, length:]), -np.sin(phase[:, 1:length])], axis=1
    )
    return jnp.asarray(packed.astype(np.float32)).astype(BF16)


def swap(values, step):
    axis, mask = step
    return lax.ppermute(values, axis, [(i, i ^ mask) for i in range(lax.axis_size(axis))])


def after(values, *others):
    return lax.optimization_barrier((values,) + others)[0]


def pick(values, index):
    return lax.dynamic_index_in_dim(values, index, 0, keepdims=False)


def by_xor(values, index):
    return jnp.stack([pick(values, place ^ index) for place in range(values.shape[0])])


def block_copies(plan, place_ref, own_ref, buffers, flat_ref, sems, wanted):
    if wanted == 0:
        return [pltpu.make_async_copy(own_ref, flat_ref.at[0], sems.at[0, 0])]
    copies = []
    for buffer, (half, blocks, start, count) in zip(buffers, plan):
        for at, (offset, other) in enumerate(blocks):
            if other == wanted:
                row = pl.multiple_of(((place_ref[1] ^ offset) * 2 + half) * count, 16)
                copies.append(
                    pltpu.make_async_copy(
                        buffer.at[at, pl.ds(start, count)],
                        flat_ref.at[wanted, pl.ds(row, count)],
                        sems.at[wanted, len(copies)],
                    )
                )
    return copies


def fill(plan, place_ref, own_ref, buffers, flat_ref, sems, per_step):
    step = pl.program_id(0)
    ranks = flat_ref.shape[0]
    args = (plan, place_ref, own_ref, buffers, flat_ref, sems)

    @pl.when(step == 0)
    def begin():
        for wanted in range(ranks):
            for copy in block_copies(*args, wanted):
                copy.start()

    for wanted in range(ranks):

        @pl.when(step == wanted // per_step)
        def arrive():
            for copy in block_copies(*args, wanted):
                copy.wait()


def spill_copies(routes, count, place_ref, rows_ref, outs, sems, slot, wanted):
    copies = []
    for targets, half, offset, start in routes:
        out, at = targets[wanted]
        row = pl.multiple_of(((place_ref[1] ^ offset) * 2 + half) * count, 16)
        copies.append(
            pltpu.make_async_copy(
                rows_ref.at[slot, pl.ds(row, count)],
                outs[out].at[at, pl.ds(start, count)],
                sems.at[slot, len(copies)],
            )
        )
    return copies


def grouped(refs, *counts):
    groups, at = ([], 0)
    for count in counts:
        groups.append(refs[at : at + count])
        at += count
    return groups


def whole(shape):
    return pl.BlockSpec(shape, lambda i: (0,) * len(shape))


SMEM = pl.BlockSpec(memory_space=pltpu.SMEM)
ANY = pl.BlockSpec(memory_space=pl.ANY)
PARAMS = pltpu.CompilerParams(vmem_limit_bytes=VMEM_BYTES)


def gelu_parts(gate):
    slope = math.sqrt(2.0 / math.pi)
    square = gate * gate
    bent = jnp.tanh(slope * (gate + 0.044715 * square * gate))
    gelu = 0.5 * gate * (1.0 + bent)
    grad = 0.5 * (1.0 + bent) + 0.5 * gate * (1.0 - bent * bent) * slope * (
        1.0 + 0.134145 * square
    )
    return (gelu, grad)


def add_total(total, part):
    step = pl.program_id(0)

    @pl.when(step == 0)
    def start():
        total[...] = part

    @pl.when(step > 0)
    def add():
        total[...] += part


def split_total(total, kept_ref, sent_ref):
    @pl.when(pl.program_id(0) == pl.num_programs(0) - 1)
    def finish():
        own = kept_ref.shape[1]
        kept_ref[...] = total[:, :own]
        sent_ref[...] = total[:, own:].astype(BF16)


def mlp_forward_kernel(plan, *refs):
    (place_ref, normed_ref, own_ref), buffers, outs, scratch = grouped(refs, 3, len(plan), 3, 3)
    gate_up_ref, kept_ref, sent_ref = outs
    flat_ref, total, sems = scratch
    fill(plan, place_ref, own_ref, buffers, flat_ref, sems, 1)
    step = pl.program_id(0)
    width = normed_ref.shape[0]
    hidden = flat_ref.shape[1] - width
    gate_up = tn(flat_ref[step, :width], normed_ref[...])
    gate_up_ref[0] = gate_up.astype(BF16)
    activated = (gelu_parts(gate_up[:hidden])[0] * gate_up[hidden:]).astype(BF16)
    add_total(total, tn(flat_ref[step, width:], activated))
    split_total(total, kept_ref, sent_ref)


def mlp_forward(place, rows, normed):
    own, buffers, plan, ranks = rows
    count, width = own.shape
    tokens = normed.shape[1]
    hidden = count - width
    half = tokens // 2
    return pl.pallas_call(
        functools.partial(mlp_forward_kernel, plan),
        grid=(ranks,),
        out_shape=[
            jax.ShapeDtypeStruct((ranks, 2 * hidden, tokens), BF16),
            jax.ShapeDtypeStruct((width, half), F32),
            jax.ShapeDtypeStruct((width, half), BF16),
        ],
        in_specs=[SMEM, whole((width, tokens)), ANY] + [ANY] * len(buffers),
        out_specs=[
            pl.BlockSpec((1, 2 * hidden, tokens), lambda r: (r, 0, 0)),
            whole((width, half)),
            whole((width, half)),
        ],
        scratch_shapes=[
            pltpu.VMEM((ranks, count, width), BF16),
            pltpu.VMEM((width, tokens), F32),
            pltpu.SemaphoreType.DMA((ranks, 8)),
        ],
        compiler_params=PARAMS,
        cost_estimate=pl.CostEstimate(flops=1, bytes_accessed=1, transcendentals=0),
        name="mlp_forward",
    )(place, normed, own, *buffers)


def spill(routes, count, place_ref, grads_ref, outs, sems, per_step):
    step = pl.program_id(0)
    ranks = per_step * pl.num_programs(0)
    for wanted in range(ranks):
        at = wanted // per_step
        slot = (at % 2) * per_step + wanted % per_step

        @pl.when(step == at)
        def leave():
            for copy in spill_copies(
                routes, count, place_ref, grads_ref, outs, sems, slot, wanted
            ):
                copy.start()


def spill_wait(routes, count, place_ref, grads_ref, outs, sems, per_step, last):
    step = pl.program_id(0)
    steps = 4 // per_step
    for wanted in range(4):
        at = wanted // per_step
        slot = (at % 2) * per_step + wanted % per_step
        due = steps - 1 if last else at + 2
        if last and at + 2 < steps:
            continue
        if not last and at + 2 >= steps:
            continue

        @pl.when(step == due)
        def gone():
            for copy in spill_copies(
                routes, count, place_ref, grads_ref, outs, sems, slot, wanted
            ):
                copy.wait()


def mlp_back_kernel(plan, routes, count, *refs):
    (place_ref, normed_ref, coming_ref, gate_up_ref, own_ref), buffers, outs, scratch = grouped(
        refs, 5, len(plan), 6, 5
    )
    kept_ref, sent_ref = outs[:2]
    flat_ref, grads_ref, total, sems, out_sems = scratch
    fill(plan, place_ref, own_ref, buffers, flat_ref, sems, 1)
    step = pl.program_id(0)
    width = normed_ref.shape[0]
    hidden = flat_ref.shape[1] - width
    spilled = (routes, count, place_ref, grads_ref, outs[2:], out_sems, 1)
    spill_wait(*spilled, False)
    slot = step % 2
    gate = gate_up_ref[0, :hidden].astype(F32)
    up = gate_up_ref[0, hidden:].astype(F32)
    grad_act = nn(flat_ref[step, width:], coming_ref[...])
    gelu, slope = gelu_parts(gate)
    activated = (gelu * up).astype(BF16)
    grad_gate = (grad_act * up * slope).astype(BF16)
    grad_up = (grad_act * gelu).astype(BF16)
    grads_ref[slot, width:] = nt(activated, coming_ref[...]).astype(BF16)
    grads_ref[slot, :width, :hidden] = nt(normed_ref[...], grad_gate).astype(BF16)
    grads_ref[slot, :width, hidden:] = nt(normed_ref[...], grad_up).astype(BF16)
    spill(*spilled)
    add_total(
        total,
        nn(flat_ref[step, :width, :hidden], grad_gate)
        + nn(flat_ref[step, :width, hidden:], grad_up),
    )
    split_total(total, kept_ref, sent_ref)
    spill_wait(*spilled, True)


def mlp_back(place, rows, normed, gate_up, coming, routes, blocks, block_rows):
    own, buffers, plan, ranks = rows
    count, width = own.shape
    tokens = normed.shape[1]
    hidden = count - width
    half = tokens // 2
    results = pl.pallas_call(
        functools.partial(mlp_back_kernel, plan, routes, plan[0][3]),
        grid=(ranks,),
        out_shape=[
            jax.ShapeDtypeStruct((width, half), F32),
            jax.ShapeDtypeStruct((width, half), BF16),
        ]
        + [jax.ShapeDtypeStruct((blocks, block_rows, width), BF16)] * 4,
        in_specs=[
            SMEM,
            whole((width, tokens)),
            whole((width, tokens)),
            pl.BlockSpec((1, 2 * hidden, tokens), lambda r: (r, 0, 0)),
            ANY,
        ]
        + [ANY] * len(buffers),
        out_specs=[whole((width, half)), whole((width, half))] + [ANY] * 4,
        scratch_shapes=[
            pltpu.VMEM((ranks, count, width), BF16),
            pltpu.VMEM((2, count, width), BF16),
            pltpu.VMEM((width, tokens), F32),
            pltpu.SemaphoreType.DMA((ranks, 8)),
            pltpu.SemaphoreType.DMA((2, 8)),
        ],
        compiler_params=PARAMS,
        cost_estimate=pl.CostEstimate(
            flops=12 * ranks * hidden * width * tokens,
            bytes_accessed=4 * ranks * own.size + 4 * ranks * hidden * tokens,
            transcendentals=ranks * hidden * tokens,
        ),
        name="mlp_back",
    )(place, normed, coming, gate_up, own, *buffers)
    return (results[0], results[1], results[2:])


def mlp_turn_kernel(plan, routes, count, *refs):
    (place_ref, normed_ref, coming_ref, own_ref), buffers, outs, scratch = grouped(
        refs, 4, len(plan), 8, 6
    )
    flat_ref, grads_ref, total, back_total, sems, out_sems = scratch
    fill(plan, place_ref, own_ref, buffers, flat_ref, sems, 1)
    step = pl.program_id(0)
    width = normed_ref.shape[0]
    hidden = flat_ref.shape[1] - width
    spilled = (routes, count, place_ref, grads_ref, outs[4:], out_sems, 1)
    spill_wait(*spilled, False)
    slot = step % 2
    gate_up = tn(flat_ref[step, :width], normed_ref[...])
    gate, up = (gate_up[:hidden], gate_up[hidden:])
    grad_act = nn(flat_ref[step, width:], coming_ref[...])
    gelu, slope = gelu_parts(gate)
    activated = (gelu * up).astype(BF16)
    grad_gate = (grad_act * up * slope).astype(BF16)
    grad_up = (grad_act * gelu).astype(BF16)
    add_total(total, tn(flat_ref[step, width:], activated))
    grads_ref[slot, width:] = nt(activated, coming_ref[...]).astype(BF16)
    grads_ref[slot, :width, :hidden] = nt(normed_ref[...], grad_gate).astype(BF16)
    grads_ref[slot, :width, hidden:] = nt(normed_ref[...], grad_up).astype(BF16)
    spill(*spilled)
    add_total(
        back_total,
        nn(flat_ref[step, :width, :hidden], grad_gate)
        + nn(flat_ref[step, :width, hidden:], grad_up),
    )
    split_total(total, outs[0], outs[1])
    split_total(back_total, outs[2], outs[3])
    spill_wait(*spilled, True)


def mlp_turn(place, rows, normed, coming, routes, blocks, block_rows):
    own, buffers, plan, ranks = rows
    count, width = own.shape
    tokens = normed.shape[1]
    hidden = count - width
    half = tokens // 2
    results = pl.pallas_call(
        functools.partial(mlp_turn_kernel, plan, routes, plan[0][3]),
        grid=(ranks,),
        out_shape=[
            jax.ShapeDtypeStruct((width, half), F32),
            jax.ShapeDtypeStruct((width, half), BF16),
        ]
        * 2
        + [jax.ShapeDtypeStruct((blocks, block_rows, width), BF16)] * 4,
        in_specs=[SMEM, whole((width, tokens)), whole((width, tokens)), ANY]
        + [ANY] * len(buffers),
        out_specs=[whole((width, half))] * 4 + [ANY] * 4,
        scratch_shapes=[
            pltpu.VMEM((ranks, count, width), BF16),
            pltpu.VMEM((2, count, width), BF16),
            pltpu.VMEM((width, tokens), F32),
            pltpu.VMEM((width, tokens), F32),
            pltpu.SemaphoreType.DMA((ranks, 8)),
            pltpu.SemaphoreType.DMA((2, 8)),
        ],
        compiler_params=PARAMS,
        cost_estimate=pl.CostEstimate(flops=1, bytes_accessed=1, transcendentals=0),
        name="mlp_turn",
    )(place, normed, coming, own, *buffers)
    return (results[:4], results[4:])


def delayed(layout, values, by):
    return jnp.where(layout["inside"] >= by, pltpu.roll(values, by, 1), 0.0)


def advanced(layout, values, by):
    moved = pltpu.roll(values, layout["tokens"] - by, 1)
    return jnp.where(layout["inside"] < layout["length"] - by, moved, 0.0)


def layout_of(long, short, tokens):
    lane = lax.broadcasted_iota(jnp.int32, (1, tokens), 1)
    return {
        "long": long,
        "short": short,
        "tokens": tokens,
        "inside": jnp.where(lane < long, lane, (lane - long) % short),
        "length": jnp.where(lane < long, long, short),
    }


def taps_forward(layout, values, taps):
    return (
        taps[0] * values
        + taps[1] * delayed(layout, values, 1)
        + taps[2] * delayed(layout, values, 2)
    )


def taps_back(layout, values, taps):
    return (
        taps[0] * values
        + taps[1] * advanced(layout, values, 1)
        + taps[2] * advanced(layout, values, 2)
    )


def taps_grad(layout, grads, values):
    moved = [values, delayed(layout, values, 1), delayed(layout, values, 2)]
    return [jnp.sum(grads * value, axis=1, keepdims=True) for value in moved]


def sequences(layout, values):
    long, short = (layout["long"], layout["short"])
    shorts = [values[:, at : at + short] for at in range(long, layout["tokens"], short)]
    return (values[:, :long], jnp.concatenate(shorts, axis=0))


def rejoined(long_part, short_part):
    rows = long_part.shape[0]
    shorts = [short_part[at * rows : (at + 1) * rows] for at in range(short_part.shape[0] // rows)]
    return jnp.concatenate([long_part] + shorts, axis=1)


def repeated(values, times):
    return jnp.concatenate([values] * times, axis=0) if times > 1 else values


def at_edge(edge, edge_values, others):
    head = jnp.where(edge[:, :128], edge_values, others[:, :128])
    return jnp.concatenate([head, others[:, 128:]], axis=1) if others.shape[1] > 128 else head


def turned_back(real_part, imag_part, cosines):
    return nt(jnp.concatenate([real_part.astype(BF16), imag_part.astype(BF16)], axis=1), cosines)


def filter_of(gated, shaped, static_rows, cosines):
    rows, length = gated.shape
    times = rows // static_rows.shape[0]
    edge = lax.broadcasted_iota(jnp.int32, (1, length), 1) == 0
    spectra = nn(jnp.concatenate([gated, shaped], axis=0).astype(BF16), cosines)
    shaped_re, shaped_im = (spectra[rows:, :length], spectra[rows:, length:])
    fixed = nn(static_rows, cosines)
    fixed_re = repeated(fixed[:, :length], times)
    fixed_im = repeated(fixed[:, length:], times)
    square = shaped_im * shaped_im
    power = shaped_re * shaped_re + jnp.where(edge, 0.0, square) + length
    inv_root = lax.rsqrt(power)
    power_last = square[:, :128] + length
    inv_root_last = lax.rsqrt(power_last)
    scale = 1.0 / math.sqrt(length)
    return {
        "length": length,
        "times": times,
        "edge": edge,
        "weight": jnp.where(edge, 0.5 / length, 1.0 / length),
        "signal_re": spectra[:rows, :length],
        "signal_im": spectra[:rows, length:],
        "shaped_re": shaped_re,
        "shaped_im": shaped_im,
        "fixed_im": fixed_im,
        "fixed_sine": jnp.where(edge, 0.0, fixed_im),
        "slope": scale * inv_root,
        "slope_last": scale * inv_root_last,
        "filter_re": fixed_re + (power * inv_root * scale - 1.0),
        "filter_last": fixed_im[:, :128] + (power_last * inv_root_last * scale - 1.0),
    }


def filtered(parts, cosines):
    signal_re, signal_im = (parts["signal_re"], parts["signal_im"])
    product_re = parts["filter_re"] * signal_re - parts["fixed_sine"] * signal_im
    product_im = at_edge(
        parts["edge"],
        parts["filter_last"] * signal_im[:, :128],
        parts["filter_re"] * signal_im + parts["fixed_im"] * signal_re,
    )
    return turned_back(product_re * parts["weight"], product_im * parts["weight"], cosines)


def filter_back(parts, grad_out, cosines):
    length, times, edge = (parts["length"], parts["times"], parts["edge"])
    signal_re, signal_im = (parts["signal_re"], parts["signal_im"])
    filter_re, fixed_im = (parts["filter_re"], parts["fixed_im"])
    turned = nn(grad_out.astype(BF16), cosines)
    product_re = turned[:, :length] * parts["weight"]
    product_im = turned[:, length:] * parts["weight"]
    grad_signal_re = filter_re * product_re + parts["fixed_sine"] * product_im
    grad_signal_im = at_edge(
        edge,
        parts["filter_last"] * product_im[:, :128],
        filter_re * product_im - fixed_im * product_re,
    )
    crossed = signal_im * product_im
    grad_filter = signal_re * product_re + jnp.where(edge, 0.0, crossed)
    grad_fixed_im = at_edge(
        edge, crossed[:, :128], signal_re * product_im - signal_im * product_re
    )
    slope = grad_filter * parts["slope"]
    grad_shaped_re = slope * parts["shaped_re"]
    grad_shaped_im = (
        at_edge(edge, crossed[:, :128] * parts["slope_last"], slope) * parts["shaped_im"]
    )
    count = grad_out.shape[0]
    rows = count // times
    grad_static = turned_back(
        sum(grad_filter[i * rows : (i + 1) * rows] for i in range(times)),
        sum(grad_fixed_im[i * rows : (i + 1) * rows] for i in range(times)),
        cosines,
    )
    back = turned_back(
        jnp.concatenate([grad_signal_re, grad_shaped_re], axis=0),
        jnp.concatenate([grad_signal_im, grad_shaped_im], axis=0),
        cosines,
    )
    return (back[:count], back[count:], grad_static)


def mixer_rows_of(flat_ref, step, per_step, chans):
    def rows(index):
        return [
            flat_ref[step * per_step + i, index * chans : (index + 1) * chans]
            for i in range(per_step)
        ]

    into = jnp.concatenate(rows(0) + rows(1) + rows(2), axis=0)
    filters = jnp.concatenate(rows(4), axis=0)
    return (into, jnp.concatenate(rows(3), axis=0), filters)


def mixer_taps(filters, start):
    lanes = filters[:, start : start + 128].astype(F32)
    taps = [lanes[:, k : k + 1] + lanes[:, 12 + k : 13 + k] for k in range(12)]
    return ([[taps[3 * k + group] for k in range(3)] for group in range(3)], taps[9:])


def own_lanes(ref, which, layout):
    half_long, short = (layout["long"] // 2, layout["short"])
    at = pl.multiple_of(which * half_long, 128)
    after = pl.multiple_of(layout["long"] + which * short, 128)
    return jnp.concatenate([ref[:, pl.ds(at, half_long)], ref[:, pl.ds(after, short)]], axis=1)


def mixer_forward_kernel(plan, sizes, *refs):
    inputs, buffers, outs, scratch = grouped(refs, 6, len(plan), 4, 4)
    place_ref, live_ref, long_ref, short_ref, normed_ref, own_ref = inputs
    proj_ref, long_out_ref, kept_ref, sent_ref = outs
    flat_ref, mixed_ref, total, sems = scratch
    long, short, chans, per_step = sizes
    fill(plan, place_ref, own_ref, buffers, flat_ref, sems, per_step)
    step = pl.program_id(0)
    layout = layout_of(long, short, normed_ref.shape[1])
    into, out_rows, filters = mixer_rows_of(flat_ref, step, per_step, chans)
    short_taps, cond_taps = mixer_taps(filters, long)
    rows = per_step * chans
    proj = nn(into, normed_ref[...])
    proj_ref[0] = proj.astype(BF16)
    query, key_part, value_part = (
        taps_forward(layout, proj[g * rows : (g + 1) * rows], short_taps[g]) for g in range(3)
    )
    gated = key_part * value_part * live_ref[:1]
    shaped = taps_forward(layout, gated, cond_taps)
    gated_parts, shaped_parts = (sequences(layout, gated), sequences(layout, shaped))
    results = [
        filtered(
            filter_of(gated_parts[i], shaped_parts[i], filters[:, :length], ref[...]), ref[...]
        )
        for i, (length, ref) in enumerate(((long, long_ref), (short, short_ref)))
    ]
    long_out = rejoined(*results)
    long_out_ref[0] = long_out.astype(BF16)
    mixed_ref[...] = (query * long_out).astype(BF16)
    core = place_ref[0]
    half = kept_ref.shape[1]
    part_kept = tn(out_rows, own_lanes(mixed_ref, core, layout))
    part_sent = tn(out_rows, own_lanes(mixed_ref, 1 - core, layout))
    add_total(total, jnp.concatenate([part_kept, part_sent], axis=1))
    split_total(total, kept_ref, sent_ref)


def mixer_forward(place, rows, normed, live, tables, sizes):
    own, buffers, plan, ranks = rows
    count, width = own.shape
    tokens = normed.shape[1]
    half = tokens // 2
    chans, per_step = sizes[2:]
    steps = ranks // per_step
    group = per_step * chans
    return pl.pallas_call(
        functools.partial(mixer_forward_kernel, plan, sizes),
        grid=(steps,),
        out_shape=[
            jax.ShapeDtypeStruct((steps, 3 * group, tokens), BF16),
            jax.ShapeDtypeStruct((steps, group, tokens), BF16),
            jax.ShapeDtypeStruct((width, half), F32),
            jax.ShapeDtypeStruct((width, half), BF16),
        ],
        in_specs=[SMEM, whole(live.shape)]
        + [whole(t.shape) for t in tables]
        + [whole((width, tokens)), ANY]
        + [ANY] * len(buffers),
        out_specs=[
            pl.BlockSpec((1, 3 * group, tokens), lambda r: (r, 0, 0)),
            pl.BlockSpec((1, group, tokens), lambda r: (r, 0, 0)),
            whole((width, half)),
            whole((width, half)),
        ],
        scratch_shapes=[
            pltpu.VMEM((ranks, count, width), BF16),
            pltpu.VMEM((group, tokens), BF16),
            pltpu.VMEM((width, tokens), F32),
            pltpu.SemaphoreType.DMA((ranks, 8)),
        ],
        compiler_params=PARAMS,
        cost_estimate=pl.CostEstimate(flops=1, bytes_accessed=1, transcendentals=0),
        name="mixer_forward",
    )(place, live, *tables, normed, own, *buffers)


def mixer_back_kernel(plan, routes, count, sizes, targets, *refs):
    inputs, buffers, outs, scratch = grouped(refs, 9, len(plan), 2 + targets, 6)
    place_ref, live_ref, long_ref, short_ref, normed_ref, coming_ref = inputs[:6]
    proj_ref, long_out_ref, own_ref = inputs[6:]
    kept_ref, sent_ref = outs[:2]
    flat_ref, grads_ref, total, rows_ref, sems, out_sems = scratch
    long, short, chans, per_step = sizes
    fill(plan, place_ref, own_ref, buffers, flat_ref, sems, per_step)
    step = pl.program_id(0)
    layout = layout_of(long, short, normed_ref.shape[1])
    into, out_rows, filters = mixer_rows_of(flat_ref, step, per_step, chans)
    short_taps, cond_taps = mixer_taps(filters, long)
    rows = per_step * chans
    grad_mixed = nn(out_rows, coming_ref[...])
    proj = [proj_ref[0, g * rows : (g + 1) * rows].astype(F32) for g in range(3)]
    query, key_part, value_part = (taps_forward(layout, proj[g], short_taps[g]) for g in range(3))
    live = live_ref[:1]
    gated = key_part * value_part * live
    shaped = taps_forward(layout, gated, cond_taps)
    long_out = long_out_ref[0].astype(F32)
    mixed = (query * long_out).astype(BF16)
    grad_query = grad_mixed * long_out
    grad_long_out = sequences(layout, grad_mixed * query)
    gated_parts, shaped_parts = (sequences(layout, gated), sequences(layout, shaped))
    backs = [
        filter_back(
            filter_of(gated_parts[i], shaped_parts[i], filters[:, :length], ref[...]),
            grad_long_out[i],
            ref[...],
        )
        for i, (length, ref) in enumerate(((long, long_ref), (short, short_ref)))
    ]
    grad_gated = rejoined(backs[0][0], backs[1][0])
    grad_shaped = rejoined(backs[0][1], backs[1][1])
    grad_static = jnp.concatenate(
        [backs[0][2][:, :short] + backs[1][2], backs[0][2][:, short:]], axis=1
    )
    grad_cond = taps_grad(layout, grad_shaped, gated)
    grad_gated = (grad_gated + taps_back(layout, grad_shaped, cond_taps)) * live
    grads = (grad_query, grad_gated * value_part, grad_gated * key_part)
    grad_taps = [taps_grad(layout, grads[g], proj[g]) for g in range(3)]
    grad_proj = jnp.concatenate(
        [taps_back(layout, grads[g], short_taps[g]) for g in range(3)], axis=0
    ).astype(BF16)
    lane = lax.broadcasted_iota(jnp.int32, (1, flat_ref.shape[2] - long), 1)
    lanes = sum(
        jnp.where(lane == 3 * k + group, grad_taps[group][k], 0.0)
        for k in range(3)
        for group in range(3)
    )
    lanes += sum(jnp.where(lane == 9 + k, grad_cond[k], 0.0) for k in range(3))
    grad_into = nt(grad_proj, normed_ref[...]).astype(BF16)
    grad_out = nt(mixed, coming_ref[...]).astype(BF16)
    grad_filters = jnp.concatenate([grad_static, lanes], axis=1).astype(BF16)
    for i in range(per_step):
        part = slice(i * chans, (i + 1) * chans)
        at = step * per_step + i
        for g in range(3):
            grads_ref[at, g * chans : (g + 1) * chans] = grad_into[g * rows : (g + 1) * rows][part]
        grads_ref[at, 3 * chans : 4 * chans] = grad_out[part]
        grads_ref[at, 4 * chans : 5 * chans] = grad_filters[part]
        spare = flat_ref.shape[1] - 5 * chans
        if spare:
            grads_ref[at, 5 * chans :] = jnp.zeros((spare, flat_ref.shape[2]), BF16)
    spilled = (routes, count, place_ref, grads_ref, outs[2:], out_sems, per_step)
    spill(*spilled)
    add_total(total, tn(into, grad_proj))

    @pl.when(step == pl.num_programs(0) - 1)
    def finish():
        core = place_ref[0]
        kept_ref[...] = own_lanes(total, core, layout)
        sent_ref[...] = own_lanes(total, 1 - core, layout).astype(BF16)

    spill_wait(*spilled, True)


def mixer_back(
    place, rows, normed, coming, proj, long_out, live, tables, sizes, routes, blocks, block_rows
):
    outs = 1 + max(target[0] for route in routes for target in route[0].values())
    own, buffers, plan, ranks = rows
    count, width = own.shape
    tokens = normed.shape[1]
    half = tokens // 2
    chans, per_step = sizes[2:]
    steps = ranks // per_step
    group = per_step * chans
    results = pl.pallas_call(
        functools.partial(mixer_back_kernel, plan, routes, plan[0][3], sizes, outs),
        grid=(steps,),
        out_shape=[
            jax.ShapeDtypeStruct((width, half), F32),
            jax.ShapeDtypeStruct((width, half), BF16),
        ]
        + [jax.ShapeDtypeStruct((blocks, block_rows, width), BF16)] * outs,
        in_specs=[SMEM, whole(live.shape)]
        + [whole(t.shape) for t in tables]
        + [
            whole((width, tokens)),
            whole((width, tokens)),
            pl.BlockSpec((1, 3 * group, tokens), lambda r: (r, 0, 0)),
            pl.BlockSpec((1, group, tokens), lambda r: (r, 0, 0)),
            ANY,
        ]
        + [ANY] * len(buffers),
        out_specs=[whole((width, half)), whole((width, half))] + [ANY] * outs,
        scratch_shapes=[
            pltpu.VMEM((ranks, count, width), BF16),
            pltpu.VMEM((ranks, count, width), BF16),
            pltpu.VMEM((width, tokens), F32),
            pltpu.VMEM((8, 128), F32),
            pltpu.SemaphoreType.DMA((ranks, 8)),
            pltpu.SemaphoreType.DMA((ranks, 8)),
        ],
        compiler_params=PARAMS,
        cost_estimate=pl.CostEstimate(flops=1, bytes_accessed=1, transcendentals=0),
        name="mixer_back",
    )(place, live, *tables, normed, coming, proj, long_out, own, *buffers)
    return (results[0], results[1], results[2:])


def final_copies(place_ref, sources, flat_ref, sems):
    copies = []
    for side, source in enumerate(sources):
        core = place_ref[0] if side == 0 else 1 - place_ref[0]
        count = source.shape[1]
        for offset in range(source.shape[0]):
            row = pl.multiple_of((place_ref[1] ^ offset) * count, 16)
            copies.append(
                pltpu.make_async_copy(
                    source.at[offset], flat_ref.at[core, pl.ds(row, count)], sems.at[len(copies)]
                )
            )
    return copies


def final_mlp_kernel(aliased, *refs):
    (place_ref,), sources, _, outs, (flat_ref, sems) = grouped(
        refs, 1, 2, 2 if aliased else 0, 2, 2
    )
    up_ref, down_ref = outs
    step = pl.program_id(0)
    width = flat_ref.shape[2]
    hidden = flat_ref.shape[1] - width

    @pl.when(step == 0)
    def gather():
        copies = final_copies(place_ref, sources, flat_ref, sems)
        for copy in copies:
            copy.start()
        for copy in copies:
            copy.wait()

    rows = up_ref.shape[1]
    part = pl.ds(pl.multiple_of(step * rows, 16), rows)
    for core in range(2):
        lanes = slice(core * hidden, (core + 1) * hidden)
        up_ref[0, :, 0, lanes] = flat_ref[core, part, :hidden].astype(F32)
        up_ref[0, :, 1, lanes] = flat_ref[core, part, hidden:].astype(F32)
    each = down_ref.shape[1]
    per_core = hidden // each
    at = pl.multiple_of(width + (step % per_core) * each, 16)
    down_ref[0] = flat_ref[step // per_core, pl.ds(at, each)].astype(F32)


def final_mlp(place, sources, count, layer, layers, into):
    width = sources[0].shape[2]
    hidden = count - width
    steps = 4
    aliased = into is not None
    return pl.pallas_call(
        functools.partial(final_mlp_kernel, aliased),
        grid=(steps,),
        out_shape=[
            jax.ShapeDtypeStruct((layers, width, 2, 2 * hidden), F32),
            jax.ShapeDtypeStruct((layers, 2 * hidden, width), F32),
        ],
        in_specs=[SMEM] + [ANY] * (4 if aliased else 2),
        out_specs=[
            pl.BlockSpec((1, width // steps, 2, 2 * hidden), lambda i: (layer, i, 0, 0)),
            pl.BlockSpec((1, 2 * hidden // steps, width), lambda i: (layer, i, 0)),
        ],
        input_output_aliases={3: 0, 4: 1} if aliased else {},
        scratch_shapes=[
            pltpu.VMEM((2, count, width), BF16),
            pltpu.SemaphoreType.DMA((2 * sources[0].shape[0],)),
        ],
        compiler_params=PARAMS,
        cost_estimate=pl.CostEstimate(flops=1, bytes_accessed=1, transcendentals=0),
        name="final_mlp",
    )(place, *sources, *(into if aliased else ()))


def final_mixer_kernel(chans, aliased, *refs):
    (place_ref,), sources, _, outs, (flat_ref, sems) = grouped(
        refs, 1, 2, 3 if aliased else 0, 3, 2
    )
    into_ref, out_ref, filter_ref = outs
    copies = final_copies(place_ref, sources, flat_ref, sems)
    for copy in copies:
        copy.start()
    for copy in copies:
        copy.wait()
    for core in range(2):
        lanes = slice(core * chans, (core + 1) * chans)
        for g in range(3):
            into_ref[0, g, lanes] = flat_ref[core, g * chans : (g + 1) * chans].astype(F32)
        out_ref[0, lanes] = flat_ref[core, 3 * chans : 4 * chans].astype(F32)
        filter_ref[0, lanes] = flat_ref[core, 4 * chans : 5 * chans].astype(F32)


def final_mixer(place, sources, count, chans, layer, layers, into):
    width = sources[0].shape[2]
    aliased = into is not None
    return pl.pallas_call(
        functools.partial(final_mixer_kernel, chans, aliased),
        grid=(1,),
        out_shape=[
            jax.ShapeDtypeStruct((layers, 3, 2 * chans, width), F32),
            jax.ShapeDtypeStruct((layers, 2 * chans, width), F32),
            jax.ShapeDtypeStruct((layers, 2 * chans, width), F32),
        ],
        in_specs=[SMEM] + [ANY] * (5 if aliased else 2),
        out_specs=[
            pl.BlockSpec((1, 3, 2 * chans, width), lambda i: (layer, 0, 0, 0)),
            pl.BlockSpec((1, 2 * chans, width), lambda i: (layer, 0, 0)),
            pl.BlockSpec((1, 2 * chans, width), lambda i: (layer, 0, 0)),
        ],
        input_output_aliases={3: 0, 4: 1, 5: 2} if aliased else {},
        scratch_shapes=[
            pltpu.VMEM((2, count, width), BF16),
            pltpu.SemaphoreType.DMA((2 * sources[0].shape[0],)),
        ],
        compiler_params=PARAMS,
        cost_estimate=pl.CostEstimate(flops=1, bytes_accessed=1, transcendentals=0),
        name="final_mixer",
    )(place, *sources, *(into if aliased else ()))


def norm_forward(values, gain):
    average = jnp.mean(values, axis=0, keepdims=True)
    centered = values - average
    inv_std = lax.rsqrt(jnp.mean(centered * centered, axis=0, keepdims=True) + EPS)
    normal_rows = centered * inv_std
    return ((normal_rows * gain).astype(BF16), (normal_rows, inv_std, gain))


def norm_back(grads, stored):
    normal_rows, inv_std, gain = stored
    scaled = grads * gain
    total = jnp.mean(scaled, axis=0, keepdims=True)
    crossed = jnp.mean(scaled * normal_rows, axis=0, keepdims=True)
    gain_grad = jnp.sum(grads * normal_rows, axis=1)
    return (inv_std * (scaled - total - normal_rows * crossed), gain_grad)


def on_device(
    input_long,
    input_short,
    length_long,
    length_short,
    gain_mixer,
    weight_in,
    short_taps,
    cond_taps,
    static_filter,
    weight_out,
    gain_mlp,
    weight_up,
    weight_down,
    grad_long,
    grad_short,
):
    count_long, seq_long, chan_width = input_long.shape
    count_short, seq_short = (input_short.shape[0], input_short.shape[1])
    layers = weight_in.shape[0]
    ranks = lax.axis_size("chan")
    pairs = lax.axis_size("batch") // 2
    place = lax.axis_index("chan")
    core = lax.axis_index("batch") % 2
    pair = lax.axis_index("batch") // 2
    width = chan_width * ranks
    hidden = weight_down.shape[1] // 2
    chans = chan_width // 2
    half_long = seq_long // 2
    tokens = half_long + seq_short
    mate = ("batch", 1)
    first = core == 0
    pieces = 4
    piece = pair % pieces
    plane = {1: ("batch", 2), 2: ("batch", 4)}
    extra_steps = []
    mask = 2 * pieces
    while mask < 2 * pairs:
        extra_steps.append(("batch", mask))
        mask *= 2
    spot = jnp.stack([core, piece, place]).astype(jnp.int32)
    plane_orders = ((1, 2), (2, 1))

    def to_tokens(long_rows, short_rows, extra=None):
        turned = jnp.swapaxes(long_rows, 1, 2).astype(BF16)
        halves = jnp.stack([turned[..., :half_long], turned[..., half_long:]])
        kept = pick(halves, core)
        came = swap(pick(halves, 1 - core), mate)
        ordered = jnp.where(first, jnp.concatenate([kept, came]), jnp.concatenate([came, kept]))
        parts = [ordered, jnp.swapaxes(short_rows, 1, 2).astype(BF16)]
        if extra is not None:
            parts.append(jnp.broadcast_to(extra[None], (ranks,) + extra.shape))
        yield from exchange(jnp.concatenate(parts, axis=2), lambda v: v.reshape(width, -1))

    def exchange(blocks, then):
        came = {0: pick(blocks, place)}
        both = jnp.stack([pick(blocks, place ^ FAR), pick(blocks, place ^ NEAR ^ FAR)])
        first_came = swap(both, ("chan", FAR))
        first_came = after(first_came, *(yield [both]))
        came[FAR] = first_came[0]
        both = jnp.stack([pick(blocks, place ^ NEAR), first_came[1]])
        second_came = swap(both, ("chan", NEAR))
        second_came = after(second_came, *(yield [both]))
        came[NEAR], came[NEAR ^ FAR] = (second_came[0], second_came[1])
        result = then(by_xor(jnp.stack([came[r] for r in range(ranks)]), place))
        yield result

    def from_tokens(values):
        steps = exchange(values.reshape(ranks, chan_width, -1), lambda gathered: gathered)
        ties = yield next(steps)
        ties = yield steps.send(ties)
        gathered = steps.send(ties)
        halves = gathered[:, :, :half_long].reshape(2, count_long, chan_width, half_long)
        kept = pick(halves, core)
        sent = pick(halves, 1 - core)
        came = swap(sent, mate)
        came = after(came, *(yield [sent]))
        ordered = jnp.where(
            first, jnp.concatenate([kept, came], axis=2), jnp.concatenate([came, kept], axis=2)
        )
        short_part = jnp.swapaxes(gathered[:, :, half_long:tokens], 1, 2)
        yield (jnp.swapaxes(ordered, 1, 2), short_part, gathered[:, :, tokens:])

    def both_cores(values):
        return jnp.concatenate([values, swap(values, mate)], axis=1)

    def both_ordered(values):
        came = swap(values, mate)
        low, high = (jnp.where(first, values, came), jnp.where(first, came, values))
        return jnp.concatenate(
            [low[:, :half_long], high[:, :half_long], low[:, half_long:], high[:, half_long:]],
            axis=1,
        )

    def own_sum(sent, kept):
        return kept + swap(sent, mate).astype(F32)

    def mlp_rows(layer):
        up = lax.dynamic_slice_in_dim(weight_up[layer], core * hidden, hidden, 2)
        down = lax.dynamic_slice_in_dim(weight_down[layer], core * hidden, hidden, 0)
        return jnp.concatenate([up.reshape(width, 2 * hidden), down])

    def mixer_rows(layer):
        into = jnp.transpose(weight_in[layer], (1, 2, 0))
        into = lax.dynamic_slice_in_dim(into, core * chans, chans, 1)
        out = lax.dynamic_slice_in_dim(weight_out[layer], core * chans, chans, 0)
        taps = jnp.concatenate([short_taps[layer].reshape(9, chan_width), cond_taps[layer]]).T
        coarse = lax.reduce_precision(taps, 8, 7)
        static = jnp.concatenate([static_filter[layer].T, coarse, taps - coarse], axis=1)
        static = jnp.pad(static.astype(BF16), ((0, 0), (0, width - static.shape[1])))
        static = lax.dynamic_slice_in_dim(static, core * chans, chans, 0)
        spare = jnp.zeros((mixer_count - 5 * chans, width), BF16)
        return jnp.concatenate([into.reshape(3 * chans, width), out, static, spare])

    mixer_count = -(-5 * chans // (32 * pieces)) * 32 * pieces
    mlp_count = width + hidden
    own_rows = [
        {"mixer": mixer_rows(layer), "mlp": mlp_rows(layer)} for layer in range(layers)
    ]

    def half_rows(kind):
        return (mixer_count if kind == "mixer" else mlp_count) // (2 * pieces)

    def own_block(layer, kind, half):
        count = half_rows(kind)
        return lax.dynamic_slice_in_dim(
            own_rows[layer][kind], (piece * 2 + half) * count, count, 0
        )

    others = (FAR, NEAR, FAR ^ NEAR)

    def gather(layer, kind):
        block = jnp.concatenate([own_block(layer, kind, half) for half in range(2)])[None]
        count = half_rows(kind)
        far = swap(block, ("chan", FAR))
        far = after(far, *(yield [block]))
        both = jnp.concatenate([block, far])
        near = swap(both, ("chan", NEAR))
        near = after(near, *(yield [both]))
        foreign = jnp.concatenate([far, near])
        held = [foreign[:, half * count : (half + 1) * count] for half in range(2)]
        came = [swap(held[half], plane[plane_orders[half][0]]) for half in range(2)]
        ties = yield held
        held = [jnp.concatenate([held[half], after(came[half], *ties)]) for half in range(2)]
        buffers, plan = ([], [])
        for half, (one, two) in enumerate(plane_orders):
            blocks = [(0, other) for other in others] + [(one, other) for other in others]
            buffers += [held[half], swap(held[half], plane[two])]
            plan.append((half, tuple(blocks), 0, count))
            plan.append((half, tuple((offset ^ two, other) for offset, other in blocks), 0, count))
        weights[layer, kind] = (own_rows[layer][kind], tuple(buffers), tuple(plan), ranks)
        yield held

    line = []

    def go(steps, *ties):
        line[:] = steps.send((*line, *ties))

    def begin(steps):
        line.extend(next(steps))
        return steps

    def finish(steps):
        return steps.send(tuple(line))

    weights = {}
    gains = jnp.stack([gain_mixer, gain_mlp], axis=1).reshape(2 * layers, chan_width)
    gains_coarse = lax.reduce_precision(gains, 8, 7)
    gains = jnp.concatenate([gains_coarse, gains - gains_coarse]).astype(BF16).T
    gains = jnp.pad(gains, ((0, 0), (0, 128 - gains.shape[1])))
    mixer_0 = begin(gather(0, "mixer"))
    input_steps = begin(to_tokens(input_long, input_short, gains))
    mlp_0 = begin(gather(0, "mlp"))
    go(mixer_0)
    go(input_steps)
    go(mixer_0)
    go(mlp_0)
    arrived = finish(input_steps)
    gains = arrived[:, tokens : tokens + 4 * layers].astype(F32)
    gains = gains[:, : 2 * layers] + gains[:, 2 * layers :]
    gains = gains.T.reshape(layers, 2, width, 1)

    own_lengths = jnp.concatenate([length_long, length_short])
    other_lengths = swap(own_lengths, mate)
    low, high = (
        jnp.where(first, own_lengths, other_lengths),
        jnp.where(first, other_lengths, own_lengths),
    )
    spans = [pick(jnp.concatenate([low[:count_long], high[:count_long]]), place)]
    spans += [pick(side[count_long:], place) for side in (low, high)]
    live = jnp.concatenate(
        [
            jnp.arange(length) < span
            for length, span in zip((seq_long, seq_short, seq_short), spans)
        ]
    )
    live = jnp.broadcast_to(live.astype(F32)[None], (8, live.shape[0]))
    tables = (table(seq_long), table(seq_short))
    sizes = (seq_long, seq_short, chans, 2)

    chan_order = (0, FAR, NEAR, NEAR ^ FAR)

    def routes(near_first, count, single=False):
        found = []
        for half, (one, two) in enumerate(((1, 2), (1, 2)) if single else plane_orders):
            for a in range(2):
                for c in range(2):
                    if near_first:
                        targets = {r: (i // 2, 4 * a + 2 * c + i % 2) for i, r in enumerate(chan_order)}
                    else:
                        targets = {r: (2 * half + a, ranks * c + i) for i, r in enumerate(chan_order)}
                    found.append((targets, half, a * one + c * two, near_first * half * count))
        return tuple(found)

    mlp_half, mixer_half = (half_rows("mlp"), half_rows("mixer"))
    residual_start = arrived[:, :tokens].astype(F32)
    residual = residual_start
    stored_all = []
    for layer in range(layers):
        normed, norm_stored = norm_forward(residual, gains[layer, 0])
        normed = both_ordered(normed)
        if layer == 0:
            mixer_1 = begin(gather(1, "mixer"))
            go(mixer_0)
            go(mlp_0)
        else:
            go(mlp_1)
        proj, long_out, kept, sent = mixer_forward(
            spot, weights[layer, "mixer"], after(normed, *line), live, tables, sizes
        )
        if layer == 0:
            go(mixer_1, kept)
        else:
            grad_steps = begin(to_tokens(grad_long, grad_short))
        sent = after(sent, *line)
        middle = residual + own_sum(sent, kept)
        normed_mlp, mlp_stored = norm_forward(middle, gains[layer, 1])
        normed_mlp = both_cores(normed_mlp)
        if layer == 0:
            go(mlp_0)
            mlp_1 = begin(gather(1, "mlp"))
            go(mixer_1)
            go(mlp_1)
            go(mixer_1)
            go(mlp_1)
            gate_up, kept, sent = mlp_forward(
                spot, weights[layer, "mlp"], after(normed_mlp, *line)
            )
        else:
            go(grad_steps)
            upstream = finish(grad_steps).astype(F32)
            coming = both_cores(upstream.astype(BF16))
            gate_up = None
            (kept, sent, *turned), blocks = mlp_turn(
                spot, weights[layer, "mlp"], after(normed_mlp, *line), coming, routes(False, mlp_half),
                2 * ranks, mlp_half,
            )
        residual = middle + own_sum(sent, kept)
        stored_all.append((normed, norm_stored, proj, long_out, normed_mlp, mlp_stored, gate_up))
    output_steps = from_tokens((residual - residual_start).astype(BF16))

    def added(values):
        return sum(value.astype(F32) for value in values).astype(BF16)

    def spread_sums(block, early):
        for step in extra_steps:
            block = added([block, swap(block, step)])
        parts = [(block, plane_orders[early])] if early is not None else []
        if early is None:
            middle = block.shape[1] // 2
            parts = [(block[:, :middle], plane_orders[0]), (block[:, middle:], plane_orders[1])]
        came = [swap(part, plane[one]) for part, (one, _) in parts]
        ties = yield [part for part, _ in parts]
        both = [jnp.concatenate([part, after(c, *ties)]) for (part, _), c in zip(parts, came)]
        came = [swap(part, plane[two]) for part, (_, (_, two)) in zip(both, parts)]
        ties = yield both
        pieces_of = []
        for part, c, (_, (one, two)) in zip(both, came, parts):
            c = after(c, *ties)
            by = {0: part[:1], one: part[1:], two: c[:1], one ^ two: c[1:]}
            pieces_of.append(jnp.concatenate([by[offset] for offset in range(pieces)]))
        mine = jnp.concatenate(pieces_of, axis=1)
        came = swap(mine, mate)
        ties = yield [mine]
        yield (mine, after(came, *ties))

    def scatter(blocks, early, single=False):
        near_first = len(blocks) == 2
        orders = ((1, 2),) if single else plane_orders
        if near_first:
            came = swap(blocks[1], ("chan", NEAR))
            ties = yield [blocks[1]]
            block = added([blocks[0], after(came, *ties)])
            count = block.shape[1] // len(orders)
            parts = [block[:, i * count : (i + 1) * count] for i in range(len(orders))]
            kept = [part[:4] for part in parts]
            sent = [part[4:] for part in parts]
        else:
            kept, sent = (blocks[0::2], blocks[1::2])
        came = [swap(part, plane[one]) for part, (one, _) in zip(sent, orders)]
        ties = yield list(sent)
        came = [after(value, *ties) for value in came]
        middle = kept[0].shape[0] // 2
        sent = [added([k[middle:], c[middle:]]) for k, c in zip(kept, came)]
        kept = [added([k[:middle], c[:middle]]) for k, c in zip(kept, came)]
        came = [swap(part, plane[two]) for part, (_, two) in zip(sent, orders)]
        ties = yield sent
        came = [after(value, *ties) for value in came]
        block = jnp.concatenate([added([k, c]) for k, c in zip(kept, came)], axis=1)
        for mask in (FAR,) if near_first else (NEAR, FAR):
            kept, sent = (block[: block.shape[0] // 2], block[block.shape[0] // 2 :])
            came = swap(sent, ("chan", mask))
            ties = yield [sent]
            block = added([kept, after(came, *ties)])
        yield from spread_sums(block, early)

    upstream_start = upstream
    gain_grads = {}
    scatters = []

    line[:] = []
    for layer in reversed(range(layers)):
        normed, norm_stored, proj, long_out, normed_mlp, mlp_stored, gate_up = stored_all[layer]
        last = layer == 0
        if gate_up is None:
            kept, sent = turned
        else:
            coming = both_cores(upstream.astype(BF16))
            kept, sent, blocks = mlp_back(
                spot, weights[layer, "mlp"], normed_mlp, gate_up, coming,
                routes(False, mlp_half), 2 * ranks, mlp_half,
            )
        if last:
            go(scatters[0], kept)
            go(scatters[1], kept)
        scatters.append(begin(scatter(blocks, None if last else 0)))
        sent = after(sent, *line)
        change, gain_grads[layer, 1] = norm_back(own_sum(sent, kept), mlp_stored)
        upstream = upstream + change
        coming = both_ordered(upstream.astype(BF16))
        if not last:
            begin(output_steps)
        kept, sent, blocks = mixer_back(
            spot, weights[layer, "mixer"], normed, after(coming, *line), proj, long_out, live,
            tables, sizes, routes(True, mixer_half, not last), 2 * ranks, 2 * mixer_half,
        )
        if last:
            scatters.append(begin(scatter(blocks, None)))
            go(scatters[2], kept)
            go(scatters[0], kept)
        else:
            go(scatters[0], kept)
            scatters.append(begin(scatter(blocks, 1, True)))
        sent = after(sent, *line)
        change, gain_grads[layer, 0] = norm_back(own_sum(sent, kept), norm_stored)
        upstream = upstream + change
        if not last:
            go(output_steps)

    mlp_early, mixer_early, mlp_late, mixer_late = scatters

    gain_parts = jnp.stack(
        [gain_grads[layer, which] for layer in range(layers) for which in range(2)], axis=1
    )
    gain_coarse = lax.reduce_precision(gain_parts, 8, 7)
    gain_lanes = jnp.concatenate([gain_coarse, gain_parts - gain_coarse], axis=1).astype(BF16)
    gain_lanes = jnp.pad(gain_lanes, ((0, 0), (0, 128 - gain_lanes.shape[1])))
    go(output_steps)
    go(mixer_early)
    go(mlp_late)
    go(mlp_early)
    gone_long, gone_short, _ = finish(output_steps)
    output_long = input_long + gone_long.astype(F32)
    output_short = input_short + gone_short.astype(F32)
    line.append(output_long)
    go(mixer_late)
    changed = jnp.concatenate([(upstream - upstream_start).astype(BF16), gain_lanes], axis=1)
    back_steps = begin(from_tokens(after(changed, *line)))
    go(mixer_early)
    go(mlp_late)
    go(mlp_early)
    go(mixer_late)
    go(mixer_early)
    go(back_steps)
    go(mlp_late)
    go(mixer_late)
    go(mlp_early)
    go(mixer_early)
    go(back_steps)
    go(mlp_late)
    go(mixer_late)
    mlp_out = final_mlp(spot, finish(mlp_early), mlp_count, 1, layers, None)
    line.append(mlp_out[1])
    go(mixer_early)
    gone_long, gone_short, gain_sums = finish(back_steps)
    back_long = grad_long + gone_long.astype(F32)
    back_short = grad_short + gone_short.astype(F32)
    line.append(back_long)
    gain_sums = jnp.sum(gain_sums[:, :, : 4 * layers].astype(F32), axis=0)
    gain_sums = (gain_sums[:, : 2 * layers] + gain_sums[:, 2 * layers :]).T


    def reduced(values):
        for step in [mate] + list(plane.values()) + extra_steps:
            came = swap(values, step)
            values = values + after(came, *(yield [values]))
        yield values

    gain_steps = begin(reduced(gain_sums))
    go(mlp_late)
    go(gain_steps)
    go(mixer_late)
    go(gain_steps)
    for _ in extra_steps:
        go(gain_steps)
    mixer_out = final_mixer(spot, finish(mixer_early), mixer_count, chans, 1, layers, None)
    line.append(mixer_out[1])
    gain_sums = finish(gain_steps)
    mlp_out = final_mlp(spot, finish(mlp_late), mlp_count, 0, layers, mlp_out)
    line.append(mlp_out[1])
    go(mixer_late)
    mixer_out = final_mixer(spot, finish(mixer_late), mixer_count, chans, 0, layers, mixer_out)
    into_out, out_out, filter_out = mixer_out
    taps = jnp.swapaxes(filter_out[:, :, seq_long : seq_long + 12], 1, 2)

    return (
        output_long,
        output_short,
        back_long,
        back_short,
        gain_sums[0::2],
        jnp.transpose(into_out, (0, 3, 1, 2)),
        taps[:, :9].reshape(layers, 3, 3, chan_width),
        taps[:, 9:],
        jnp.swapaxes(filter_out[:, :, :seq_long], 1, 2),
        out_out,
        gain_sums[1::2],
        mlp_out[0],
        mlp_out[1],
    )


def solution(mesh):
    tokens = P("batch", None, "chan")
    placed = (
        tokens,
        tokens,
        P("batch"),
        P("batch"),
        P(None, "chan"),
        P(None, None, None, "chan"),
        P(None, None, None, "chan"),
        P(None, None, "chan"),
        P(None, None, "chan"),
        P(None, "chan", None),
        P(None, "chan"),
        P(None, None, None, "chan"),
        P(None, "chan", None),
        tokens,
        tokens,
    )
    return jax.shard_map(
        on_device,
        mesh=mesh,
        in_specs=placed,
        out_specs=(tokens,) * 4 + placed[4:13],
        check_vma=False,
    )
```

```python
import functools
import math

import jax
import jax.numpy as jnp
import numpy as np
from jax import lax
from jax.experimental import pallas as pl
from jax.experimental.pallas import tpu as pltpu
from jax.sharding import PartitionSpec as P

EPS = 1e-05
BF16 = jnp.bfloat16
F32 = jnp.float32
VMEM_BYTES = 52 * 2**20
FAR, NEAR = (3, 1)


def nn(left, right):
    return lax.dot_general(left, right, (((1,), (0,)), ((), ())), preferred_element_type=F32)


def nt(left, right):
    return lax.dot_general(left, right, (((1,), (1,)), ((), ())), preferred_element_type=F32)


def tn(left, right):
    return lax.dot_general(left, right, (((0,), (0,)), ((), ())), preferred_element_type=F32)


def table(length):
    places = np.arange(length)[:, None]
    phase = (places * np.arange(length + 1)[None, :] % (2 * length)) * (np.pi / length)
    packed = np.concatenate(
        [np.cos(phase[:, :length]), np.cos(phase[:, length:]), -np.sin(phase[:, 1:length])], axis=1
    )
    return jnp.asarray(packed.astype(np.float32)).astype(BF16)


def swap(values, step):
    axis, mask = step
    return lax.ppermute(values, axis, [(i, i ^ mask) for i in range(lax.axis_size(axis))])


def after(values, *others):
    return lax.optimization_barrier((values,) + others)[0]


def pick(values, index):
    return lax.dynamic_index_in_dim(values, index, 0, keepdims=False)


def by_xor(values, index):
    return jnp.stack([pick(values, place ^ index) for place in range(values.shape[0])])


def block_copies(plan, place_ref, own_ref, buffers, flat_ref, sems, wanted):
    if wanted == 0:
        return [pltpu.make_async_copy(own_ref, flat_ref.at[0], sems.at[0, 0])]
    copies = []
    for buffer, (half, blocks, start, count) in zip(buffers, plan):
        for at, (offset, other) in enumerate(blocks):
            if other == wanted:
                row = pl.multiple_of(((place_ref[1] ^ offset) * 2 + half) * count, 16)
                copies.append(
                    pltpu.make_async_copy(
                        buffer.at[at, pl.ds(start, count)],
                        flat_ref.at[wanted, pl.ds(row, count)],
                        sems.at[wanted, len(copies)],
                    )
                )
    return copies


def fill(plan, place_ref, own_ref, buffers, flat_ref, sems, per_step):
    step = pl.program_id(0)
    ranks = flat_ref.shape[0]
    args = (plan, place_ref, own_ref, buffers, flat_ref, sems)

    @pl.when(step == 0)
    def begin():
        for wanted in range(ranks):
            for copy in block_copies(*args, wanted):
                copy.start()

    for wanted in range(ranks):

        @pl.when(step == wanted // per_step)
        def arrive():
            for copy in block_copies(*args, wanted):
                copy.wait()


def spill_copies(routes, count, place_ref, rows_ref, outs, sems, slot, wanted):
    copies = []
    for targets, half, offset, start in routes:
        out, at = targets[wanted]
        row = pl.multiple_of(((place_ref[1] ^ offset) * 2 + half) * count, 16)
        copies.append(
            pltpu.make_async_copy(
                rows_ref.at[slot, pl.ds(row, count)],
                outs[out].at[at, pl.ds(start, count)],
                sems.at[slot, len(copies)],
            )
        )
    return copies


def grouped(refs, *counts):
    groups, at = ([], 0)
    for count in counts:
        groups.append(refs[at : at + count])
        at += count
    return groups


def whole(shape):
    return pl.BlockSpec(shape, lambda i: (0,) * len(shape))


SMEM = pl.BlockSpec(memory_space=pltpu.SMEM)
ANY = pl.BlockSpec(memory_space=pl.ANY)
PARAMS = pltpu.CompilerParams(vmem_limit_bytes=VMEM_BYTES)


def gelu_parts(gate):
    slope = math.sqrt(2.0 / math.pi)
    square = gate * gate
    bent = jnp.tanh(slope * (gate + 0.044715 * square * gate))
    gelu = 0.5 * gate * (1.0 + bent)
    grad = 0.5 * (1.0 + bent) + 0.5 * gate * (1.0 - bent * bent) * slope * (
        1.0 + 0.134145 * square
    )
    return (gelu, grad)


def add_total(total, part):
    step = pl.program_id(0)

    @pl.when(step == 0)
    def start():
        total[...] = part

    @pl.when(step > 0)
    def add():
        total[...] += part


def split_total(total, kept_ref, sent_ref):
    @pl.when(pl.program_id(0) == pl.num_programs(0) - 1)
    def finish():
        own = kept_ref.shape[1]
        kept_ref[...] = total[:, :own]
        sent_ref[...] = total[:, own:].astype(BF16)


def mlp_forward_kernel(plan, *refs):
    (place_ref, normed_ref, own_ref), buffers, outs, scratch = grouped(refs, 3, len(plan), 3, 3)
    gate_up_ref, kept_ref, sent_ref = outs
    flat_ref, total, sems = scratch
    fill(plan, place_ref, own_ref, buffers, flat_ref, sems, 1)
    step = pl.program_id(0)
    width = normed_ref.shape[0]
    hidden = flat_ref.shape[1] - width
    gate_up = tn(flat_ref[step, :width], normed_ref[...])
    gate_up_ref[0] = gate_up.astype(BF16)
    activated = (gelu_parts(gate_up[:hidden])[0] * gate_up[hidden:]).astype(BF16)
    add_total(total, tn(flat_ref[step, width:], activated))
    split_total(total, kept_ref, sent_ref)


def mlp_forward(place, rows, normed):
    own, buffers, plan, ranks = rows
    count, width = own.shape
    tokens = normed.shape[1]
    hidden = count - width
    half = tokens // 2
    return pl.pallas_call(
        functools.partial(mlp_forward_kernel, plan),
        grid=(ranks,),
        out_shape=[
            jax.ShapeDtypeStruct((ranks, 2 * hidden, tokens), BF16),
            jax.ShapeDtypeStruct((width, half), F32),
            jax.ShapeDtypeStruct((width, half), BF16),
        ],
        in_specs=[SMEM, whole((width, tokens)), ANY] + [ANY] * len(buffers),
        out_specs=[
            pl.BlockSpec((1, 2 * hidden, tokens), lambda r: (r, 0, 0)),
            whole((width, half)),
            whole((width, half)),
        ],
        scratch_shapes=[
            pltpu.VMEM((ranks, count, width), BF16),
            pltpu.VMEM((width, tokens), F32),
            pltpu.SemaphoreType.DMA((ranks, 8)),
        ],
        compiler_params=PARAMS,
        cost_estimate=pl.CostEstimate(flops=1, bytes_accessed=1, transcendentals=0),
        name="mlp_forward",
    )(place, normed, own, *buffers)


def spill(routes, count, place_ref, grads_ref, outs, sems, per_step):
    step = pl.program_id(0)
    ranks = per_step * pl.num_programs(0)
    for wanted in range(ranks):
        at = wanted // per_step
        slot = (at % 2) * per_step + wanted % per_step

        @pl.when(step == at)
        def leave():
            for copy in spill_copies(
                routes, count, place_ref, grads_ref, outs, sems, slot, wanted
            ):
                copy.start()


def spill_wait(routes, count, place_ref, grads_ref, outs, sems, per_step, last):
    step = pl.program_id(0)
    steps = 4 // per_step
    for wanted in range(4):
        at = wanted // per_step
        slot = (at % 2) * per_step + wanted % per_step
        due = steps - 1 if last else at + 2
        if last and at + 2 < steps:
            continue
        if not last and at + 2 >= steps:
            continue

        @pl.when(step == due)
        def gone():
            for copy in spill_copies(
                routes, count, place_ref, grads_ref, outs, sems, slot, wanted
            ):
                copy.wait()


def mlp_back_kernel(plan, routes, count, *refs):
    (place_ref, normed_ref, coming_ref, gate_up_ref, own_ref), buffers, outs, scratch = grouped(
        refs, 5, len(plan), 6, 5
    )
    kept_ref, sent_ref = outs[:2]
    flat_ref, grads_ref, total, sems, out_sems = scratch
    fill(plan, place_ref, own_ref, buffers, flat_ref, sems, 1)
    step = pl.program_id(0)
    width = normed_ref.shape[0]
    hidden = flat_ref.shape[1] - width
    spilled = (routes, count, place_ref, grads_ref, outs[2:], out_sems, 1)
    spill_wait(*spilled, False)
    slot = step % 2
    gate = gate_up_ref[0, :hidden].astype(F32)
    up = gate_up_ref[0, hidden:].astype(F32)
    grad_act = nn(flat_ref[step, width:], coming_ref[...])
    gelu, slope = gelu_parts(gate)
    activated = (gelu * up).astype(BF16)
    grad_gate = (grad_act * up * slope).astype(BF16)
    grad_up = (grad_act * gelu).astype(BF16)
    grads_ref[slot, width:] = nt(activated, coming_ref[...]).astype(BF16)
    grads_ref[slot, :width, :hidden] = nt(normed_ref[...], grad_gate).astype(BF16)
    grads_ref[slot, :width, hidden:] = nt(normed_ref[...], grad_up).astype(BF16)
    spill(*spilled)
    add_total(
        total,
        nn(flat_ref[step, :width, :hidden], grad_gate)
        + nn(flat_ref[step, :width, hidden:], grad_up),
    )
    split_total(total, kept_ref, sent_ref)
    spill_wait(*spilled, True)


def mlp_back(place, rows, normed, gate_up, coming, routes, blocks, block_rows):
    own, buffers, plan, ranks = rows
    count, width = own.shape
    tokens = normed.shape[1]
    hidden = count - width
    half = tokens // 2
    results = pl.pallas_call(
        functools.partial(mlp_back_kernel, plan, routes, plan[0][3]),
        grid=(ranks,),
        out_shape=[
            jax.ShapeDtypeStruct((width, half), F32),
            jax.ShapeDtypeStruct((width, half), BF16),
        ]
        + [jax.ShapeDtypeStruct((blocks, block_rows, width), BF16)] * 4,
        in_specs=[
            SMEM,
            whole((width, tokens)),
            whole((width, tokens)),
            pl.BlockSpec((1, 2 * hidden, tokens), lambda r: (r, 0, 0)),
            ANY,
        ]
        + [ANY] * len(buffers),
        out_specs=[whole((width, half)), whole((width, half))] + [ANY] * 4,
        scratch_shapes=[
            pltpu.VMEM((ranks, count, width), BF16),
            pltpu.VMEM((2, count, width), BF16),
            pltpu.VMEM((width, tokens), F32),
            pltpu.SemaphoreType.DMA((ranks, 8)),
            pltpu.SemaphoreType.DMA((2, 8)),
        ],
        compiler_params=PARAMS,
        cost_estimate=pl.CostEstimate(
            flops=12 * ranks * hidden * width * tokens,
            bytes_accessed=4 * ranks * own.size + 4 * ranks * hidden * tokens,
            transcendentals=ranks * hidden * tokens,
        ),
        name="mlp_back",
    )(place, normed, coming, gate_up, own, *buffers)
    return (results[0], results[1], results[2:])


def mlp_turn_kernel(plan, routes, count, *refs):
    (place_ref, normed_ref, coming_ref, own_ref), buffers, outs, scratch = grouped(
        refs, 4, len(plan), 8, 6
    )
    flat_ref, grads_ref, total, back_total, sems, out_sems = scratch
    fill(plan, place_ref, own_ref, buffers, flat_ref, sems, 1)
    step = pl.program_id(0)
    width = normed_ref.shape[0]
    hidden = flat_ref.shape[1] - width
    spilled = (routes, count, place_ref, grads_ref, outs[4:], out_sems, 1)
    spill_wait(*spilled, False)
    slot = step % 2
    gate_up = tn(flat_ref[step, :width], normed_ref[...])
    gate, up = (gate_up[:hidden], gate_up[hidden:])
    grad_act = nn(flat_ref[step, width:], coming_ref[...])
    gelu, slope = gelu_parts(gate)
    activated = (gelu * up).astype(BF16)
    grad_gate = (grad_act * up * slope).astype(BF16)
    grad_up = (grad_act * gelu).astype(BF16)
    add_total(total, tn(flat_ref[step, width:], activated))
    grads_ref[slot, width:] = nt(activated, coming_ref[...]).astype(BF16)
    grads_ref[slot, :width, :hidden] = nt(normed_ref[...], grad_gate).astype(BF16)
    grads_ref[slot, :width, hidden:] = nt(normed_ref[...], grad_up).astype(BF16)
    spill(*spilled)
    add_total(
        back_total,
        nn(flat_ref[step, :width, :hidden], grad_gate)
        + nn(flat_ref[step, :width, hidden:], grad_up),
    )
    split_total(total, outs[0], outs[1])
    split_total(back_total, outs[2], outs[3])
    spill_wait(*spilled, True)


def mlp_turn(place, rows, normed, coming, routes, blocks, block_rows):
    own, buffers, plan, ranks = rows
    count, width = own.shape
    tokens = normed.shape[1]
    hidden = count - width
    half = tokens // 2
    results = pl.pallas_call(
        functools.partial(mlp_turn_kernel, plan, routes, plan[0][3]),
        grid=(ranks,),
        out_shape=[
            jax.ShapeDtypeStruct((width, half), F32),
            jax.ShapeDtypeStruct((width, half), BF16),
        ]
        * 2
        + [jax.ShapeDtypeStruct((blocks, block_rows, width), BF16)] * 4,
        in_specs=[SMEM, whole((width, tokens)), whole((width, tokens)), ANY]
        + [ANY] * len(buffers),
        out_specs=[whole((width, half))] * 4 + [ANY] * 4,
        scratch_shapes=[
            pltpu.VMEM((ranks, count, width), BF16),
            pltpu.VMEM((2, count, width), BF16),
            pltpu.VMEM((width, tokens), F32),
            pltpu.VMEM((width, tokens), F32),
            pltpu.SemaphoreType.DMA((ranks, 8)),
            pltpu.SemaphoreType.DMA((2, 8)),
        ],
        compiler_params=PARAMS,
        cost_estimate=pl.CostEstimate(flops=1, bytes_accessed=1, transcendentals=0),
        name="mlp_turn",
    )(place, normed, coming, own, *buffers)
    return (results[:4], results[4:])


def delayed(layout, values, by):
    return jnp.where(layout["inside"] >= by, pltpu.roll(values, by, 1), 0.0)


def advanced(layout, values, by):
    moved = pltpu.roll(values, layout["tokens"] - by, 1)
    return jnp.where(layout["inside"] < layout["length"] - by, moved, 0.0)


def layout_of(long, short, tokens):
    lane = lax.broadcasted_iota(jnp.int32, (1, tokens), 1)
    return {
        "long": long,
        "short": short,
        "tokens": tokens,
        "inside": jnp.where(lane < long, lane, (lane - long) % short),
        "length": jnp.where(lane < long, long, short),
    }


def taps_forward(layout, values, taps):
    return (
        taps[0] * values
        + taps[1] * delayed(layout, values, 1)
        + taps[2] * delayed(layout, values, 2)
    )


def taps_back(layout, values, taps):
    return (
        taps[0] * values
        + taps[1] * advanced(layout, values, 1)
        + taps[2] * advanced(layout, values, 2)
    )


def taps_grad(layout, grads, values):
    moved = [values, delayed(layout, values, 1), delayed(layout, values, 2)]
    return [jnp.sum(grads * value, axis=1, keepdims=True) for value in moved]


def sequences(layout, values):
    long, short = (layout["long"], layout["short"])
    shorts = [values[:, at : at + short] for at in range(long, layout["tokens"], short)]
    return (values[:, :long], jnp.concatenate(shorts, axis=0))


def rejoined(long_part, short_part):
    rows = long_part.shape[0]
    shorts = [short_part[at * rows : (at + 1) * rows] for at in range(short_part.shape[0] // rows)]
    return jnp.concatenate([long_part] + shorts, axis=1)


def repeated(values, times):
    return jnp.concatenate([values] * times, axis=0) if times > 1 else values


def at_edge(edge, edge_values, others):
    head = jnp.where(edge[:, :128], edge_values, others[:, :128])
    return jnp.concatenate([head, others[:, 128:]], axis=1) if others.shape[1] > 128 else head


def turned_back(real_part, imag_part, cosines):
    return nt(jnp.concatenate([real_part.astype(BF16), imag_part.astype(BF16)], axis=1), cosines)


def filter_of(gated, shaped, static_rows, cosines):
    rows, length = gated.shape
    times = rows // static_rows.shape[0]
    edge = lax.broadcasted_iota(jnp.int32, (1, length), 1) == 0
    spectra = nn(jnp.concatenate([gated, shaped], axis=0).astype(BF16), cosines)
    shaped_re, shaped_im = (spectra[rows:, :length], spectra[rows:, length:])
    fixed = nn(static_rows, cosines)
    fixed_re = repeated(fixed[:, :length], times)
    fixed_im = repeated(fixed[:, length:], times)
    square = shaped_im * shaped_im
    power = shaped_re * shaped_re + jnp.where(edge, 0.0, square) + length
    inv_root = lax.rsqrt(power)
    power_last = square[:, :128] + length
    inv_root_last = lax.rsqrt(power_last)
    scale = 1.0 / math.sqrt(length)
    return {
        "length": length,
        "times": times,
        "edge": edge,
        "weight": jnp.where(edge, 0.5 / length, 1.0 / length),
        "signal_re": spectra[:rows, :length],
        "signal_im": spectra[:rows, length:],
        "shaped_re": shaped_re,
        "shaped_im": shaped_im,
        "fixed_im": fixed_im,
        "fixed_sine": jnp.where(edge, 0.0, fixed_im),
        "slope": scale * inv_root,
        "slope_last": scale * inv_root_last,
        "filter_re": fixed_re + (power * inv_root * scale - 1.0),
        "filter_last": fixed_im[:, :128] + (power_last * inv_root_last * scale - 1.0),
    }


def filtered(parts, cosines):
    signal_re, signal_im = (parts["signal_re"], parts["signal_im"])
    product_re = parts["filter_re"] * signal_re - parts["fixed_sine"] * signal_im
    product_im = at_edge(
        parts["edge"],
        parts["filter_last"] * signal_im[:, :128],
        parts["filter_re"] * signal_im + parts["fixed_im"] * signal_re,
    )
    return turned_back(product_re * parts["weight"], product_im * parts["weight"], cosines)


def filter_back(parts, grad_out, cosines):
    length, times, edge = (parts["length"], parts["times"], parts["edge"])
    signal_re, signal_im = (parts["signal_re"], parts["signal_im"])
    filter_re, fixed_im = (parts["filter_re"], parts["fixed_im"])
    turned = nn(grad_out.astype(BF16), cosines)
    product_re = turned[:, :length] * parts["weight"]
    product_im = turned[:, length:] * parts["weight"]
    grad_signal_re = filter_re * product_re + parts["fixed_sine"] * product_im
    grad_signal_im = at_edge(
        edge,
        parts["filter_last"] * product_im[:, :128],
        filter_re * product_im - fixed_im * product_re,
    )
    crossed = signal_im * product_im
    grad_filter = signal_re * product_re + jnp.where(edge, 0.0, crossed)
    grad_fixed_im = at_edge(
        edge, crossed[:, :128], signal_re * product_im - signal_im * product_re
    )
    slope = grad_filter * parts["slope"]
    grad_shaped_re = slope * parts["shaped_re"]
    grad_shaped_im = (
        at_edge(edge, crossed[:, :128] * parts["slope_last"], slope) * parts["shaped_im"]
    )
    count = grad_out.shape[0]
    rows = count // times
    grad_static = turned_back(
        sum(grad_filter[i * rows : (i + 1) * rows] for i in range(times)),
        sum(grad_fixed_im[i * rows : (i + 1) * rows] for i in range(times)),
        cosines,
    )
    back = turned_back(
        jnp.concatenate([grad_signal_re, grad_shaped_re], axis=0),
        jnp.concatenate([grad_signal_im, grad_shaped_im], axis=0),
        cosines,
    )
    return (back[:count], back[count:], grad_static)


def mixer_rows_of(flat_ref, step, per_step, chans):
    def rows(index):
        return [
            flat_ref[step * per_step + i, index * chans : (index + 1) * chans]
            for i in range(per_step)
        ]

    into = jnp.concatenate(rows(0) + rows(1) + rows(2), axis=0)
    filters = jnp.concatenate(rows(4), axis=0)
    return (into, jnp.concatenate(rows(3), axis=0), filters)


def mixer_taps(filters, start):
    lanes = filters[:, start : start + 128].astype(F32)
    taps = [lanes[:, k : k + 1] + lanes[:, 12 + k : 13 + k] for k in range(12)]
    return ([[taps[3 * k + group] for k in range(3)] for group in range(3)], taps[9:])


def own_lanes(ref, which, layout):
    half_long, short = (layout["long"] // 2, layout["short"])
    at = pl.multiple_of(which * half_long, 128)
    after = pl.multiple_of(layout["long"] + which * short, 128)
    return jnp.concatenate([ref[:, pl.ds(at, half_long)], ref[:, pl.ds(after, short)]], axis=1)


def mixer_forward_kernel(plan, sizes, *refs):
    inputs, buffers, outs, scratch = grouped(refs, 6, len(plan), 4, 4)
    place_ref, live_ref, long_ref, short_ref, normed_ref, own_ref = inputs
    proj_ref, long_out_ref, kept_ref, sent_ref = outs
    flat_ref, mixed_ref, total, sems = scratch
    long, short, chans, per_step = sizes
    fill(plan, place_ref, own_ref, buffers, flat_ref, sems, per_step)
    step = pl.program_id(0)
    layout = layout_of(long, short, normed_ref.shape[1])
    into, out_rows, filters = mixer_rows_of(flat_ref, step, per_step, chans)
    short_taps, cond_taps = mixer_taps(filters, long)
    rows = per_step * chans
    proj = nn(into, normed_ref[...])
    proj_ref[0] = proj.astype(BF16)
    query, key_part, value_part = (
        taps_forward(layout, proj[g * rows : (g + 1) * rows], short_taps[g]) for g in range(3)
    )
    gated = key_part * value_part * live_ref[:1]
    shaped = taps_forward(layout, gated, cond_taps)
    gated_parts, shaped_parts = (sequences(layout, gated), sequences(layout, shaped))
    results = [
        filtered(
            filter_of(gated_parts[i], shaped_parts[i], filters[:, :length], ref[...]), ref[...]
        )
        for i, (length, ref) in enumerate(((long, long_ref), (short, short_ref)))
    ]
    long_out = rejoined(*results)
    long_out_ref[0] = long_out.astype(BF16)
    mixed_ref[...] = (query * long_out).astype(BF16)
    core = place_ref[0]
    half = kept_ref.shape[1]
    part_kept = tn(out_rows, own_lanes(mixed_ref, core, layout))
    part_sent = tn(out_rows, own_lanes(mixed_ref, 1 - core, layout))
    add_total(total, jnp.concatenate([part_kept, part_sent], axis=1))
    split_total(total, kept_ref, sent_ref)


def mixer_forward(place, rows, normed, live, tables, sizes):
    own, buffers, plan, ranks = rows
    count, width = own.shape
    tokens = normed.shape[1]
    half = tokens // 2
    chans, per_step = sizes[2:]
    steps = ranks // per_step
    group = per_step * chans
    return pl.pallas_call(
        functools.partial(mixer_forward_kernel, plan, sizes),
        grid=(steps,),
        out_shape=[
            jax.ShapeDtypeStruct((steps, 3 * group, tokens), BF16),
            jax.ShapeDtypeStruct((steps, group, tokens), BF16),
            jax.ShapeDtypeStruct((width, half), F32),
            jax.ShapeDtypeStruct((width, half), BF16),
        ],
        in_specs=[SMEM, whole(live.shape)]
        + [whole(t.shape) for t in tables]
        + [whole((width, tokens)), ANY]
        + [ANY] * len(buffers),
        out_specs=[
            pl.BlockSpec((1, 3 * group, tokens), lambda r: (r, 0, 0)),
            pl.BlockSpec((1, group, tokens), lambda r: (r, 0, 0)),
            whole((width, half)),
            whole((width, half)),
        ],
        scratch_shapes=[
            pltpu.VMEM((ranks, count, width), BF16),
            pltpu.VMEM((group, tokens), BF16),
            pltpu.VMEM((width, tokens), F32),
            pltpu.SemaphoreType.DMA((ranks, 8)),
        ],
        compiler_params=PARAMS,
        cost_estimate=pl.CostEstimate(flops=1, bytes_accessed=1, transcendentals=0),
        name="mixer_forward",
    )(place, live, *tables, normed, own, *buffers)


def mixer_back_kernel(plan, routes, count, sizes, targets, *refs):
    inputs, buffers, outs, scratch = grouped(refs, 9, len(plan), 2 + targets, 6)
    place_ref, live_ref, long_ref, short_ref, normed_ref, coming_ref = inputs[:6]
    proj_ref, long_out_ref, own_ref = inputs[6:]
    kept_ref, sent_ref = outs[:2]
    flat_ref, grads_ref, total, rows_ref, sems, out_sems = scratch
    long, short, chans, per_step = sizes
    fill(plan, place_ref, own_ref, buffers, flat_ref, sems, per_step)
    step = pl.program_id(0)
    layout = layout_of(long, short, normed_ref.shape[1])
    into, out_rows, filters = mixer_rows_of(flat_ref, step, per_step, chans)
    short_taps, cond_taps = mixer_taps(filters, long)
    rows = per_step * chans
    grad_mixed = nn(out_rows, coming_ref[...])
    proj = [proj_ref[0, g * rows : (g + 1) * rows].astype(F32) for g in range(3)]
    query, key_part, value_part = (taps_forward(layout, proj[g], short_taps[g]) for g in range(3))
    live = live_ref[:1]
    gated = key_part * value_part * live
    shaped = taps_forward(layout, gated, cond_taps)
    long_out = long_out_ref[0].astype(F32)
    mixed = (query * long_out).astype(BF16)
    grad_query = grad_mixed * long_out
    grad_long_out = sequences(layout, grad_mixed * query)
    gated_parts, shaped_parts = (sequences(layout, gated), sequences(layout, shaped))
    backs = [
        filter_back(
            filter_of(gated_parts[i], shaped_parts[i], filters[:, :length], ref[...]),
            grad_long_out[i],
            ref[...],
        )
        for i, (length, ref) in enumerate(((long, long_ref), (short, short_ref)))
    ]
    grad_gated = rejoined(backs[0][0], backs[1][0])
    grad_shaped = rejoined(backs[0][1], backs[1][1])
    grad_static = jnp.concatenate(
        [backs[0][2][:, :short] + backs[1][2], backs[0][2][:, short:]], axis=1
    )
    grad_cond = taps_grad(layout, grad_shaped, gated)
    grad_gated = (grad_gated + taps_back(layout, grad_shaped, cond_taps)) * live
    grads = (grad_query, grad_gated * value_part, grad_gated * key_part)
    grad_taps = [taps_grad(layout, grads[g], proj[g]) for g in range(3)]
    grad_proj = jnp.concatenate(
        [taps_back(layout, grads[g], short_taps[g]) for g in range(3)], axis=0
    ).astype(BF16)
    lane = lax.broadcasted_iota(jnp.int32, (1, flat_ref.shape[2] - long), 1)
    lanes = sum(
        jnp.where(lane == 3 * k + group, grad_taps[group][k], 0.0)
        for k in range(3)
        for group in range(3)
    )
    lanes += sum(jnp.where(lane == 9 + k, grad_cond[k], 0.0) for k in range(3))
    grad_into = nt(grad_proj, normed_ref[...]).astype(BF16)
    grad_out = nt(mixed, coming_ref[...]).astype(BF16)
    grad_filters = jnp.concatenate([grad_static, lanes], axis=1).astype(BF16)
    for i in range(per_step):
        part = slice(i * chans, (i + 1) * chans)
        at = step * per_step + i
        for g in range(3):
            grads_ref[at, g * chans : (g + 1) * chans] = grad_into[g * rows : (g + 1) * rows][part]
        grads_ref[at, 3 * chans : 4 * chans] = grad_out[part]
        grads_ref[at, 4 * chans : 5 * chans] = grad_filters[part]
        spare = flat_ref.shape[1] - 5 * chans
        if spare:
            grads_ref[at, 5 * chans :] = jnp.zeros((spare, flat_ref.shape[2]), BF16)
    spilled = (routes, count, place_ref, grads_ref, outs[2:], out_sems, per_step)
    spill(*spilled)
    add_total(total, tn(into, grad_proj))

    @pl.when(step == pl.num_programs(0) - 1)
    def finish():
        core = place_ref[0]
        kept_ref[...] = own_lanes(total, core, layout)
        sent_ref[...] = own_lanes(total, 1 - core, layout).astype(BF16)

    spill_wait(*spilled, True)


def mixer_back(
    place, rows, normed, coming, proj, long_out, live, tables, sizes, routes, blocks, block_rows
):
    outs = 1 + max(target[0] for route in routes for target in route[0].values())
    own, buffers, plan, ranks = rows
    count, width = own.shape
    tokens = normed.shape[1]
    half = tokens // 2
    chans, per_step = sizes[2:]
    steps = ranks // per_step
    group = per_step * chans
    results = pl.pallas_call(
        functools.partial(mixer_back_kernel, plan, routes, plan[0][3], sizes, outs),
        grid=(steps,),
        out_shape=[
            jax.ShapeDtypeStruct((width, half), F32),
            jax.ShapeDtypeStruct((width, half), BF16),
        ]
        + [jax.ShapeDtypeStruct((blocks, block_rows, width), BF16)] * outs,
        in_specs=[SMEM, whole(live.shape)]
        + [whole(t.shape) for t in tables]
        + [
            whole((width, tokens)),
            whole((width, tokens)),
            pl.BlockSpec((1, 3 * group, tokens), lambda r: (r, 0, 0)),
            pl.BlockSpec((1, group, tokens), lambda r: (r, 0, 0)),
            ANY,
        ]
        + [ANY] * len(buffers),
        out_specs=[whole((width, half)), whole((width, half))] + [ANY] * outs,
        scratch_shapes=[
            pltpu.VMEM((ranks, count, width), BF16),
            pltpu.VMEM((ranks, count, width), BF16),
            pltpu.VMEM((width, tokens), F32),
            pltpu.VMEM((8, 128), F32),
            pltpu.SemaphoreType.DMA((ranks, 8)),
            pltpu.SemaphoreType.DMA((ranks, 8)),
        ],
        compiler_params=PARAMS,
        cost_estimate=pl.CostEstimate(flops=1, bytes_accessed=1, transcendentals=0),
        name="mixer_back",
    )(place, live, *tables, normed, coming, proj, long_out, own, *buffers)
    return (results[0], results[1], results[2:])


def final_copies(place_ref, sources, flat_ref, sems):
    copies = []
    for side, source in enumerate(sources):
        core = place_ref[0] if side == 0 else 1 - place_ref[0]
        count = source.shape[1]
        for offset in range(source.shape[0]):
            row = pl.multiple_of((place_ref[1] ^ offset) * count, 16)
            copies.append(
                pltpu.make_async_copy(
                    source.at[offset], flat_ref.at[core, pl.ds(row, count)], sems.at[len(copies)]
                )
            )
    return copies


def final_mlp_kernel(aliased, *refs):
    (place_ref,), sources, _, outs, (flat_ref, sems) = grouped(
        refs, 1, 2, 2 if aliased else 0, 2, 2
    )
    up_ref, down_ref = outs
    step = pl.program_id(0)
    width = flat_ref.shape[2]
    hidden = flat_ref.shape[1] - width

    @pl.when(step == 0)
    def gather():
        copies = final_copies(place_ref, sources, flat_ref, sems)
        for copy in copies:
            copy.start()
        for copy in copies:
            copy.wait()

    rows = up_ref.shape[1]
    part = pl.ds(pl.multiple_of(step * rows, 16), rows)
    for core in range(2):
        lanes = slice(core * hidden, (core + 1) * hidden)
        up_ref[0, :, 0, lanes] = flat_ref[core, part, :hidden].astype(F32)
        up_ref[0, :, 1, lanes] = flat_ref[core, part, hidden:].astype(F32)
    each = down_ref.shape[1]
    per_core = hidden // each
    at = pl.multiple_of(width + (step % per_core) * each, 16)
    down_ref[0] = flat_ref[step // per_core, pl.ds(at, each)].astype(F32)


def final_mlp(place, sources, count, layer, layers, into):
    width = sources[0].shape[2]
    hidden = count - width
    steps = 4
    aliased = into is not None
    return pl.pallas_call(
        functools.partial(final_mlp_kernel, aliased),
        grid=(steps,),
        out_shape=[
            jax.ShapeDtypeStruct((layers, width, 2, 2 * hidden), F32),
            jax.ShapeDtypeStruct((layers, 2 * hidden, width), F32),
        ],
        in_specs=[SMEM] + [ANY] * (4 if aliased else 2),
        out_specs=[
            pl.BlockSpec((1, width // steps, 2, 2 * hidden), lambda i: (layer, i, 0, 0)),
            pl.BlockSpec((1, 2 * hidden // steps, width), lambda i: (layer, i, 0)),
        ],
        input_output_aliases={3: 0, 4: 1} if aliased else {},
        scratch_shapes=[
            pltpu.VMEM((2, count, width), BF16),
            pltpu.SemaphoreType.DMA((2 * sources[0].shape[0],)),
        ],
        compiler_params=PARAMS,
        cost_estimate=pl.CostEstimate(flops=1, bytes_accessed=1, transcendentals=0),
        name="final_mlp",
    )(place, *sources, *(into if aliased else ()))


def final_mixer_kernel(chans, aliased, *refs):
    (place_ref,), sources, _, outs, (flat_ref, sems) = grouped(
        refs, 1, 2, 3 if aliased else 0, 3, 2
    )
    into_ref, out_ref, filter_ref = outs
    copies = final_copies(place_ref, sources, flat_ref, sems)
    for copy in copies:
        copy.start()
    for copy in copies:
        copy.wait()
    for core in range(2):
        lanes = slice(core * chans, (core + 1) * chans)
        for g in range(3):
            into_ref[0, g, lanes] = flat_ref[core, g * chans : (g + 1) * chans].astype(F32)
        out_ref[0, lanes] = flat_ref[core, 3 * chans : 4 * chans].astype(F32)
        filter_ref[0, lanes] = flat_ref[core, 4 * chans : 5 * chans].astype(F32)


def final_mixer(place, sources, count, chans, layer, layers, into):
    width = sources[0].shape[2]
    aliased = into is not None
    return pl.pallas_call(
        functools.partial(final_mixer_kernel, chans, aliased),
        grid=(1,),
        out_shape=[
            jax.ShapeDtypeStruct((layers, 3, 2 * chans, width), F32),
            jax.ShapeDtypeStruct((layers, 2 * chans, width), F32),
            jax.ShapeDtypeStruct((layers, 2 * chans, width), F32),
        ],
        in_specs=[SMEM] + [ANY] * (5 if aliased else 2),
        out_specs=[
            pl.BlockSpec((1, 3, 2 * chans, width), lambda i: (layer, 0, 0, 0)),
            pl.BlockSpec((1, 2 * chans, width), lambda i: (layer, 0, 0)),
            pl.BlockSpec((1, 2 * chans, width), lambda i: (layer, 0, 0)),
        ],
        input_output_aliases={3: 0, 4: 1, 5: 2} if aliased else {},
        scratch_shapes=[
            pltpu.VMEM((2, count, width), BF16),
            pltpu.SemaphoreType.DMA((2 * sources[0].shape[0],)),
        ],
        compiler_params=PARAMS,
        cost_estimate=pl.CostEstimate(flops=1, bytes_accessed=1, transcendentals=0),
        name="final_mixer",
    )(place, *sources, *(into if aliased else ()))


def norm_forward(values, gain):
    average = jnp.mean(values, axis=0, keepdims=True)
    centered = values - average
    inv_std = lax.rsqrt(jnp.mean(centered * centered, axis=0, keepdims=True) + EPS)
    normal_rows = centered * inv_std
    return ((normal_rows * gain).astype(BF16), (normal_rows, inv_std, gain))


def norm_back(grads, stored):
    normal_rows, inv_std, gain = stored
    scaled = grads * gain
    total = jnp.mean(scaled, axis=0, keepdims=True)
    crossed = jnp.mean(scaled * normal_rows, axis=0, keepdims=True)
    gain_grad = jnp.sum(grads * normal_rows, axis=1)
    return (inv_std * (scaled - total - normal_rows * crossed), gain_grad)


def on_device(
    input_long,
    input_short,
    length_long,
    length_short,
    gain_mixer,
    weight_in,
    short_taps,
    cond_taps,
    static_filter,
    weight_out,
    gain_mlp,
    weight_up,
    weight_down,
    grad_long,
    grad_short,
):
    count_long, seq_long, chan_width = input_long.shape
    count_short, seq_short = (input_short.shape[0], input_short.shape[1])
    layers = weight_in.shape[0]
    ranks = lax.axis_size("chan")
    pairs = lax.axis_size("batch") // 2
    place = lax.axis_index("chan")
    core = lax.axis_index("batch") % 2
    pair = lax.axis_index("batch") // 2
    width = chan_width * ranks
    hidden = weight_down.shape[1] // 2
    chans = chan_width // 2
    half_long = seq_long // 2
    tokens = half_long + seq_short
    mate = ("batch", 1)
    first = core == 0
    pieces = 4
    piece = pair % pieces
    plane = {1: ("batch", 2), 2: ("batch", 4)}
    extra_steps = []
    mask = 2 * pieces
    while mask < 2 * pairs:
        extra_steps.append(("batch", mask))
        mask *= 2
    spot = jnp.stack([core, piece, place]).astype(jnp.int32)
    plane_orders = ((1, 2), (2, 1))

    def to_tokens(long_rows, short_rows, extra=None):
        turned = jnp.swapaxes(long_rows, 1, 2).astype(BF16)
        halves = jnp.stack([turned[..., :half_long], turned[..., half_long:]])
        kept = pick(halves, core)
        came = swap(pick(halves, 1 - core), mate)
        ordered = jnp.where(first, jnp.concatenate([kept, came]), jnp.concatenate([came, kept]))
        parts = [ordered, jnp.swapaxes(short_rows, 1, 2).astype(BF16)]
        if extra is not None:
            parts.append(jnp.broadcast_to(extra[None], (ranks,) + extra.shape))
        yield from exchange(jnp.concatenate(parts, axis=2), lambda v: v.reshape(width, -1))

    def exchange(blocks, then):
        came = {0: pick(blocks, place)}
        both = jnp.stack([pick(blocks, place ^ FAR), pick(blocks, place ^ NEAR ^ FAR)])
        first_came = swap(both, ("chan", FAR))
        first_came = after(first_came, *(yield [both]))
        came[FAR] = first_came[0]
        both = jnp.stack([pick(blocks, place ^ NEAR), first_came[1]])
        second_came = swap(both, ("chan", NEAR))
        second_came = after(second_came, *(yield [both]))
        came[NEAR], came[NEAR ^ FAR] = (second_came[0], second_came[1])
        result = then(by_xor(jnp.stack([came[r] for r in range(ranks)]), place))
        yield result

    def from_tokens(values):
        steps = exchange(values.reshape(ranks, chan_width, -1), lambda gathered: gathered)
        ties = yield next(steps)
        ties = yield steps.send(ties)
        gathered = steps.send(ties)
        halves = gathered[:, :, :half_long].reshape(2, count_long, chan_width, half_long)
        kept = pick(halves, core)
        sent = pick(halves, 1 - core)
        came = swap(sent, mate)
        came = after(came, *(yield [sent]))
        ordered = jnp.where(
            first, jnp.concatenate([kept, came], axis=2), jnp.concatenate([came, kept], axis=2)
        )
        short_part = jnp.swapaxes(gathered[:, :, half_long:tokens], 1, 2)
        yield (jnp.swapaxes(ordered, 1, 2), short_part, gathered[:, :, tokens:])

    def both_cores(values):
        return jnp.concatenate([values, swap(values, mate)], axis=1)

    def both_ordered(values):
        came = swap(values, mate)
        low, high = (jnp.where(first, values, came), jnp.where(first, came, values))
        return jnp.concatenate(
            [low[:, :half_long], high[:, :half_long], low[:, half_long:], high[:, half_long:]],
            axis=1,
        )

    def own_sum(sent, kept):
        return kept + swap(sent, mate).astype(F32)

    def mlp_rows(layer):
        up = lax.dynamic_slice_in_dim(weight_up[layer], core * hidden, hidden, 2)
        down = lax.dynamic_slice_in_dim(weight_down[layer], core * hidden, hidden, 0)
        return jnp.concatenate([up.reshape(width, 2 * hidden), down])

    def mixer_rows(layer):
        into = jnp.transpose(weight_in[layer], (1, 2, 0))
        into = lax.dynamic_slice_in_dim(into, core * chans, chans, 1)
        out = lax.dynamic_slice_in_dim(weight_out[layer], core * chans, chans, 0)
        taps = jnp.concatenate([short_taps[layer].reshape(9, chan_width), cond_taps[layer]]).T
        coarse = lax.reduce_precision(taps, 8, 7)
        static = jnp.concatenate([static_filter[layer].T, coarse, taps - coarse], axis=1)
        static = jnp.pad(static.astype(BF16), ((0, 0), (0, width - static.shape[1])))
        static = lax.dynamic_slice_in_dim(static, core * chans, chans, 0)
        spare = jnp.zeros((mixer_count - 5 * chans, width), BF16)
        return jnp.concatenate([into.reshape(3 * chans, width), out, static, spare])

    mixer_count = -(-5 * chans // (32 * pieces)) * 32 * pieces
    mlp_count = width + hidden
    own_rows = [
        {"mixer": mixer_rows(layer), "mlp": mlp_rows(layer)} for layer in range(layers)
    ]

    def half_rows(kind):
        return (mixer_count if kind == "mixer" else mlp_count) // (2 * pieces)

    def own_block(layer, kind, half):
        count = half_rows(kind)
        return lax.dynamic_slice_in_dim(
            own_rows[layer][kind], (piece * 2 + half) * count, count, 0
        )

    others = (FAR, NEAR, FAR ^ NEAR)

    def gather(layer, kind):
        block = jnp.concatenate([own_block(layer, kind, half) for half in range(2)])[None]
        count = half_rows(kind)
        far = swap(block, ("chan", FAR))
        far = after(far, *(yield [block]))
        both = jnp.concatenate([block, far])
        near = swap(both, ("chan", NEAR))
        near = after(near, *(yield [both]))
        foreign = jnp.concatenate([far, near])
        held = [foreign[:, half * count : (half + 1) * count] for half in range(2)]
        came = [swap(held[half], plane[plane_orders[half][0]]) for half in range(2)]
        ties = yield held
        held = [jnp.concatenate([held[half], after(came[half], *ties)]) for half in range(2)]
        buffers, plan = ([], [])
        for half, (one, two) in enumerate(plane_orders):
            blocks = [(0, other) for other in others] + [(one, other) for other in others]
            buffers += [held[half], swap(held[half], plane[two])]
            plan.append((half, tuple(blocks), 0, count))
            plan.append((half, tuple((offset ^ two, other) for offset, other in blocks), 0, count))
        weights[layer, kind] = (own_rows[layer][kind], tuple(buffers), tuple(plan), ranks)
        yield held

    line = []

    def go(steps, *ties):
        line[:] = steps.send((*line, *ties))

    def begin(steps):
        line.extend(next(steps))
        return steps

    def finish(steps):
        return steps.send(tuple(line))

    weights = {}
    gains = jnp.stack([gain_mixer, gain_mlp], axis=1).reshape(2 * layers, chan_width)
    gains_coarse = lax.reduce_precision(gains, 8, 7)
    gains = jnp.concatenate([gains_coarse, gains - gains_coarse]).astype(BF16).T
    gains = jnp.pad(gains, ((0, 0), (0, 128 - gains.shape[1])))
    mixer_0 = begin(gather(0, "mixer"))
    input_steps = begin(to_tokens(input_long, input_short, gains))
    mlp_0 = begin(gather(0, "mlp"))
    go(mixer_0)
    go(input_steps)
    go(mixer_0)
    go(mlp_0)
    arrived = finish(input_steps)
    gains = arrived[:, tokens : tokens + 4 * layers].astype(F32)
    gains = gains[:, : 2 * layers] + gains[:, 2 * layers :]
    gains = gains.T.reshape(layers, 2, width, 1)

    own_lengths = jnp.concatenate([length_long, length_short])
    other_lengths = swap(own_lengths, mate)
    low, high = (
        jnp.where(first, own_lengths, other_lengths),
        jnp.where(first, other_lengths, own_lengths),
    )
    spans = [pick(jnp.concatenate([low[:count_long], high[:count_long]]), place)]
    spans += [pick(side[count_long:], place) for side in (low, high)]
    live = jnp.concatenate(
        [
            jnp.arange(length) < span
            for length, span in zip((seq_long, seq_short, seq_short), spans)
        ]
    )
    live = jnp.broadcast_to(live.astype(F32)[None], (8, live.shape[0]))
    tables = (table(seq_long), table(seq_short))
    sizes = (seq_long, seq_short, chans, 2)

    chan_order = (0, FAR, NEAR, NEAR ^ FAR)

    def routes(near_first, count, single=False):
        found = []
        for half, (one, two) in enumerate(((1, 2), (1, 2)) if single else plane_orders):
            for a in range(2):
                for c in range(2):
                    if near_first:
                        targets = {r: (i // 2, 4 * a + 2 * c + i % 2) for i, r in enumerate(chan_order)}
                    else:
                        targets = {r: (2 * half + a, ranks * c + i) for i, r in enumerate(chan_order)}
                    found.append((targets, half, a * one + c * two, near_first * half * count))
        return tuple(found)

    mlp_half, mixer_half = (half_rows("mlp"), half_rows("mixer"))
    residual_start = arrived[:, :tokens].astype(F32)
    residual = residual_start
    stored_all = []
    for layer in range(layers):
        normed, norm_stored = norm_forward(residual, gains[layer, 0])
        normed = both_ordered(normed)
        if layer == 0:
            mixer_1 = begin(gather(1, "mixer"))
            go(mixer_0)
            go(mlp_0)
        else:
            go(mlp_1)
        proj, long_out, kept, sent = mixer_forward(
            spot, weights[layer, "mixer"], after(normed, *line), live, tables, sizes
        )
        if layer == 0:
            go(mixer_1, kept)
        else:
            grad_steps = begin(to_tokens(grad_long, grad_short))
        sent = after(sent, *line)
        middle = residual + own_sum(sent, kept)
        normed_mlp, mlp_stored = norm_forward(middle, gains[layer, 1])
        normed_mlp = both_cores(normed_mlp)
        if layer == 0:
            go(mlp_0)
            mlp_1 = begin(gather(1, "mlp"))
            go(mixer_1)
            go(mlp_1)
            go(mixer_1)
            go(mlp_1)
            gate_up, kept, sent = mlp_forward(
                spot, weights[layer, "mlp"], after(normed_mlp, *line)
            )
        else:
            go(grad_steps)
            upstream = finish(grad_steps).astype(F32)
            coming = both_cores(upstream.astype(BF16))
            gate_up = None
            (kept, sent, *turned), blocks = mlp_turn(
                spot, weights[layer, "mlp"], after(normed_mlp, *line), coming, routes(False, mlp_half),
                2 * ranks, mlp_half,
            )
        residual = middle + own_sum(sent, kept)
        stored_all.append((normed, norm_stored, proj, long_out, normed_mlp, mlp_stored, gate_up))
    output_steps = from_tokens((residual - residual_start).astype(BF16))

    def added(values):
        return sum(value.astype(F32) for value in values).astype(BF16)

    def spread_sums(block, early):
        for step in extra_steps:
            block = added([block, swap(block, step)])
        parts = [(block, plane_orders[early])] if early is not None else []
        if early is None:
            middle = block.shape[1] // 2
            parts = [(block[:, :middle], plane_orders[0]), (block[:, middle:], plane_orders[1])]
        came = [swap(part, plane[one]) for part, (one, _) in parts]
        ties = yield [part for part, _ in parts]
        both = [jnp.concatenate([part, after(c, *ties)]) for (part, _), c in zip(parts, came)]
        came = [swap(part, plane[two]) for part, (_, (_, two)) in zip(both, parts)]
        ties = yield both
        pieces_of = []
        for part, c, (_, (one, two)) in zip(both, came, parts):
            c = after(c, *ties)
            by = {0: part[:1], one: part[1:], two: c[:1], one ^ two: c[1:]}
            pieces_of.append(jnp.concatenate([by[offset] for offset in range(pieces)]))
        mine = jnp.concatenate(pieces_of, axis=1)
        came = swap(mine, mate)
        ties = yield [mine]
        yield (mine, after(came, *ties))

    def scatter(blocks, early, single=False):
        near_first = len(blocks) == 2
        orders = ((1, 2),) if single else plane_orders
        if near_first:
            came = swap(blocks[1], ("chan", NEAR))
            ties = yield [blocks[1]]
            block = added([blocks[0], after(came, *ties)])
            count = block.shape[1] // len(orders)
            parts = [block[:, i * count : (i + 1) * count] for i in range(len(orders))]
            kept = [part[:4] for part in parts]
            sent = [part[4:] for part in parts]
        else:
            kept, sent = (blocks[0::2], blocks[1::2])
        came = [swap(part, plane[one]) for part, (one, _) in zip(sent, orders)]
        ties = yield list(sent)
        came = [after(value, *ties) for value in came]
        middle = kept[0].shape[0] // 2
        sent = [added([k[middle:], c[middle:]]) for k, c in zip(kept, came)]
        kept = [added([k[:middle], c[:middle]]) for k, c in zip(kept, came)]
        came = [swap(part, plane[two]) for part, (_, two) in zip(sent, orders)]
        ties = yield sent
        came = [after(value, *ties) for value in came]
        block = jnp.concatenate([added([k, c]) for k, c in zip(kept, came)], axis=1)
        for mask in (FAR,) if near_first else (NEAR, FAR):
            kept, sent = (block[: block.shape[0] // 2], block[block.shape[0] // 2 :])
            came = swap(sent, ("chan", mask))
            ties = yield [sent]
            block = added([kept, after(came, *ties)])
        yield from spread_sums(block, early)

    upstream_start = upstream
    gain_grads = {}
    scatters = []

    line[:] = []
    for layer in reversed(range(layers)):
        normed, norm_stored, proj, long_out, normed_mlp, mlp_stored, gate_up = stored_all[layer]
        last = layer == 0
        if gate_up is None:
            kept, sent = turned
        else:
            coming = both_cores(upstream.astype(BF16))
            kept, sent, blocks = mlp_back(
                spot, weights[layer, "mlp"], normed_mlp, gate_up, coming,
                routes(False, mlp_half), 2 * ranks, mlp_half,
            )
        if last:
            go(scatters[0], kept)
            go(scatters[1], kept)
        scatters.append(begin(scatter(blocks, None if last else 0)))
        sent = after(sent, *line)
        change, gain_grads[layer, 1] = norm_back(own_sum(sent, kept), mlp_stored)
        upstream = upstream + change
        coming = both_ordered(upstream.astype(BF16))
        if not last:
            begin(output_steps)
        kept, sent, blocks = mixer_back(
            spot, weights[layer, "mixer"], normed, after(coming, *line), proj, long_out, live,
            tables, sizes, routes(True, mixer_half, not last), 2 * ranks, 2 * mixer_half,
        )
        if last:
            scatters.append(begin(scatter(blocks, None)))
            go(scatters[2], kept)
            go(scatters[0], kept)
        else:
            scatters.append(begin(scatter(blocks, 1, True)))
        sent = after(sent, *line)
        change, gain_grads[layer, 0] = norm_back(own_sum(sent, kept), norm_stored)
        upstream = upstream + change
        if not last:
            go(scatters[0])
            go(output_steps)

    mlp_early, mixer_early, mlp_late, mixer_late = scatters

    gain_parts = jnp.stack(
        [gain_grads[layer, which] for layer in range(layers) for which in range(2)], axis=1
    )
    gain_coarse = lax.reduce_precision(gain_parts, 8, 7)
    gain_lanes = jnp.concatenate([gain_coarse, gain_parts - gain_coarse], axis=1).astype(BF16)
    gain_lanes = jnp.pad(gain_lanes, ((0, 0), (0, 128 - gain_lanes.shape[1])))
    go(output_steps)
    go(mixer_early)
    go(mlp_late)
    go(mlp_early)
    gone_long, gone_short, _ = finish(output_steps)
    output_long = input_long + gone_long.astype(F32)
    output_short = input_short + gone_short.astype(F32)
    line.append(output_long)
    go(mixer_late)
    changed = jnp.concatenate([(upstream - upstream_start).astype(BF16), gain_lanes], axis=1)
    back_steps = begin(from_tokens(after(changed, *line)))
    go(mixer_early)
    go(mlp_late)
    go(mlp_early)
    go(mixer_late)
    go(mixer_early)
    go(back_steps)
    go(mlp_late)
    go(mixer_late)
    go(mlp_early)
    go(mixer_early)
    go(back_steps)
    go(mlp_late)
    go(mixer_late)
    mlp_out = final_mlp(spot, finish(mlp_early), mlp_count, 1, layers, None)
    line.append(mlp_out[1])
    go(mixer_early)
    gone_long, gone_short, gain_sums = finish(back_steps)
    back_long = grad_long + gone_long.astype(F32)
    back_short = grad_short + gone_short.astype(F32)
    line.append(back_long)
    gain_sums = jnp.sum(gain_sums[:, :, : 4 * layers].astype(F32), axis=0)
    gain_sums = (gain_sums[:, : 2 * layers] + gain_sums[:, 2 * layers :]).T


    def reduced(values):
        came = swap(values, mate)
        values = values + after(came, *(yield [values]))
        came = [swap(values, ("batch", 2 * offset)) for offset in range(1, pieces)]
        ties = yield [values]
        values = values + sum(after(value, *ties) for value in came)
        for step in extra_steps:
            came = swap(values, step)
            values = values + after(came, *(yield [values]))
        yield values

    gain_steps = begin(reduced(gain_sums))
    go(mlp_late)
    go(gain_steps)
    go(mixer_late)
    for _ in extra_steps:
        go(gain_steps)
    mixer_out = final_mixer(spot, finish(mixer_early), mixer_count, chans, 1, layers, None)
    line.append(mixer_out[1])
    gain_sums = finish(gain_steps)
    mlp_out = final_mlp(spot, finish(mlp_late), mlp_count, 0, layers, mlp_out)
    line.append(mlp_out[1])
    go(mixer_late)
    mixer_out = final_mixer(spot, finish(mixer_late), mixer_count, chans, 0, layers, mixer_out)
    into_out, out_out, filter_out = mixer_out
    taps = jnp.swapaxes(filter_out[:, :, seq_long : seq_long + 12], 1, 2)

    return (
        output_long,
        output_short,
        back_long,
        back_short,
        gain_sums[0::2],
        jnp.transpose(into_out, (0, 3, 1, 2)),
        taps[:, :9].reshape(layers, 3, 3, chan_width),
        taps[:, 9:],
        jnp.swapaxes(filter_out[:, :, :seq_long], 1, 2),
        out_out,
        gain_sums[1::2],
        mlp_out[0],
        mlp_out[1],
    )


def solution(mesh):
    tokens = P("batch", None, "chan")
    placed = (
        tokens,
        tokens,
        P("batch"),
        P("batch"),
        P(None, "chan"),
        P(None, None, None, "chan"),
        P(None, None, None, "chan"),
        P(None, None, "chan"),
        P(None, None, "chan"),
        P(None, "chan", None),
        P(None, "chan"),
        P(None, None, None, "chan"),
        P(None, "chan", None),
        tokens,
        tokens,
    )
    return jax.shard_map(
        on_device,
        mesh=mesh,
        in_specs=placed,
        out_specs=(tokens,) * 4 + placed[4:13],
        check_vma=False,
    )
```
